32 devices in a mesh: rows: 4 (over z), fsdp: 8 (over y, x, core).
Axes of the slice: x: 2, y: 2, z: 4, core: 2. Of those that a mesh axis runs over, the one named last changes fastest.
Arguments:
- tokens: bfloat16 [32, 512, 1024], P(('rows', 'fsdp')), may hold values from -6 to 6
- time_embed: bfloat16 [32, 256], P(('rows', 'fsdp')), may hold values from -6 to 6
- segment_ids: int32 [32, 512], P(('rows', 'fsdp')), may hold values from 0 to 3, never falling along the last dimension, each value on 1 to 256 neighbouring positions
- cotangent: bfloat16 [32, 512, 1024], P(('rows', 'fsdp')), may hold values from -6 to 6
- mixing_w: float32 [4, 1024, 1024], P(None, 'fsdp'), may hold values from -0.25 to 0.25
- mixing_m: float32 [4, 1024, 1024], P(None, 'fsdp'), may hold values from -384 to 384
- mixing_v: float32 [4, 1024, 1024], P(None, 'fsdp'), may hold values from 4096 to 16384
- mixing_avg: float32 [4, 1024, 1024], P(None, 'fsdp'), may hold values from -0.25 to 0.25
- cond_w: float32 [2, 256, 1024], P(None, 'fsdp'), may hold values from -0.1875 to 0.1875
- cond_m: float32 [2, 256, 1024], P(None, 'fsdp'), may hold values from -768 to 768
- cond_v: float32 [2, 256, 1024], P(None, 'fsdp'), may hold values from 16384 to 65536
- cond_avg: float32 [2, 256, 1024], P(None, 'fsdp'), may hold values from -0.1875 to 0.1875
- up_w: float32 [1024, 4096], P('fsdp'), may hold values from -0.1875 to 0.1875
- up_m: float32 [1024, 4096], P('fsdp'), may hold values from -224 to 224
- up_v: float32 [1024, 4096], P('fsdp'), may hold values from 1489 to 5957
- up_avg: float32 [1024, 4096], P('fsdp'), may hold values from -0.1875 to 0.1875
- down_w: float32 [4096, 1024], P('fsdp'), may hold values from -0.09375 to 0.09375
- down_m: float32 [4096, 1024], P('fsdp'), may hold values from -448 to 448
- down_v: float32 [4096, 1024], P('fsdp'), may hold values from 5898 to 23592
- down_avg: float32 [4096, 1024], P('fsdp'), may hold values from -0.09375 to 0.09375
Outputs:
- output: bfloat16 [32, 512, 1024], P(('rows', 'fsdp'))
- input_grad: bfloat16 [32, 512, 1024], P(('rows', 'fsdp'))
- mixing_grad: float32 [4, 1024, 1024], P(None, 'fsdp')
- mixing_m_out: float32 [4, 1024, 1024], P(None, 'fsdp')
- mixing_v_out: float32 [4, 1024, 1024], P(None, 'fsdp')
- mixing_w_out: float32 [4, 1024, 1024], P(None, 'fsdp')
- mixing_avg_out: float32 [4, 1024, 1024], P(None, 'fsdp')
- cond_grad: float32 [2, 256, 1024], P(None, 'fsdp')
- cond_m_out: float32 [2, 256, 1024], P(None, 'fsdp')
- cond_v_out: float32 [2, 256, 1024], P(None, 'fsdp')
- cond_w_out: float32 [2, 256, 1024], P(None, 'fsdp')
- cond_avg_out: float32 [2, 256, 1024], P(None, 'fsdp')
- up_grad: float32 [1024, 4096], P('fsdp')
- up_m_out: float32 [1024, 4096], P('fsdp')
- up_v_out: float32 [1024, 4096], P('fsdp')
- up_w_out: float32 [1024, 4096], P('fsdp')
- up_avg_out: float32 [1024, 4096], P('fsdp')
- down_grad: float32 [4096, 1024], P('fsdp')
- down_m_out: float32 [4096, 1024], P('fsdp')
- down_v_out: float32 [4096, 1024], P('fsdp')
- down_w_out: float32 [4096, 1024], P('fsdp')
- down_avg_out: float32 [4096, 1024], P('fsdp')
The draws below stay inside these ranges and needn't reach their ends.
Inputs may be any that keep to these rules, and one draw needn't show every extreme that they name: `segment_ids`: ids never fall along a row; a row has at most 4 segments, each of 1 to 256 tokens, and one segment of a row has exactly 256.
All inputs are finite; a program needn't handle non-finite values.
Results may differ from the reference program's by a relative error of at most 0.023.
The reference program's roundings to bfloat16 on the way count: a program that leaves them out, or rounds other values in their place, can miss the bound.
Values may be sent and summed in bfloat16 or wider, within the bound.
A program may use at most 320 MiB of HBM per device.

```python
import math
import jax
import jax.numpy as jnp
import numpy as np
from jax import lax

D = 1024
FF = 4096
HEADS = 16
HEAD_DIM = 64
EMBED = 256
TOK_DEV = 512
STEP = 7
SEQS = 32
TOKENS = 16384


def raised(array, stream_key, source, target, shards_of, factor):
    def block_of(axis_at):
        return (jnp.arange(array.shape[axis_at]) // (array.shape[axis_at] // shards_of)).reshape((-1,) + (1,) * (array.ndim - 1 - axis_at))

    first = jax.random.permutation(stream_key, shards_of)[block_of(target)]
    other_side = (block_of(target) + shards_of // 2) % shards_of
    return jnp.where((block_of(source) == first) | (block_of(source) == other_side), factor * array, array)


def block_levels(stream_key, extent, pieces, least, largest):
    def one(dim, shards_of):
        steps = jax.random.uniform(jax.random.fold_in(jax.random.fold_in(stream_key, 6), dim), (shards_of,), jnp.float32, least / len(pieces), largest / len(pieces))
        return jnp.repeat(jnp.exp(steps), extent[dim] // shards_of).reshape((-1,) + (1,) * (len(extent) - dim - 1))

    loudness = one(*pieces[0])
    for cut in pieces[1:]:
        loudness = loudness * one(*cut)
    return loudness


def profile(amount, total, reach, lean):
    weights = [(1 << 20) // math.isqrt(grade ** lean) + 1 for grade in range(2, amount + 1)]
    rest, holding = total - reach - (amount - 1), [1] * (amount - 1)
    while rest > 0:
        free = [i for i in range(amount - 1) if holding[i] < reach]
        whole, remaining = sum([weights[i] for i in free]), rest
        for i in free:
            extra = min(reach - holding[i], max(1, remaining * weights[i] // whole), rest)
            holding[i] = holding[i] + extra
            rest = rest - extra
    return np.array([reach] + holding)


def ragged_sizes(stream_key, amount, total, bound, lean):
    if amount == 2:
        one = jax.random.randint(stream_key, (), max(1, total - bound), min(bound, total - 1) + 1)
        return jnp.stack([one, total - one])
    tallies = jnp.asarray(profile(amount, total, bound, lean), jnp.int32)
    twos = (amount - 1) // 2
    source_of, receiver = tallies[1:1 + 2 * twos:2], tallies[2:2 + 2 * twos:2]
    slack = jnp.minimum(source_of - 1, bound - receiver)
    shifted = jax.random.randint(jax.random.fold_in(stream_key, 1), (twos,), 0, 1 << 20) % (slack + 1)
    tallies = tallies.at[1:1 + 2 * twos:2].set(source_of - shifted).at[2:2 + 2 * twos:2].set(receiver + shifted)
    return tallies[jax.random.permutation(jax.random.fold_in(stream_key, 2), amount)]


def bell_draw(own_key, extent, scale, reach, pieces=(), held_as=jnp.bfloat16):
    result = scale * jax.random.normal(own_key, extent, jnp.float32)
    if pieces:
        result = result * block_levels(own_key, extent, pieces, -0.22, 0.18)
    return jnp.clip(result, -reach, reach).astype(held_as)


def bell_draw_with(key, dims, width, limit, cuts, heavy, held_as=jnp.bfloat16):
    result = width * jax.random.normal(key, dims, jnp.float32)
    if cuts:
        result = result * block_levels(key, dims, cuts, -0.22, 0.18)
    return jnp.clip(raised(result, jax.random.fold_in(key, 3), *heavy), -limit, limit).astype(held_as)


def setup_inputs(seed: int = 0) -> dict:
    seeds = jax.random.split(jax.random.key(seed), 21)
    return {
        "tokens": bell_draw_with(seeds[0], (SEQS, TOK_DEV, D), 1.0, 6.0, ((0, 32),), (0, 2, 32, 2.75)),
        "time_embed": bell_draw(seeds[1], (SEQS, EMBED), 1.0, 6.0, ((0, 32),)),
        "segment_ids": jax.vmap(lambda own: jnp.searchsorted(jnp.cumsum(ragged_sizes(own, 4, TOK_DEV, TOK_DEV // 2, 1)), jnp.arange(TOK_DEV), side="right"))(jax.random.split(seeds[2], SEQS)).reshape((SEQS, TOK_DEV)).astype(jnp.int32),
        "cotangent": bell_draw_with(seeds[3], (SEQS, TOK_DEV, D), 1.0, 6.0, ((0, 32),), (0, 2, 32, 2.75)),
        "mixing_w": bell_draw(seeds[4], (4, D, D), (D // 2) ** -0.5, 0.25, ((1, 8),), jnp.float32),
        "mixing_m": bell_draw(seeds[5], (4, D, D), (0.5 * TOKENS ** 0.5), 384.0, ((1, 8),), jnp.float32),
        "mixing_v": jnp.clip(jnp.exp(math.log(16384.0) - 1.3862944 * jax.random.uniform(seeds[6], (4, D, D), jnp.float32) ** block_levels(seeds[6], (4, D, D), ((1, 8),), -0.2, 0.2)), 4096.0, 16384.0),
        "mixing_avg": bell_draw(seeds[7], (4, D, D), (D // 2) ** -0.5, 0.25, ((1, 8),), jnp.float32),
        "cond_w": bell_draw(seeds[8], (2, EMBED, D), (4 * EMBED) ** -0.5, 0.1875, ((1, 8),), jnp.float32),
        "cond_m": bell_draw(seeds[9], (2, EMBED, D), (1.0 * TOKENS ** 0.5), 768.0, ((1, 8),), jnp.float32),
        "cond_v": jnp.clip(jnp.exp(math.log(65536.0) - 1.3862944 * jax.random.uniform(seeds[10], (2, EMBED, D), jnp.float32) ** block_levels(seeds[10], (2, EMBED, D), ((1, 8),), -0.2, 0.2)), 16384.0, 65536.0),
        "cond_avg": bell_draw(seeds[11], (2, EMBED, D), (4 * EMBED) ** -0.5, 0.1875, ((1, 8),), jnp.float32),
        "up_w": bell_draw(seeds[12], (D, FF), D ** -0.5, 0.1875, ((0, 8),), jnp.float32),
        "up_m": bell_draw(seeds[13], (D, FF), (0.3 * TOKENS ** 0.5), 224.0, ((0, 8),), jnp.float32),
        "up_v": jnp.clip(jnp.exp(math.log(5957.0) - 1.3864622 * jax.random.uniform(seeds[14], (D, FF), jnp.float32) ** block_levels(seeds[14], (D, FF), ((0, 8),), -0.2, 0.2)), 1489.0, 5957.0),
        "up_avg": bell_draw(seeds[15], (D, FF), D ** -0.5, 0.1875, ((0, 8),), jnp.float32),
        "down_w": bell_draw(seeds[16], (FF, D), FF ** -0.5, 0.09375, ((0, 8),), jnp.float32),
        "down_m": bell_draw(seeds[17], (FF, D), (0.6 * TOKENS ** 0.5), 448.0, ((0, 8),), jnp.float32),
        "down_v": jnp.clip(jnp.exp(math.log(23592.0) - 1.3862944 * jax.random.uniform(seeds[18], (FF, D), jnp.float32) ** block_levels(seeds[18], (FF, D), ((0, 8),), -0.2, 0.2)), 5898.0, 23592.0),
        "down_avg": bell_draw(seeds[19], (FF, D), FF ** -0.5, 0.09375, ((0, 8),), jnp.float32),
    }


HIGH = lax.Precision.HIGHEST

@jax.custom_vjp
def low(v):
    return lax.optimization_barrier(v.astype(jnp.bfloat16)).astype(jnp.float32)

@jax.custom_vjp
def low_back(v):
    return v

def low_keep(v):
    return (low(v), None)

def low_pass(kept, grad):
    return (grad,)

def back_keep(v):
    return (v, None)

def back_low(kept, grad):
    return (low(grad),)
low.defvjp(low_keep, low_pass)
low_back.defvjp(back_keep, back_low)

def normed(values):
    center = values - lax.optimization_barrier(jnp.mean(values, axis=-1, keepdims=True))
    spread = lax.optimization_barrier(jnp.mean(center * center, axis=-1, keepdims=True))
    return center * lax.rsqrt(spread + 1e-05)

def rotary_tables(segments):
    length = segments.shape[0]
    position = jnp.arange(length, dtype=jnp.int32)
    is_start = jnp.concatenate([jnp.ones((1,), dtype=bool), segments[1:] != segments[:-1]])
    seg_start = lax.cummax(jnp.where(is_start, position, jnp.zeros_like(position)), axis=0)
    offset = (position - seg_start).astype(jnp.float32)
    frequency = 10000.0 ** (-jnp.arange(HEAD_DIM // 2, dtype=jnp.float32) * 2.0 / HEAD_DIM)
    turned = offset[:, None] * frequency[None, :]
    return (jnp.cos(turned)[:, None, :], jnp.sin(turned)[:, None, :])

def rotate(parts, cos_table, sin_table):
    half_dim = parts.shape[-1] // 2
    part_a = parts[..., :half_dim]
    part_b = parts[..., half_dim:]
    return jnp.concatenate([part_a * cos_table - part_b * sin_table, part_b * cos_table + part_a * sin_table], axis=-1)

def one_sequence(weights, rows_in, embed_one, seg_one):
    mixing, cond, up_proj, down_proj = weights
    length = rows_in.shape[0]
    scales = 1.0 + jnp.einsum('e,ked->kd', embed_one, cond, precision=HIGH)
    normed_one = low(normed(rows_in) * scales[0][None, :])
    projected = jnp.einsum('td,kde->kte', normed_one, mixing[:3], precision=HIGH)
    cos_table, sin_table = rotary_tables(seg_one)
    queries = low_back(projected[0]).reshape(length, HEADS, HEAD_DIM)
    keys_in = low_back(projected[1]).reshape(length, HEADS, HEAD_DIM)
    values_in = low(low_back(projected[2])).reshape(length, HEADS, HEAD_DIM)
    queries = low(rotate(queries, cos_table, sin_table))
    keys_in = low(rotate(keys_in, cos_table, sin_table))
    scores = low_back(jnp.einsum('qhd,khd->hqk', queries, keys_in, precision=HIGH) * 0.125)
    same_seg = seg_one[:, None] == seg_one[None, :]
    scores = jnp.where(same_seg[None], scores, -1e+30)
    peak = lax.optimization_barrier(jnp.max(scores, axis=-1, keepdims=True))
    exp_scores = jnp.exp(scores - peak)
    probs = low(exp_scores / lax.optimization_barrier(jnp.sum(exp_scores, axis=-1, keepdims=True)))
    attended = jnp.einsum('hqk,khd->qhd', probs, values_in, precision=HIGH)
    attended = low(low_back(attended.reshape(length, HEADS * HEAD_DIM)))
    branch = low_back(jnp.dot(attended, mixing[3], precision=HIGH))
    middle = rows_in + branch
    normed_two = low(normed(middle) * scales[1][None, :])
    hidden_pre = low_back(jnp.dot(normed_two, up_proj, precision=HIGH))
    hidden_act = low(jax.nn.gelu(hidden_pre))
    return middle + low_back(jnp.dot(hidden_act, down_proj, precision=HIGH))

def forward_pass(weights, tokens, embedding, segments):
    rounded = tuple((low(weight) for weight in weights))
    checked = jax.checkpoint(one_sequence)

    def scan_step(state_in, element):
        rows_in, embed_one, seg_one = element
        return (state_in, checked(rounded, rows_in, embed_one, seg_one))
    _, outputs = lax.scan(scan_step, jnp.zeros((), jnp.float32), (tokens, embedding, segments))
    return outputs

def adam_update(gradient, weight, moment_one, moment_two, average):
    moment_one_new = 0.5 * moment_one + 0.5 * gradient
    moment_two_new = 0.5 * moment_two + 0.5 * gradient * gradient
    correction = 1.0 - 0.5 ** STEP
    update = moment_one_new / correction / (jnp.sqrt(moment_two_new / correction) + 1e-08) + 0.1 * weight
    weight_new = weight - 0.01 * update
    average_new = 0.8 * average + 0.2 * weight_new
    return (moment_one_new, moment_two_new, weight_new, average_new)

def reference(tokens, time_embed, segment_ids, cotangent, mixing_w, mixing_m, mixing_v, mixing_avg, cond_w, cond_m, cond_v, cond_avg, up_w, up_m, up_v, up_avg, down_w, down_m, down_v, down_avg):
    embedding = time_embed.astype(jnp.float32)

    def whole_layer(weights, rows_all):
        return forward_pass(weights, rows_all, embedding, segment_ids)
    outputs, pullback = jax.vjp(whole_layer, (mixing_w, cond_w, up_w, down_w), tokens.astype(jnp.float32))
    weight_grads, input_grad = pullback(cotangent.astype(jnp.float32))
    mixing_grad, cond_grad, up_grad, down_grad = weight_grads
    mix_one, mix_two, mix_new, mix_average = adam_update(mixing_grad, mixing_w, mixing_m, mixing_v, mixing_avg)
    cond_one, cond_two, cond_new, cond_average = adam_update(cond_grad, cond_w, cond_m, cond_v, cond_avg)
    up_one, up_two, up_new, up_average = adam_update(up_grad, up_w, up_m, up_v, up_avg)
    down_one, down_two, down_new, down_average = adam_update(down_grad, down_w, down_m, down_v, down_avg)
    return (outputs.astype(jnp.bfloat16), input_grad.astype(jnp.bfloat16), mixing_grad, mix_one, mix_two, mix_new, mix_average, cond_grad, cond_one, cond_two, cond_new, cond_average, up_grad, up_one, up_two, up_new, up_average, down_grad, down_one, down_two, down_new, down_average)
```

```python
import jax
import jax.numpy as jnp
import numpy as np
from jax import lax
from jax.experimental import pallas as pl
from jax.experimental.pallas import tpu as pltpu
from jax.sharding import PartitionSpec as P

D = 1024
HEADS = 16
HEAD_DIM = 64
STEP = 7
F32 = jnp.float32
BF = jnp.bfloat16


MESH = pl.DeviceIdType.MESH
CHUNKS = 25
SLOTS = 4
SIB_SLOTS = 6
LINE_SLOTS = 6
LAGS = (1, 3, 5, 7, 9, 11)


class Reducer:
    def __init__(self, refs):
        (self.away, self.part, self.sib, self.diag, self.near, self.zin, self.zmid, self.tsum, self.out_a, self.out_b,
         self.sems_sib, self.sems_diag, self.sems_near, self.sems_zin, self.sems_zmid) = refs
        self.me = lax.axis_index("fsdp")
        self.core = lax.rem(self.me, 2)
        self.chip = lax.div(self.me, 2)
        self.row = lax.axis_index("rows")
        self.inner = jnp.logical_and(self.row >= 1, self.row <= 2)
        self.outer = jnp.logical_not(self.inner)
        self.line_to = jnp.where(self.row == 0, 1, jnp.where(self.row == 1, 0, jnp.where(self.row == 2, 3, 2)))
        self.mid_to = jnp.where(self.row == 1, 2, 1)
        xbit = lax.rem(self.chip, 2)
        ybit = lax.div(self.chip, 2)
        self.chip_x = ybit * 2 + (1 - xbit)
        self.chip_y = (1 - ybit) * 2 + xbit
        self.chip_d = (1 - ybit) * 2 + (1 - xbit)
        self.to_sib = {"fsdp": self.chip * 2 + (1 - self.core)}
        self.to_x = {"fsdp": self.chip_x * 2 + self.core}
        self.to_y = {"fsdp": self.chip_y * 2 + self.core}

    @staticmethod
    def scratch():
        s = SLOTS
        bf = jnp.bfloat16
        dma = pltpu.SemaphoreType.DMA
        return [
            pltpu.VMEM((SIB_SLOTS, 4, 128, 512), bf),
            pltpu.VMEM((s, 4, 128, 512), bf),
            pltpu.VMEM((SIB_SLOTS, 4, 128, 512), bf),
            pltpu.VMEM((s, 128, 512), bf),
            pltpu.VMEM((s, 2, 128, 512), bf),
            pltpu.VMEM((LINE_SLOTS, 128, 512), bf),
            pltpu.VMEM((LINE_SLOTS, 128, 512), bf),
            pltpu.VMEM((LINE_SLOTS, 128, 512), jnp.float32),
            pltpu.VMEM((LINE_SLOTS, 128, 512), bf),
            pltpu.VMEM((LINE_SLOTS, 128, 512), bf),
            dma((2, SIB_SLOTS)),
            dma((2, s)),
            dma((2, s)),
            dma((2, LINE_SLOTS)),
            dma((2, LINE_SLOTS)),
        ]

    def enter(self):
        barrier = pltpu.get_barrier_semaphore()
        for to in (self.to_sib, self.to_x, self.to_y, {"rows": self.line_to}):
            pl.semaphore_signal(barrier, inc=1, device_id=to, device_id_type=MESH)

        @pl.when(self.inner)
        def _():
            pl.semaphore_signal(barrier, inc=1, device_id={"rows": self.mid_to}, device_id_type=MESH)
            pl.semaphore_wait(barrier, 5)

        @pl.when(self.outer)
        def _():
            pl.semaphore_wait(barrier, 4)

    def copy(self, src, dst, sems, which, slot, to):
        return pltpu.make_async_remote_copy(
            src_ref=src, dst_ref=dst, send_sem=sems.at[which, slot], recv_sem=sems.at[which + sems.shape[0] // 2, slot],
            device_id=to, device_id_type=MESH)

    def c_sib(self, s):
        return self.copy(self.away.at[s], self.sib.at[s], self.sems_sib, 0, s, self.to_sib)

    def c_diag(self, s, k):
        to, half = (self.to_x if k == 0 else self.to_y), pl.ds(64 * k, 64)
        return self.copy(self.part.at[s, self.chip_d, half], self.diag.at[s, half], self.sems_diag, 0, s, to)

    def c_near(self, s, k):
        to, chip = (self.to_x, self.chip_x) if k == 0 else (self.to_y, self.chip_y)
        return self.copy(self.part.at[s, chip], self.near.at[s, k], self.sems_near, 0, s, to)

    def both_diag(self, s):
        return self.copy(self.part.at[s, self.chip_d], self.diag.at[s], self.sems_diag, 0, s, self.to_x)

    def both_near(self, s):
        return self.copy(self.part.at[s, pl.ds(0, 2)], self.near.at[s], self.sems_near, 0, s, self.to_x)

    def c_line(self, s):
        return self.copy(self.out_a.at[s], self.zin.at[s], self.sems_zin, 0, s, {"rows": self.line_to})

    def c_mid(self, s):
        return self.copy(self.out_b.at[s], self.zmid.at[s], self.sems_zmid, 0, s, {"rows": self.mid_to})

    def stage_b(self, g, keep):
        s = lax.rem(g, SLOTS)
        n = lax.rem(g, SIB_SLOTS)
        self.c_sib(n).wait()
        keep(g, s, n)
        self.c_diag(s, 0).start()
        self.c_diag(s, 1).start()

    def stage_c(self, g):
        s = lax.rem(g, SLOTS)
        self.both_diag(s).wait()
        lo = self.part[s, self.chip_y, :64].astype(jnp.float32) + self.diag[s, :64].astype(jnp.float32)
        self.part[s, self.chip_y, :64] = lo.astype(jnp.bfloat16)
        self.c_near(s, 1).start()
        hi = self.part[s, self.chip_x, 64:].astype(jnp.float32) + self.diag[s, 64:].astype(jnp.float32)
        self.part[s, self.chip_x, 64:] = hi.astype(jnp.bfloat16)
        self.c_near(s, 0).start()

    def stage_e(self, g):
        s = lax.rem(g, SLOTS)
        self.both_near(s).wait()
        total = (self.part[s, self.chip].astype(jnp.float32) + self.near[s, 0].astype(jnp.float32)) + self.near[s, 1].astype(jnp.float32)
        n = lax.rem(g, LINE_SLOTS)
        self.tsum[n] = total

        @pl.when(self.outer)
        def _():
            self.out_a[n] = total.astype(jnp.bfloat16)
            self.c_line(n).start()

    def stage_f(self, g):
        s = lax.rem(g, LINE_SLOTS)

        @pl.when(self.inner)
        def _():
            self.c_line(s).wait_recv()
            self.out_b[s] = (self.tsum[s] + self.zin[s].astype(jnp.float32)).astype(jnp.bfloat16)
            self.c_mid(s).start()

    def stage_h(self, g, put):
        s = lax.rem(g, LINE_SLOTS)

        @pl.when(self.inner)
        def _():
            self.c_mid(s).wait()
            total = (self.out_b[s].astype(jnp.float32) + self.zmid[s].astype(jnp.float32)).astype(jnp.bfloat16)
            self.out_a[s] = total
            self.c_line(s).start()
            put(g, total)

    def stage_i(self, g, put):
        s = lax.rem(g, LINE_SLOTS)

        @pl.when(self.outer)
        def _():
            self.c_line(s).wait()
            put(g, self.zin[s])

        @pl.when(self.inner)
        def _():
            self.c_line(s).wait_send()

    def tick(self, t, keep, put):
        b, c, e, f, h, i = LAGS

        def run(lag, stage, *args):
            g = t - lag
            pl.when(jnp.logical_and(g >= 0, g < CHUNKS))(lambda: stage(g, *args))

        run(i, self.stage_i, put)
        run(h, self.stage_h, put)
        run(f, self.stage_f)
        run(e, self.stage_e)
        run(c, self.stage_c)
        run(b, self.stage_b, keep)


def dot(a, b):
    return lax.dot_general(a, b, (((1,), (0,)), ((), ())), preferred_element_type=F32)


def dot_nt(a, b):
    return lax.dot_general(a, b, (((1,), (1,)), ((), ())), preferred_element_type=F32)


START, LINK, SIBLING, HOP, ISSUE, LEAD = 6.0, 50.0, 300.0, 2.0, 0.05, 4.0
PIECES = [(-1, 0, 1024, True)]
PIECES += [(k, 512 * h, 512, k == 2 and h == 0) for h in range(2) for k in range(3)]
PIECES += [(-2, 0, 1024, True), (3, 0, 1024, False)]
PIECES += [(4 + n, 0, 1024, n in (1, 4, 6, 7)) for n in range(8)]
COND_TWO, OUT_W, UP_W, DOWN_W = 7, 8, 9, 13


SHARED = {4: 3, 5: 0, 6: 0, 7: 0, 9: 8, 10: 8}


class Gatherer:
    def __init__(self, refs):
        self.cond, self.thirds, self.mats, self.send, self.recv = refs
        self.me = lax.axis_index("fsdp")
        core = lax.rem(self.me, 2)
        chip = lax.div(self.me, 2)
        xbit, ybit = lax.rem(chip, 2), lax.div(chip, 2)
        self.x = (ybit * 2 + 1 - xbit) * 2 + core
        self.y = ((1 - ybit) * 2 + xbit) * 2 + core
        self.d = ((1 - ybit) * 2 + 1 - xbit) * 2 + core
        self.sib = chip * 2 + 1 - core
        row = lax.axis_index("rows")
        self.half = lax.rem(row, 2)
        self.to_z = {"rows": row + 1 - 2 * self.half}
        self.time = START
        self.free = {"x": 0.0, "y": 0.0, "z": 0.0, "s": 0.0}
        self.due = {}
        self.waiting = []
        self.begun, self.whole = 0, set()

    @staticmethod
    def scratch():
        return [
            pltpu.VMEM((8, 64, 1024), BF),
            pltpu.VMEM((3, 2, 8, 128, 512), BF),
            pltpu.VMEM((9, 8, 128, 1024), BF),
            pltpu.SemaphoreType.DMA((len(PIECES), 11)),
            pltpu.SemaphoreType.DMA((len(PIECES), 11)),
        ]

    def enter(self):
        barrier = pltpu.get_barrier_semaphore()
        for to in ({"fsdp": self.sib}, {"fsdp": self.x}, {"fsdp": self.y}, self.to_z):
            pl.semaphore_signal(barrier, inc=1, device_id=to, device_id_type=MESH)
        pl.semaphore_wait(barrier, 4)

    @staticmethod
    def direct(c):
        return PIECES[c][3]

    def shard(self, c, owner, start=0, size=None):
        mat, col, cols, _ = PIECES[c]
        if mat < 0:
            base = 32 * (-1 - mat)
            return self.cond.at[owner, pl.ds(base + start, 32 if size is None else size)]
        rows = pl.ds(start, 128 if size is None else size)
        return self.thirds.at[mat, col // 512, owner, rows] if mat < 3 else self.mats.at[mat - 3, owner, rows]

    def copy(self, c, kind, owner, to, start=0, size=None):
        ref = self.shard(c, owner, start, size)
        return pltpu.make_async_remote_copy(
            src_ref=ref, dst_ref=ref, send_sem=self.send.at[c, kind], recv_sem=self.recv.at[c, SHARED.get(kind, kind)],
            device_id=to, device_id_type=MESH)

    def landed(self, c, kind, rows):
        mat, _, cols, _ = PIECES[c]
        if mat < 0:
            ref = self.cond.at[pl.ds(0, 4), pl.ds(0, 32)] if rows == 128 else self.cond.at[0, pl.ds(0, rows)]
        else:
            base = self.thirds.at[mat, 0] if mat < 3 else self.mats.at[mat - 3]
            ref = base.at[pl.ds(0, rows // 128)] if rows >= 128 else base.at[0, pl.ds(0, rows)]
            if rows == 192:
                ref = base.at[pl.ds(0, 3), pl.ds(0, 64)]
        pltpu.make_async_remote_copy(
            src_ref=ref, dst_ref=ref, send_sem=self.send.at[c, kind], recv_sem=self.recv.at[c, kind],
            device_id={"fsdp": self.sib}, device_id_type=MESH).wait_recv()

    def span(self, c, k=None):
        rows = 32 if PIECES[c][0] < 0 else 128
        if self.direct(c):
            return (0, None) if k is None else (k * (rows // 2), rows // 2)
        return (self.half * 64, 64) if k is None else (self.half * 64 + 32 * k, 32)

    def post(self, link, mark, copy):
        copy.start()
        rows, cols = copy.src_ref.shape[-2:]
        self.time += ISSUE
        self.free[link] = max(self.free[link], self.time) + rows * cols * 2e-3 / (SIBLING if link == "s" else LINK)
        self.due[mark] = self.free[link] + HOP

    def take(self, mark, copy):
        copy.wait_recv()
        self.time = max(self.time, self.due[mark]) + ISSUE

    def take_all(self, c, kinds, rows):
        self.landed(c, kinds[0], rows)
        self.time = max([self.time] + [self.due[c, kind] for kind in kinds]) + ISSUE

    def onward(self, c, kind, owner):
        if self.direct(c):
            self.post("s", (c, 5 + kind), self.copy(c, 5 + kind, owner, {"fsdp": self.sib}))
        else:
            self.post("z", (c, 8 + kind), self.copy(c, 8 + kind, owner, self.to_z, *self.span(c)))

    def s1(self, c):
        self.post("x", (c, 1), self.copy(c, 1, self.me, {"fsdp": self.x}, *self.span(c)))
        self.post("y", (c, 2), self.copy(c, 2, self.me, {"fsdp": self.y}, *self.span(c)))
        self.post("s", (c, 0), self.copy(c, 0, self.me, {"fsdp": self.sib}))
        self.begun = c + 1
        self.waiting.append((2, c))

    def s2(self, c):
        self.take((c, 1), self.copy(c, 1, self.x, {"fsdp": self.x}, *self.span(c)))
        self.post("y", (c, 3), self.copy(c, 3, self.x, {"fsdp": self.y}, *self.span(c, 0)))
        self.onward(c, 0, self.x)
        self.take((c, 2), self.copy(c, 2, self.y, {"fsdp": self.y}, *self.span(c)))
        self.post("x", (c, 4), self.copy(c, 4, self.y, {"fsdp": self.x}, *self.span(c, 1)))
        self.onward(c, 1, self.y)
        self.waiting.append((3, c))

    def s3(self, c):
        self.take_all(c, (3, 4), self.moved(c))
        self.onward(c, 2, self.d)
        self.waiting.append((5 if self.direct(c) else 4, c))

    def s4(self, c):
        self.take_all(c, (8, 9, 10), 192)
        for kind, owner in enumerate((self.x, self.y, self.d)):
            self.post("s", (c, 5 + kind), self.copy(c, 5 + kind, owner, {"fsdp": self.sib}))
        self.waiting.append((5, c))

    def moved(self, c):
        rows = 32 if PIECES[c][0] < 0 else 128
        return rows if self.direct(c) else rows // 2

    def s5(self, c):
        self.take_all(c, (0, 5, 6, 7), 128 if PIECES[c][0] < 0 else 512)
        self.whole.add(c)

    def ready(self, event):
        stage, c = event
        marks = {2: (1, 2), 3: (3, 4), 4: (8, 9, 10), 5: (0, 5, 6, 7)}[stage]
        return max(self.due[c, kind] for kind in marks)

    def feed(self):
        while self.begun < len(PIECES) and min(self.free["x"], self.free["y"]) - self.time < LEAD:
            self.s1(self.begun)

    def step(self, event):
        self.waiting.remove(event)
        stage, c = event
        (self.s2, self.s3, self.s4, self.s5)[stage - 2](c)

    def spend(self, time):
        self.time += time
        while True:
            self.feed()
            landed = [event for event in self.waiting if self.ready(event) <= self.time]
            if not landed:
                break
            self.step(min(landed, key=lambda event: (self.ready(event), event)))

    def need(self, c):
        while c not in self.whole:
            self.feed()
            self.step(min(self.waiting, key=lambda event: (self.ready(event), event)))

    def finish(self):
        for c in range(len(PIECES)):
            self.copy(c, 0, self.me, {"fsdp": self.sib}).wait_send()
            for kind in (1, 2):
                self.copy(c, kind, self.me, {"fsdp": self.x}, *self.span(c)).wait_send()
            for k in range(2):
                self.copy(c, 3 + k, self.x, {"fsdp": self.x}, *self.span(c, k)).wait_send()
            for kind in range(3):
                self.copy(c, 5 + kind, self.x, {"fsdp": self.sib}).wait_send()
                if not self.direct(c):
                    self.copy(c, 8 + kind, self.x, self.to_z, *self.span(c)).wait_send()


def forward_kernel(
    seg_in, freq_in, te_in, x_in, cot_hbm, mixing_hbm, cond_hbm, up_hbm, down_hbm,
    lse_out, scales_out, turn_out, feat_out, thirds_hbm, w_hbm, lt_hbm, dpre_hbm, qkv_hbm, mid_hbm, back_hbm, out_hbm,
    four, wide, condf, nrm, qkv, att, mid, te_at, act, cot, ltb, gbuf, eye, in_sem, w_sem, lt_sem, g_sem, o_sem, *shared,
):
    gat = Gatherer(shared)
    me = gat.me
    thirds, mats = gat.thirds, gat.mats

    def load(src, dst, n):
        return pltpu.make_async_copy(src, dst, in_sem.at[n])

    loads = [load(cond_hbm, condf, 0)]
    loads += [load(mixing_hbm.at[k], four.at[k], 1 + k) for k in range(4)]
    loads += [load(up_hbm, wide, 5), load(cot_hbm, cot, 6)]
    for copy in loads:
        copy.start()
    gat.enter()
    obuf = att
    loads[0].wait()
    for k in range(2):
        gat.cond[me, 32 * k:32 * k + 32] = condf[k].astype(BF)
    gat.s1(0)
    for k in range(4):
        loads[1 + k].wait()
        if k < 3:
            for h in range(2):
                thirds[k, h, me] = four[k, :, 512 * h:512 * h + 512].astype(BF)
            if k < 2:
                gat.s1(1 + k)
        else:
            mats[0, me] = four[k].astype(BF)
    later = [load(down_hbm.at[pl.ds(128 * i, 128)], four.at[i], 7 + i) for i in range(4)]
    for copy in later:
        copy.start()
    ids = seg_in[...].astype(F32)
    column = jnp.broadcast_to(ids, (128, 512)).T[:, :1]
    before = jnp.sum(jnp.where(ids < column, 1.0, 0.0), axis=1, keepdims=True)
    offset = lax.broadcasted_iota(jnp.int32, (512, 1), 0).astype(F32) - before
    angle = offset * freq_in[...]
    lanes = lax.broadcasted_iota(jnp.int32, (1, 128), 1)
    lane_in = lax.rem(lanes, 64)
    low_half = lane_in < 32
    turn_out[0] = jnp.cos(angle)
    turn_out[1] = jnp.where(low_half, -1.0, 1.0) * jnp.sin(angle)
    spot = lane_in.astype(F32)
    square = (lax.broadcasted_iota(jnp.int32, (256, 256), n) for n in range(2))
    eye[...] = jnp.where(next(square) == next(square), 1.0, 0.0).astype(BF)
    feat_out[0] = jnp.where(jnp.logical_and(lane_in < 4, spot != column), 1.0, 0.0).astype(BF)
    feat_out[1] = jnp.where(spot == column, -1e30, 0.0).astype(BF)
    te_column = jnp.broadcast_to(te_in[...].astype(F32), (128, 256)).T[:, :1]
    for f in range(8):
        te_at[f] = te_column[32 * f:32 * f + 32]
    loads[5].wait()
    for i in range(4):
        for f in range(8):
            mats[1 + i, me, :, 128 * f:128 * f + 128] = wide[:, 512 * f + 128 * i:512 * f + 128 * i + 128].astype(BF)
    for i in range(4):
        later[i].wait()
        mats[5 + i, me] = four[i].astype(BF)

    def save_w(m):
        if m < 3:
            return pltpu.make_async_copy(thirds.at[m], thirds_hbm.at[m], w_sem.at[m])
        return pltpu.make_async_copy(mats.at[0], w_hbm, w_sem.at[m])

    def save_lt(n, slot):
        return pltpu.make_async_copy(ltb.at[slot], lt_hbm.at[n], lt_sem.at[slot])

    def turn(block, b, slot):
        rows = slice(128 * b, 128 * b + 128) if isinstance(b, int) else pl.ds(pl.multiple_of(b * 128, 128), 128)
        turned = dot_nt(eye[...], block).astype(BF)
        for a in range(2):
            ltb[slot, a, rows] = turned[128 * a:128 * a + 128]

    def scale_of(k):
        total = jnp.zeros((32, 1024), F32)
        for f in range(8):
            total = total + te_at[f] * gat.cond[f, 32 * k:32 * k + 32].astype(F32)
        scales_out[k:k + 1] = 1.0 + jnp.sum(total, axis=0, keepdims=True)

    def norm_rows(source, scale):
        def block(b, carry):
            rows = pl.ds(pl.multiple_of(b * 64, 64), 64)
            values = source[rows].astype(F32)
            center = values - jnp.mean(values, axis=-1, keepdims=True)
            spread = jnp.mean(center * center, axis=-1, keepdims=True)
            nrm[rows] = (center * lax.rsqrt(spread + 1e-05) * scale).astype(BF)
            return carry

        lax.fori_loop(0, 8, block, 0, unroll=2)

    gat.need(0)
    scale_of(0)
    norm_rows(x_in, scales_out[0:1])
    gat.spend(1.2)

    def save_qkv(k):
        return pltpu.make_async_copy(qkv.at[k], qkv_hbm.at[k], o_sem.at[k])

    def project(k, half):
        at = slice(512 * half, 512 * half + 512)
        result = dot(nrm[...], thirds[k, half].reshape(1024, 512))
        if k == 0:
            for b in range(2):
                turn(nrm[:, 512 * half + 256 * b:512 * half + 256 * b + 256], 2 * half + b, 0)
        if k < 2:
            sides = []
            for n in range(4):
                part = result[:, 128 * n:128 * n + 128]
                other = jnp.where(low_half, pltpu.roll(part, 96, 1), pltpu.roll(part, 32, 1))
                sides.append(part * turn_out[0] + other * turn_out[1])
            result = jnp.concatenate(sides, axis=1)
        result = result.astype(BF)
        qkv[k, :, at] = result * jnp.asarray(0.125, BF) if k == 0 else result

    def attend(pair, carry):
        at = pl.ds(pl.multiple_of(pair * 128, 128), 128)
        q_pair, k_pair = qkv[0, :, at], qkv[1, :, at]
        v_turned = qkv[2, :, at].T
        heads = [lax.div(lanes, 64) == j for j in range(2)]
        raws = [dot_nt(jnp.where(mine, k_pair, feat_out[1]), jnp.where(mine, q_pair, feat_out[0])) for mine in heads]
        peaks = [jnp.max(raw, axis=0, keepdims=True) for raw in raws]
        grown = [jnp.exp(raw - peak) for raw, peak in zip(raws, peaks)]
        totals = [jnp.sum(value, axis=0, keepdims=True) for value in grown]
        sides = [dot(v_turned[64 * j:64 * j + 64], grown[j].astype(BF)) * (1.0 / totals[j]) for j in range(2)]
        sums = [peak + jnp.log(total) for peak, total in zip(peaks, totals)]
        lse_out[pair] = jnp.concatenate(sums, axis=0)
        block = jnp.concatenate(sides, axis=0).astype(BF)
        ltb[1, lax.rem(pair, 2), pl.ds(pl.multiple_of(lax.div(pair, 2) * 128, 128), 128)] = block
        att[:, at] = block.T
        return carry

    for half in range(2):
        for k in range(3):
            gat.need(1 + 3 * half + k)
            project(k, half)
            gat.spend(0.9)
        if half == 1:
            for k in range(3):
                save_w(k).start()
                save_qkv(k).start()
            save_lt(6, 0).start()
        for part in range(2):
            begin = 4 * half + 2 * part
            lax.fori_loop(begin, begin + 2, attend, 0)
            gat.spend(3.6)
    save_lt(5, 1).start()
    gat.need(COND_TWO)
    scale_of(1)
    gat.need(OUT_W)
    save_w(3).start()

    def join(b, carry):
        at = pl.ds(pl.multiple_of(b * 512, 512), 512)
        mid[:, at] = x_in[:, at].astype(F32) + dot(att[...], mats[0, :, :, at].reshape(1024, 512))
        return carry

    lax.fori_loop(0, 2, join, 0)
    gat.spend(1.8)
    save_mid = pltpu.make_async_copy(mid, mid_hbm, o_sem.at[3])
    save_mid.start()
    norm_rows(mid, scales_out[1:2])
    gat.spend(2.4)
    befores = {0: 6, 1: 5, 2: 4}

    def save_dpre(i):
        return pltpu.make_async_copy(gbuf.at[i], dpre_hbm.at[i], g_sem.at[i])

    for i in range(4):
        gat.need(UP_W + i)
        save_lt(befores[i % 3], i % 3).wait()

        def expand(b, carry):
            at = pl.ds(pl.multiple_of(b * 512, 512), 512)
            u = dot(nrm[...], mats[1 + i, :, :, at].reshape(1024, 512))
            root = 0.7978845608028654
            square = u * u
            bend = jnp.tanh(root * u * (1.0 + 0.044715 * square))
            side = 0.5 * (1.0 + bend)
            result = (u * side).astype(BF)
            act[i, :, at] = result
            for n in range(2):
                turn(result[:, 256 * n:256 * n + 256], 2 * b + n, i % 3)
                if i == 0:
                    turn(nrm[:, pl.ds(pl.multiple_of(b * 512 + n * 256, 256), 256)], 2 * b + n, 2)
            slope = side + 0.5 * u * (1.0 - bend * bend) * (root * (1.0 + 3.0 * 0.044715 * square))
            gbuf[i, :, at] = slope.astype(BF)
            return carry

        lax.fori_loop(0, 2, expand, 0)
        save_lt(i, i % 3).start()
        befores[i % 3] = i
        if i == 0:
            save_lt(4, 2).start()
        gat.spend(3.0)
    for i in range(4):
        gat.need(DOWN_W + i)
        if i == 0:
            loads[6].wait()

        def slopes(b, carry):
            at = pl.ds(pl.multiple_of(b * 512, 512), 512)
            d_act = dot_nt(cot[...], mats[5 + i, pl.ds(4 * b, 4)].reshape(512, 1024))
            gbuf[i, :, at] = (d_act * gbuf[i, :, at].astype(F32)).astype(BF)
            return carry

        lax.fori_loop(0, 2, slopes, 0)
        save_dpre(i).start()
        gat.spend(1.2)

    def shrink(b, carry):
        at = pl.ds(pl.multiple_of(b * 512, 512), 512)
        total = mid[:, at]
        for i in range(4):
            total = total + dot(act[i], mats[5 + i, :, :, at].reshape(1024, 512))
        obuf[:, at] = total.astype(BF)
        back = dot_nt(gbuf[0], mats[1, pl.ds(4 * b, 4)].reshape(512, 1024))
        for i in range(1, 4):
            back = back + dot_nt(gbuf[i], mats[1 + i, pl.ds(4 * b, 4)].reshape(512, 1024))
        four[:, :, at] = back.reshape(4, 128, 512)
        return carry

    lax.fori_loop(0, 2, shrink, 0)
    save_out = pltpu.make_async_copy(obuf, out_hbm, o_sem.at[4])
    save_out.start()
    save_back = pltpu.make_async_copy(four, back_hbm, o_sem.at[5])
    save_back.start()
    gat.finish()
    for m in range(4):
        save_w(m).wait()
    for k in range(3):
        save_qkv(k).wait()
        save_lt(befores[k], k).wait()
    save_mid.wait()
    for i in range(4):
        save_dpre(i).wait()
    save_out.wait()
    save_back.wait()


def forward(seg, te, x, cot, mixing_w, cond_w, up_w, down_w):
    vmem = pl.BlockSpec(memory_space=pltpu.VMEM)
    anyw = pl.BlockSpec(memory_space=pl.ANY)
    shape = jax.ShapeDtypeStruct
    freq = 10000.0 ** (-(np.arange(128) % 32) * 2.0 / HEAD_DIM)
    return pl.pallas_call(
        forward_kernel,
        out_shape=(
            shape((8, 2, 512), F32), shape((2, 1024), F32), shape((2, 512, 128), F32), shape((2, 512, 128), BF),
            shape((3, 2, 8, 128, 512), BF), shape((8, 128, 1024), BF), shape((7, 2, 512, 512), BF), shape((4, 512, 1024), BF),
            shape((3, 512, 1024), BF), shape((512, 1024), F32), shape((4, 128, 1024), F32), shape((512, 1024), BF)),
        in_specs=[vmem] * 4 + [anyw] * 5,
        out_specs=(vmem,) * 4 + (anyw,) * 8,
        scratch_shapes=[
            pltpu.VMEM((4, 128, 1024), F32),
            pltpu.VMEM((128, 4096), F32),
            pltpu.VMEM((2, 32, 1024), F32),
            pltpu.VMEM((512, 1024), BF),
            pltpu.VMEM((3, 512, 1024), BF),
            pltpu.VMEM((512, 1024), BF),
            pltpu.VMEM((512, 1024), F32),
            pltpu.VMEM((8, 32, 1), F32),
            pltpu.VMEM((4, 512, 1024), BF),
            pltpu.VMEM((512, 1024), BF),
            pltpu.VMEM((3, 2, 512, 512), BF),
            pltpu.VMEM((4, 512, 1024), BF),
            pltpu.VMEM((256, 256), BF),
            pltpu.SemaphoreType.DMA((11,)),
            pltpu.SemaphoreType.DMA((4,)),
            pltpu.SemaphoreType.DMA((3,)),
            pltpu.SemaphoreType.DMA((4,)),
            pltpu.SemaphoreType.DMA((6,)),
        ] + Gatherer.scratch(),
        compiler_params=pltpu.CompilerParams(collective_id=2, has_side_effects=True, vmem_limit_bytes=63 * 2**20),
    )(seg, jnp.asarray(freq[None], F32), te, x, cot, mixing_w, cond_w, up_w, down_w)


def norm_back(values, grads, scale):
    center = values - jnp.mean(values, axis=-1, keepdims=True)
    recip = lax.rsqrt(jnp.mean(center * center, axis=-1, keepdims=True) + 1e-05)
    unit = center * recip
    g = grads * scale
    back = recip * (g - jnp.mean(g, axis=-1, keepdims=True) - unit * jnp.mean(g * unit, axis=-1, keepdims=True))
    return back, grads * unit


def backward_kernel(
    turn_in, lse_in, scales_in, te_in, feat_in, thirds_hbm, w_hbm, lt_hbm, cot_hbm, dpre_hbm, qkv_hbm, mid_hbm, back_hbm, x_hbm,
    sums, in_grad,
    lt, rh, thirds, wout, qkv, mid, acc, dmid, datt, xin, dscale, obuf, te_at, load_sem, out_sem, *shared,
):
    red = Reducer(shared)
    core = red.core

    def load(src, dst, n):
        return pltpu.make_async_copy(src, dst, load_sem.at[n])

    load_lt = [load(lt_hbm.at[n], lt.at[n], n) for n in range(7)]
    load_cot = load(cot_hbm, rh.at[0], 7)
    load_mid = load(mid_hbm, mid, 8)
    load_back = load(back_hbm, acc, 9)
    load_w3 = load(w_hbm, wout, 10)
    load_qkv = load(qkv_hbm, qkv, 11)
    load_dpre = load(dpre_hbm, rh.at[pl.ds(1, 4)], 12)
    load_w = load(thirds_hbm, thirds, 13)
    load_x = load(x_hbm, xin, 14)
    for copy in (load_cot, load_lt[0], load_mid, load_back, load_w3):
        copy.start()
    later = (load_lt[1], load_qkv, load_lt[2], load_lt[3], load_lt[4], load_dpre, load_lt[5], load_w, load_lt[6], load_x)
    arrivals = {1: (load_lt[1], load_qkv), 2: (load_lt[2],), 3: (load_lt[3],), 4: (load_lt[4], load_dpre), 8: (load_lt[5],),
                9: (load_lt[6], load_w, load_x)}
    red.enter()

    def operands(g):
        left = jnp.where(g < 8, lax.div(g, 2), jnp.where(g < 16, 4, jnp.where(g < 18, 5, 6)))
        right = jnp.where(g < 8, 0, jnp.where(g < 16, 1 + lax.div(g - 8, 2), jnp.where(g < 18, 5, 6 + lax.div(g - 18, 2))))
        return left, rh[right, :, pl.ds(pl.multiple_of(lax.rem(g, 2) * 512, 512), 512)]

    def give(g):
        left, right = operands(g)
        n = lax.rem(g, SIB_SLOTS)
        red.away[n] = dot(lt[left, 1 - core], right).astype(BF).reshape(4, 128, 512)
        red.c_sib(n).start()

    def cond_part(parity):
        rows = []
        for chip in range(4):
            column = te_at[2 * chip + parity]
            rows.append(jnp.concatenate([column * dscale[k:k + 1, 512 * h:512 * h + 512] for k in range(2) for h in range(2)], axis=0)[None])
        return jnp.concatenate(rows, axis=0)

    def keep(g, s, n):
        @pl.when(g < CHUNKS - 1)
        def _():
            left, right = operands(g)
            own = dot(lt[left, core], right).reshape(4, 128, 512)
            red.part[s] = (own + red.sib[n].astype(F32)).astype(BF)

        @pl.when(g == CHUNKS - 1)
        def _():
            red.part[s] = (cond_part(core) + red.sib[n].astype(F32)).astype(BF)

    def put(g, value):
        sums[g] = value

    te_column = jnp.broadcast_to(te_in[...].astype(F32), (128, 256)).T[:, :1]
    for f in range(8):
        te_at[f] = te_column[32 * f:32 * f + 32]
    lanes = lax.broadcasted_iota(jnp.int32, (1, 128), 1)
    low_half = lax.rem(lanes, 64) < 32

    def unrotate(block):
        other = jnp.where(low_half, pltpu.roll(block, 96, 1), pltpu.roll(block, 32, 1))
        return block * turn_in[0] - other * turn_in[1]

    def middle_back():
        for copy in later:
            copy.start()
        load_mid.wait()
        load_back.wait()

        def norm_two(b, total):
            rows = pl.ds(pl.multiple_of(b * 64, 64), 64)
            back, terms = norm_back(mid[rows], acc[rows], scales_in[1:2])
            back = back + rh[0, rows].astype(F32)
            dmid[rows] = back
            rh[5, rows] = back.astype(BF)
            return total + jnp.sum(terms.reshape(8, 8, 1024), axis=0)

        total = lax.fori_loop(0, 8, norm_two, jnp.zeros((8, 1024), F32), unroll=2)
        dscale[1:2] = jnp.sum(total, axis=0, keepdims=True)
        load_w3.wait()
        for n in range(2):
            cols = slice(512 * n, 512 * n + 512)
            datt[:, cols] = dot_nt(rh[5], wout[cols, :]).astype(BF)

    def attend_back(pair):
        at = pl.ds(pl.multiple_of(pair * 128, 128), 128)
        q_pair, k_pair, v_pair, d_pair = qkv[0, :, at], qkv[1, :, at], qkv[2, :, at], datt[:, at]
        k_turned = (k_pair * jnp.asarray(0.125, BF)).T
        heads = [lax.div(lanes, 64) == j for j in range(2)]
        raws = [dot_nt(jnp.where(mine, k_pair, feat_in[1]), jnp.where(mine, q_pair, feat_in[0])) for mine in heads]
        d_probs = [dot_nt(v_pair, jnp.where(mine, d_pair, jnp.zeros_like(d_pair))) for mine in heads]
        made = []
        for j in range(2):
            probs = jnp.exp(raws[j] - lse_in[pair, j:j + 1])
            delta = jnp.sum(probs * d_probs[j], axis=0, keepdims=True)
            d_raw = (probs * (d_probs[j] - delta)).astype(BF)
            made.append((dot(k_turned[64 * j:64 * j + 64], d_raw), dot(d_raw, q_pair), dot(probs.astype(BF), d_pair)))
        rh[6, :, at] = unrotate(jnp.concatenate([made[0][0], made[1][0]], axis=0).T).astype(BF)
        rh[7, :, at] = unrotate(jnp.where(heads[0], made[0][1], made[1][1])).astype(BF)
        rh[8, :, at] = jnp.where(heads[0], made[0][2], made[1][2]).astype(BF)

    def first_back(k):
        for h in range(2):
            cols = slice(512 * h, 512 * h + 512)
            part = dot_nt(rh[6 + k, :, :512], thirds[k, 0, cols]) + dot_nt(rh[6 + k, :, 512:], thirds[k, 1, cols])

            @pl.when(k == 0)
            def _():
                acc[:, cols] = part

            @pl.when(k > 0)
            def _():
                acc[:, cols] += part

    def input_back():
        def norm_one(b, total):
            rows = pl.ds(pl.multiple_of(b * 64, 64), 64)
            back, terms = norm_back(xin[rows].astype(F32), acc[rows], scales_in[0:1])
            obuf[rows] = (dmid[rows] + back).astype(BF)
            return total + jnp.sum(terms.reshape(8, 8, 1024), axis=0)

        total = lax.fori_loop(0, 8, norm_one, jnp.zeros((8, 1024), F32), unroll=2)
        dscale[0:1] = jnp.sum(total, axis=0, keepdims=True)
        store_out.start()
        n = (CHUNKS - 1) % SIB_SLOTS
        red.away[n] = cond_part(1 - core).astype(BF)
        red.c_sib(n).start()

    store_out = pltpu.make_async_copy(obuf, in_grad, out_sem)
    load_cot.wait()
    load_lt[0].wait()

    def turn(m, carry):
        for when, copies in arrivals.items():
            @pl.when(m == when)
            def _(copies=copies):
                for copy in copies:
                    copy.wait()

        @pl.when(m < 12)
        def _():
            give(2 * m)
            give(2 * m + 1)

        pl.when(m == 0)(middle_back)
        pl.when(jnp.logical_and(m >= 1, m < 9))(lambda: attend_back(m - 1))

        pl.when(jnp.logical_and(m >= 9, m < 12))(lambda: first_back(m - 9))
        pl.when(m == 12)(input_back)
        def ticks(t, carry):
            red.tick(t, keep, put)
            return carry

        lax.fori_loop(2 * m, 2 * m + 2, ticks, 0)

        return carry

    lax.fori_loop(0, (CHUNKS + LAGS[-1] + 1) // 2, turn, 0)
    store_out.wait()


def backward(turn, lse, scales, te, feat, thirds, w, lt, cot, dpre, qkv, mid, back, x):
    vmem = pl.BlockSpec(memory_space=pltpu.VMEM)
    anyw = pl.BlockSpec(memory_space=pl.ANY)
    shape = jax.ShapeDtypeStruct
    return pl.pallas_call(
        backward_kernel,
        out_shape=(
            shape((CHUNKS, 128, 512), BF), shape((512, 1024), BF)),
        in_specs=[vmem] * 5 + [anyw] * 9,
        out_specs=(vmem, anyw),
        scratch_shapes=[
            pltpu.VMEM((7, 2, 512, 512), BF),
            pltpu.VMEM((9, 512, 1024), BF),
            pltpu.VMEM((3, 2, 1024, 512), BF),
            pltpu.VMEM((1024, 1024), BF),
            pltpu.VMEM((3, 512, 1024), BF),
            pltpu.VMEM((512, 1024), F32),
            pltpu.VMEM((512, 1024), F32),
            pltpu.VMEM((512, 1024), F32),
            pltpu.VMEM((512, 1024), BF),
            pltpu.VMEM((512, 1024), BF),
            pltpu.VMEM((2, 1024), F32),
            pltpu.VMEM((512, 1024), BF),
            pltpu.VMEM((8, 32, 1), F32),
            pltpu.SemaphoreType.DMA((16,)),
            pltpu.SemaphoreType.DMA,
        ] + Reducer.scratch(),
        compiler_params=pltpu.CompilerParams(collective_id=1, has_side_effects=True, vmem_limit_bytes=63 * 2**20),
    )(turn, lse, scales, te, feat, thirds.reshape(3, 2, 1024, 512), w.reshape(1024, 1024), lt, cot, dpre, qkv, mid, back.reshape(512, 1024), x)


def update_kernel(*refs):
    sums, states, rows, outs, rows_out = refs[0], refs[1:17], refs[17:19], refs[19:39], refs[39:41]
    fresh, held, made, passed, in_sem, out_sem, pass_sem = refs[41:]
    mix, cond, up, down = range(4)
    units = [(kind, i) for kind in (down, up, mix) for i in range(4)] + [(cond, 0)]
    keep_one = 1.0 / (1.0 - 0.5**STEP)

    def piece(ref, kind, i):
        if kind == up:
            return ref.at[:, pl.ds(1024 * i, 1024)]
        if kind == cond:
            return ref
        return ref.at[i] if len(ref.shape) == 3 else ref.at[pl.ds(128 * i, 128)]

    def summed(kind, i, buffer):
        if kind == cond:
            return [(sums.at[24, pl.ds(64 * k + 32 * h, 32)], buffer.at[pl.ds(32 * k, 32), pl.ds(512 * h, 512)])
                    for k in range(2) for h in range(2)]
        if kind == up:
            half, first = i // 2, 2 * (i % 2)
            return [(sums.at[8 + 2 * n + half, :, pl.ds(128 * (first + a), 128)], buffer.at[:, pl.ds(512 * a + 128 * n, 128)])
                    for n in range(4) for a in range(2)]
        chunk = 2 * i if kind == down else 16 + 2 * ((i + 1) % 4)
        return [(sums.at[chunk + h], buffer.at[:, pl.ds(512 * h, 512)]) for h in range(2)]

    def loads(u):
        kind, i = units[u]
        s = u % RING
        copies = [(a, b, in_sem.at[s, 8 + n]) for n, (a, b) in enumerate(summed(kind, i, fresh.at[s]))]
        for n, ref in enumerate(states[4 * kind:4 * kind + 4]):
            if kind == cond:
                for k in range(2):
                    copies.append((ref.at[k], held.at[s, n, pl.ds(32 * k, 32)], in_sem.at[s, 4 * k + n]))
            else:
                copies.append((piece(ref, kind, i), held.at[s, n], in_sem.at[s, n]))
        return [pltpu.make_async_copy(*c) for c in copies]

    def saves(u):
        kind, i = units[u]
        s = u % RING
        copies = []
        for n in range(5):
            ref, buffer = outs[5 * kind + n], made.at[s, n]
            if kind == cond:
                for k in range(2):
                    copies.append((buffer.at[pl.ds(32 * k, 32)], ref.at[k], out_sem.at[s, 5 * k + n]))
            else:
                copies.append((buffer, piece(ref, kind, i), out_sem.at[s, n]))
        return [pltpu.make_async_copy(*c) for c in copies]

    enter = [pltpu.make_async_copy(rows[n], passed.at[n], pass_sem.at[n]) for n in range(2)]
    leave = [pltpu.make_async_copy(passed.at[n], rows_out[n].at[0], pass_sem.at[n]) for n in range(2)]
    for u in range(RING - 1):
        for copy in loads(u):
            copy.start()
    for copy in enter:
        copy.start()
    for u in range(len(units)):
        s = u % RING
        if u == 2:
            for n in range(2):
                enter[n].wait()
                leave[n].start()
        if u + RING - 1 < len(units):
            for copy in loads(u + RING - 1):
                copy.start()
        if u >= RING:
            for copy in saves(u - RING):
                copy.wait()
        for copy in loads(u):
            copy.wait()

        def rows_step(b, carry):
            rows = pl.ds(pl.multiple_of(b * 16, 16), 16)
            g = fresh[s, rows].astype(F32)
            w = held[s, 0, rows]
            m = 0.5 * held[s, 1, rows] + 0.5 * g
            v = 0.5 * held[s, 2, rows] + 0.5 * g * g
            w_new = w - 0.01 * (m * keep_one / (jnp.sqrt(v * keep_one) + 1e-08) + 0.1 * w)
            made[s, 0, rows] = g
            made[s, 1, rows] = m
            made[s, 2, rows] = v
            made[s, 3, rows] = w_new
            made[s, 4, rows] = 0.8 * held[s, 3, rows] + 0.2 * w_new
            return carry

        lax.fori_loop(0, 4 if units[u][0] == cond else 8, rows_step, 0)
        for copy in saves(u):
            copy.start()
    for u in range(len(units) - RING, len(units)):
        for copy in saves(u):
            copy.wait()
    for copy in leave:
        copy.wait()


RING = 4


def update(sums, states, rows):
    anyw = pl.BlockSpec(memory_space=pl.ANY)
    outs = []
    for n in range(4):
        outs += [jax.ShapeDtypeStruct(states[4 * n].shape, F32)] * 5
    outs += [jax.ShapeDtypeStruct((1, 512, 1024), BF)] * 2
    *made, output, input_grad = pl.pallas_call(
        update_kernel,
        out_shape=tuple(outs),
        in_specs=[anyw] * 19,
        out_specs=(anyw,) * 22,
        scratch_shapes=[
            pltpu.VMEM((RING, 128, 1024), BF),
            pltpu.VMEM((RING, 4, 128, 1024), F32),
            pltpu.VMEM((RING, 5, 128, 1024), F32),
            pltpu.VMEM((2, 512, 1024), BF),
            pltpu.SemaphoreType.DMA((RING, 16)),
            pltpu.SemaphoreType.DMA((RING, 10)),
            pltpu.SemaphoreType.DMA((2,)),
        ],
        compiler_params=pltpu.CompilerParams(vmem_limit_bytes=63 * 2**20),
    )(sums, *states, *rows)
    return (output, input_grad, *made)


def normed(values):
    center = values - jnp.mean(values, axis=-1, keepdims=True)
    spread = jnp.mean(center * center, axis=-1, keepdims=True)
    return center * lax.rsqrt(spread + 1e-05)


def scaled_norm(values, gain):
    return normed(values) * gain[None, :]


def rotary_tables(segments):
    length = segments.shape[0]
    position = jnp.arange(length, dtype=jnp.int32)
    is_start = jnp.concatenate([jnp.ones((1,), dtype=bool), segments[1:] != segments[:-1]])
    seg_start = lax.cummax(jnp.where(is_start, position, jnp.zeros_like(position)), axis=0)
    offset = (position - seg_start).astype(jnp.float32)
    frequency = 10000.0 ** (-jnp.arange(HEAD_DIM // 2, dtype=jnp.float32) * 2.0 / HEAD_DIM)
    turned = offset[:, None] * frequency[None, :]
    return (jnp.cos(turned)[:, None, :], jnp.sin(turned)[:, None, :])


def rotate(parts, cos_table, sin_table):
    half_dim = parts.shape[-1] // 2
    part_a = parts[..., :half_dim]
    part_b = parts[..., half_dim:]
    return jnp.concatenate(
        [part_a * cos_table - part_b * sin_table, part_b * cos_table + part_a * sin_table], axis=-1
    )


def unrotate(grads, cos_table, sin_table):
    half_dim = grads.shape[-1] // 2
    grad_a = grads[..., :half_dim]
    grad_b = grads[..., half_dim:]
    return jnp.concatenate(
        [grad_a * cos_table + grad_b * sin_table, grad_b * cos_table - grad_a * sin_table], axis=-1
    )


def adam_update(gradient, weight, moment_one, moment_two, average):
    moment_one_new = 0.5 * moment_one + 0.5 * gradient
    moment_two_new = 0.5 * moment_two + 0.5 * gradient * gradient
    correction = 1.0 - 0.5**STEP
    update = (
        moment_one_new / correction / (jnp.sqrt(moment_two_new / correction) + 1e-08) + 0.1 * weight
    )
    weight_new = weight - 0.01 * update
    average_new = 0.8 * average + 0.2 * weight_new
    return (moment_one_new, moment_two_new, weight_new, average_new)


def local(
    tokens,
    time_embed,
    segment_ids,
    cotangent,
    mixing_w,
    mixing_m,
    mixing_v,
    mixing_avg,
    cond_w,
    cond_m,
    cond_v,
    cond_avg,
    up_w,
    up_m,
    up_v,
    up_avg,
    down_w,
    down_m,
    down_v,
    down_avg,
):
    rows_in = tokens[0].astype(jnp.float32)
    embedding = time_embed[0]
    segments = segment_ids[0]
    length = rows_in.shape[0]
    block_rows = min(512, length)
    block_count = length // block_rows
    mixing_g, cond_g = (
        lax.all_gather(mixing_w.astype(jnp.bfloat16), "fsdp", axis=1, tiled=True),
        lax.all_gather(cond_w.astype(jnp.bfloat16), "fsdp", axis=1, tiled=True),
    )
    up_g, down_g = (
        lax.all_gather(up_w.astype(jnp.bfloat16), "fsdp", axis=0, tiled=True),
        lax.all_gather(down_w.astype(jnp.bfloat16), "fsdp", axis=0, tiled=True),
    )
    scales = 1.0 + jnp.einsum("e,ked->kd", embedding, cond_g, preferred_element_type=jnp.float32)
    cos_table, sin_table = rotary_tables(segments)
    normed_one = (normed(rows_in) * scales[0][None, :]).astype(jnp.bfloat16)
    projected = jnp.einsum(
        "td,kde->kte", normed_one, mixing_g[:3], preferred_element_type=jnp.float32
    )
    queries = rotate(projected[0].reshape(length, HEADS, HEAD_DIM), cos_table, sin_table).astype(
        jnp.bfloat16
    )
    keys_rot = rotate(projected[1].reshape(length, HEADS, HEAD_DIM), cos_table, sin_table).astype(
        jnp.bfloat16
    )
    values_b = projected[2].astype(jnp.bfloat16).reshape(length, HEADS, HEAD_DIM)
    query_blocks = queries.reshape(block_count, block_rows, HEADS, HEAD_DIM)
    seg_blocks = segments.reshape(block_count, block_rows)

    def block_scores(q_block, seg_block):
        raw = (
            jnp.einsum("qhd,khd->hqk", q_block, keys_rot, preferred_element_type=jnp.float32)
            * 0.125
        )
        same_seg = seg_block[:, None] == segments[None, :]
        return jnp.where(same_seg[None], raw, -1e30)

    def attend_block(element):
        q_block, seg_block = element
        raw = block_scores(q_block, seg_block)
        peak = jnp.max(raw, axis=-1, keepdims=True)
        exp_scores = jnp.exp(raw - peak)
        totals = jnp.sum(exp_scores, axis=-1, keepdims=True)
        probs = (exp_scores / totals).astype(jnp.bfloat16)
        out_block = jnp.einsum(
            "hqk,khd->qhd", probs, values_b, preferred_element_type=jnp.float32
        ).astype(jnp.bfloat16)
        return (out_block, peak[..., 0] + jnp.log(totals[..., 0]))

    attended, log_totals = lax.map(attend_block, (query_blocks, seg_blocks))
    attended = attended.reshape(length, D)
    middle = rows_in + jnp.dot(attended, mixing_g[3], preferred_element_type=jnp.float32)
    normed_two = (normed(middle) * scales[1][None, :]).astype(jnp.bfloat16)
    hidden_pre = jnp.dot(normed_two, up_g, preferred_element_type=jnp.float32)
    hidden_act = jax.nn.gelu(hidden_pre).astype(jnp.bfloat16)
    output = (middle + jnp.dot(hidden_act, down_g, preferred_element_type=jnp.float32)).astype(
        jnp.bfloat16
    )
    mixing_b, cond_b = (
        lax.all_gather(mixing_w.astype(jnp.bfloat16), "fsdp", axis=1, tiled=True),
        lax.all_gather(cond_w.astype(jnp.bfloat16), "fsdp", axis=1, tiled=True),
    )
    up_b, down_b = (
        lax.all_gather(up_w.astype(jnp.bfloat16), "fsdp", axis=0, tiled=True),
        lax.all_gather(down_w.astype(jnp.bfloat16), "fsdp", axis=0, tiled=True),
    )
    back_out = cotangent[0]
    d_act = jnp.einsum("td,fd->tf", back_out, down_b, preferred_element_type=jnp.float32)
    d_down = jnp.einsum("tf,td->fd", hidden_act, back_out, preferred_element_type=jnp.float32)
    _, gelu_pull = jax.vjp(jax.nn.gelu, hidden_pre)
    d_pre = gelu_pull(d_act)[0].astype(jnp.bfloat16)
    d_up = jnp.einsum("td,tf->df", normed_two, d_pre, preferred_element_type=jnp.float32)
    d_normed_two = jnp.einsum("tf,df->td", d_pre, up_b, preferred_element_type=jnp.float32)
    _, norm_pull_two = jax.vjp(scaled_norm, middle, scales[1])
    d_middle, d_scale_two = norm_pull_two(d_normed_two)
    d_middle = d_middle + back_out.astype(jnp.float32)
    d_middle_b = d_middle.astype(jnp.bfloat16)
    d_out_proj = jnp.einsum("td,te->de", attended, d_middle_b, preferred_element_type=jnp.float32)
    d_attended = jnp.einsum(
        "te,de->td", d_middle_b, mixing_b[3], preferred_element_type=jnp.float32
    ).astype(jnp.bfloat16)
    d_att_blocks = d_attended.reshape(block_count, block_rows, HEADS, HEAD_DIM)

    def back_block(state_in, element):
        q_block, seg_block, d_block, log_block = element
        raw = block_scores(q_block, seg_block)
        probs_f = jnp.exp(raw - log_block[..., None])
        probs_b = probs_f.astype(jnp.bfloat16)
        d_probs = jnp.einsum("qhd,khd->hqk", d_block, values_b, preferred_element_type=jnp.float32)
        d_raw = (probs_f * (d_probs - jnp.sum(probs_f * d_probs, axis=-1, keepdims=True))).astype(
            jnp.bfloat16
        )
        d_query = (
            jnp.einsum("hqk,khd->qhd", d_raw, keys_rot, preferred_element_type=jnp.float32) * 0.125
        )
        keys_acc = (
            state_in[0]
            + jnp.einsum("hqk,qhd->khd", d_raw, q_block, preferred_element_type=jnp.float32) * 0.125
        )
        values_acc = state_in[1] + jnp.einsum(
            "hqk,qhd->khd", probs_b, d_block, preferred_element_type=jnp.float32
        )
        return ((keys_acc, values_acc), d_query)

    zero_heads = jnp.zeros((length, HEADS, HEAD_DIM), jnp.float32)
    (d_keys, d_values), d_queries = lax.scan(
        back_block, (zero_heads, zero_heads), (query_blocks, seg_blocks, d_att_blocks, log_totals)
    )
    d_queries = unrotate(d_queries.reshape(length, HEADS, HEAD_DIM), cos_table, sin_table)
    d_keys = unrotate(d_keys, cos_table, sin_table)
    d_projected = (
        jnp.stack([d_queries, d_keys, d_values]).reshape(3, length, D).astype(jnp.bfloat16)
    )
    d_qkv = jnp.einsum("td,kte->kde", normed_one, d_projected, preferred_element_type=jnp.float32)
    d_normed_one = jnp.einsum(
        "kte,kde->td", d_projected, mixing_b[:3], preferred_element_type=jnp.float32
    )
    _, norm_pull_one = jax.vjp(scaled_norm, rows_in, scales[0])
    d_rows, d_scale_one = norm_pull_one(d_normed_one)
    input_grad = (d_middle + d_rows).astype(jnp.bfloat16)
    d_scales = jnp.stack([d_scale_one, d_scale_two])
    d_cond = embedding.astype(jnp.float32)[None, :, None] * d_scales[:, None, :]
    d_mixing = jnp.concatenate([d_qkv, d_out_proj[None]], axis=0)
    mixing_part, cond_part = (
        lax.psum_scatter(d_mixing, "fsdp", scatter_dimension=1, tiled=True),
        lax.psum_scatter(d_cond, "fsdp", scatter_dimension=1, tiled=True),
    )
    up_part, down_part = (
        lax.psum_scatter(d_up, "fsdp", scatter_dimension=0, tiled=True),
        lax.psum_scatter(d_down, "fsdp", scatter_dimension=0, tiled=True),
    )
    mixing_grad, cond_grad, up_grad, down_grad = (
        lax.psum(mixing_part.astype(jnp.bfloat16), "rows").astype(jnp.float32),
        lax.psum(cond_part.astype(jnp.bfloat16), "rows").astype(jnp.float32),
        lax.psum(up_part.astype(jnp.bfloat16), "rows").astype(jnp.float32),
        lax.psum(down_part.astype(jnp.bfloat16), "rows").astype(jnp.float32),
    )
    mix_one, mix_two, mix_new, mix_average = adam_update(
        mixing_grad, mixing_w, mixing_m, mixing_v, mixing_avg
    )
    cond_one, cond_two, cond_new, cond_average = adam_update(
        cond_grad, cond_w, cond_m, cond_v, cond_avg
    )
    up_one, up_two, up_new, up_average = adam_update(up_grad, up_w, up_m, up_v, up_avg)
    down_one, down_two, down_new, down_average = adam_update(
        down_grad, down_w, down_m, down_v, down_avg
    )
    return (
        output[None],
        input_grad[None],
        mixing_grad,
        mix_one,
        mix_two,
        mix_new,
        mix_average,
        cond_grad,
        cond_one,
        cond_two,
        cond_new,
        cond_average,
        up_grad,
        up_one,
        up_two,
        up_new,
        up_average,
        down_grad,
        down_one,
        down_two,
        down_new,
        down_average,
    )


def local_small(
    tokens, time_embed, segment_ids, cotangent,
    mixing_w, mixing_m, mixing_v, mixing_avg,
    cond_w, cond_m, cond_v, cond_avg,
    up_w, up_m, up_v, up_avg,
    down_w, down_m, down_v, down_avg,
):
    x, cot = tokens[0], cotangent[0]
    lse, scales, turn, feat, thirds, w, lt, dpre, qkv, middle, back, output = forward(
        segment_ids, time_embed, x, cot, mixing_w, cond_w, up_w, down_w)
    sums, input_grad = backward(turn, lse, scales, time_embed, feat, thirds, w, lt, cot, dpre, qkv, middle, back, x)
    states = (
        mixing_w, mixing_m, mixing_v, mixing_avg, cond_w, cond_m, cond_v, cond_avg,
        up_w, up_m, up_v, up_avg, down_w, down_m, down_v, down_avg)
    return update(sums, states, (output, input_grad))


def solution(mesh):
    small = mesh.shape["rows"] == 4 and mesh.shape["fsdp"] == 8
    placed = (
        P(("rows", "fsdp"), None, None),
        P(("rows", "fsdp"), None),
        P(("rows", "fsdp"), None),
        P(("rows", "fsdp"), None, None),
        P(None, "fsdp", None),
        P(None, "fsdp", None),
        P(None, "fsdp", None),
        P(None, "fsdp", None),
        P(None, "fsdp", None),
        P(None, "fsdp", None),
        P(None, "fsdp", None),
        P(None, "fsdp", None),
        P("fsdp", None),
        P("fsdp", None),
        P("fsdp", None),
        P("fsdp", None),
        P("fsdp", None),
        P("fsdp", None),
        P("fsdp", None),
        P("fsdp", None),
    )
    return jax.shard_map(
        local_small if small else local,
        mesh=mesh,
        in_specs=placed,
        out_specs=(
            P(("rows", "fsdp"), None, None),
            P(("rows", "fsdp"), None, None),
            P(None, "fsdp", None),
            P(None, "fsdp", None),
            P(None, "fsdp", None),
            P(None, "fsdp", None),
            P(None, "fsdp", None),
            P(None, "fsdp", None),
            P(None, "fsdp", None),
            P(None, "fsdp", None),
            P(None, "fsdp", None),
            P(None, "fsdp", None),
            P("fsdp", None),
            P("fsdp", None),
            P("fsdp", None),
            P("fsdp", None),
            P("fsdp", None),
            P("fsdp", None),
            P("fsdp", None),
            P("fsdp", None),
            P("fsdp", None),
            P("fsdp", None),
        ),
        check_vma=False,
    )
```

```python
import jax
import jax.numpy as jnp
import numpy as np
from jax import lax
from jax.experimental import pallas as pl
from jax.experimental.pallas import tpu as pltpu
from jax.sharding import PartitionSpec as P

D = 1024
HEADS = 16
HEAD_DIM = 64
STEP = 7
F32 = jnp.float32
BF = jnp.bfloat16


MESH = pl.DeviceIdType.MESH
CHUNKS = 25
SLOTS = 4
SIB_SLOTS = 6
LINE_SLOTS = 6
PART_SLOTS = 10
LAGS = (1, 3, 5, 7, 9, 11, 13)


class Reducer:
    def __init__(self, refs):
        (self.away, self.part, self.sib, self.swap, self.diag, self.near, self.zin, self.zmid, self.tsum, self.out_a, self.out_b,
         self.sems_sib, self.sems_swap, self.sems_diag, self.sems_near, self.sems_zin, self.sems_zmid) = refs
        self.me = lax.axis_index("fsdp")
        self.core = lax.rem(self.me, 2)
        self.chip = lax.div(self.me, 2)
        self.row = lax.axis_index("rows")
        self.inner = jnp.logical_and(self.row >= 1, self.row <= 2)
        self.outer = jnp.logical_not(self.inner)
        self.line_to = jnp.where(self.row == 0, 1, jnp.where(self.row == 1, 0, jnp.where(self.row == 2, 3, 2)))
        self.mid_to = jnp.where(self.row == 1, 2, 1)
        xbit = lax.rem(self.chip, 2)
        ybit = lax.div(self.chip, 2)
        self.chip_x = ybit * 2 + (1 - xbit)
        self.chip_y = (1 - ybit) * 2 + xbit
        self.chip_d = (1 - ybit) * 2 + (1 - xbit)
        self.mine = pl.multiple_of(lax.rem(self.row, 2) * 64, 64)
        self.to_sib = {"fsdp": self.chip * 2 + (1 - self.core)}
        self.to_x = {"fsdp": self.chip_x * 2 + self.core}
        self.to_y = {"fsdp": self.chip_y * 2 + self.core}

    @staticmethod
    def scratch():
        s = SLOTS
        bf = jnp.bfloat16
        dma = pltpu.SemaphoreType.DMA
        return [
            pltpu.VMEM((SLOTS, 4, 128, 512), bf),
            pltpu.VMEM((PART_SLOTS, 4, 128, 512), bf),
            pltpu.VMEM((SIB_SLOTS, 4, 128, 512), bf),
            pltpu.VMEM((LINE_SLOTS, 64, 512), bf),
            pltpu.VMEM((s, 128, 512), bf),
            pltpu.VMEM((s, 2, 128, 512), bf),
            pltpu.VMEM((LINE_SLOTS, 128, 512), bf),
            pltpu.VMEM((LINE_SLOTS, 128, 512), bf),
            pltpu.VMEM((LINE_SLOTS, 128, 512), jnp.float32),
            pltpu.VMEM((LINE_SLOTS, 128, 512), bf),
            pltpu.VMEM((LINE_SLOTS, 128, 512), bf),
            dma((2, SIB_SLOTS)),
            dma((2, LINE_SLOTS)),
            dma((2, s)),
            dma((2, s)),
            dma((2, LINE_SLOTS)),
            dma((2, LINE_SLOTS)),
        ]

    def enter(self):
        barrier = pltpu.get_barrier_semaphore()
        for to in (self.to_sib, self.to_x, self.to_y, {"rows": self.line_to}):
            pl.semaphore_signal(barrier, inc=1, device_id=to, device_id_type=MESH)

        @pl.when(self.inner)
        def _():
            pl.semaphore_signal(barrier, inc=1, device_id={"rows": self.mid_to}, device_id_type=MESH)
            pl.semaphore_wait(barrier, 5)

        @pl.when(self.outer)
        def _():
            pl.semaphore_wait(barrier, 4)

    def copy(self, src, dst, sems, which, slot, to):
        return pltpu.make_async_remote_copy(
            src_ref=src, dst_ref=dst, send_sem=sems.at[which, slot], recv_sem=sems.at[which + sems.shape[0] // 2, slot],
            device_id=to, device_id_type=MESH)

    def c_sib(self, g):
        n = lax.rem(g, SIB_SLOTS)
        return self.copy(self.away.at[lax.rem(g, SLOTS)], self.sib.at[n], self.sems_sib, 0, n, self.to_sib)

    def shared(self, g):
        return jnp.logical_and(lax.rem(g, 3) != 2, g < CHUNKS - 4)

    def by_kind(self, g, stage):
        pl.when(self.shared(g))(lambda: stage(g, self.mine, 32))
        pl.when(jnp.logical_not(self.shared(g)))(lambda: stage(g, 0, 64))

    def c_swap(self, g):
        s = lax.rem(g, LINE_SLOTS)
        theirs = pl.ds(pl.multiple_of(64 - self.mine, 64), 64)
        return self.copy(self.part.at[lax.rem(g, PART_SLOTS), self.chip_d, theirs], self.swap.at[s], self.sems_swap, 0, s, {"rows": self.line_to})

    def c_diag(self, g, k, first, size):
        s, to, rows = lax.rem(g, SLOTS), (self.to_x if k == 0 else self.to_y), pl.ds(first + size * k, size)
        return self.copy(self.part.at[lax.rem(g, PART_SLOTS), self.chip_d, rows], self.diag.at[s, rows], self.sems_diag, 0, s, to)

    def c_near(self, g, k):
        s, (to, chip) = lax.rem(g, SLOTS), ((self.to_x, self.chip_x) if k == 0 else (self.to_y, self.chip_y))
        return self.copy(self.part.at[lax.rem(g, PART_SLOTS), chip], self.near.at[s, k], self.sems_near, 0, s, to)

    def both_diag(self, g, first, size):
        s, rows = lax.rem(g, SLOTS), pl.ds(first, 2 * size)
        return self.copy(self.part.at[lax.rem(g, PART_SLOTS), self.chip_d, rows], self.diag.at[s, rows], self.sems_diag, 0, s, self.to_x)

    def both_near(self, g):
        s = lax.rem(g, SLOTS)
        return self.copy(self.part.at[lax.rem(g, PART_SLOTS), pl.ds(0, 2)], self.near.at[s], self.sems_near, 0, s, self.to_x)

    def c_line(self, s):
        return self.copy(self.out_a.at[s], self.zin.at[s], self.sems_zin, 0, s, {"rows": self.line_to})

    def c_mid(self, s):
        return self.copy(self.out_b.at[s], self.zmid.at[s], self.sems_zmid, 0, s, {"rows": self.mid_to})

    def stage_b(self, g):
        p, n = lax.rem(g, PART_SLOTS), lax.rem(g, SIB_SLOTS)
        self.c_sib(g).wait()
        self.part[p] = (self.part[p].astype(jnp.float32) + self.sib[n].astype(jnp.float32)).astype(jnp.bfloat16)
        pl.when(self.shared(g))(lambda: self.c_swap(g).start())

    def add(self, g, chip, first, size, more):
        p, rows = lax.rem(g, PART_SLOTS), pl.ds(first, size)
        total = self.part[p, chip, rows].astype(jnp.float32) + more.astype(jnp.float32)
        self.part[p, chip, rows] = total.astype(jnp.bfloat16)

    def stage_d(self, g, first, size):
        if size == 32:
            self.c_swap(g).wait()
            self.add(g, self.chip_d, first, 64, self.swap[lax.rem(g, LINE_SLOTS)])
        self.c_diag(g, 0, first, size).start()
        self.c_diag(g, 1, first, size).start()

    def stage_c(self, g, first, size):
        s = lax.rem(g, SLOTS)
        self.both_diag(g, first, size).wait()
        self.add(g, self.chip_y, first, size, self.diag[s, pl.ds(first, size)])
        self.c_near(g, 1).start()
        self.add(g, self.chip_x, first + size, size, self.diag[s, pl.ds(first + size, size)])
        self.c_near(g, 0).start()

    def stage_e(self, g):
        s, p = lax.rem(g, SLOTS), lax.rem(g, PART_SLOTS)
        self.both_near(g).wait()
        total = (self.part[p, self.chip].astype(jnp.float32) + self.near[s, 0].astype(jnp.float32)) + self.near[s, 1].astype(jnp.float32)
        n = lax.rem(g, LINE_SLOTS)
        self.tsum[n] = total

        @pl.when(self.outer)
        def _():
            self.out_a[n] = total.astype(jnp.bfloat16)
            self.c_line(n).start()

    def stage_f(self, g):
        s = lax.rem(g, LINE_SLOTS)

        @pl.when(self.inner)
        def _():
            self.c_line(s).wait_recv()
            self.out_b[s] = (self.tsum[s] + self.zin[s].astype(jnp.float32)).astype(jnp.bfloat16)
            self.c_mid(s).start()

    def stage_h(self, g, put):
        s = lax.rem(g, LINE_SLOTS)

        @pl.when(self.inner)
        def _():
            self.c_mid(s).wait()
            total = (self.out_b[s].astype(jnp.float32) + self.zmid[s].astype(jnp.float32)).astype(jnp.bfloat16)
            self.out_a[s] = total
            self.c_line(s).start()
            put(g, total)

    def stage_i(self, g, put):
        s = lax.rem(g, LINE_SLOTS)

        @pl.when(self.outer)
        def _():
            self.c_line(s).wait()
            put(g, self.zin[s])

        @pl.when(self.inner)
        def _():
            self.c_line(s).wait_send()

    def tick(self, t, put):
        b, d, c, e, f, h, i = LAGS

        def run(lag, stage, *args):
            g = t - lag
            pl.when(jnp.logical_and(g >= 0, g < CHUNKS))(lambda: stage(g, *args))

        run(i, self.stage_i, put)
        run(h, self.stage_h, put)
        run(f, self.stage_f)
        run(e, self.stage_e)
        run(c, lambda g: self.by_kind(g, self.stage_c))
        run(d, lambda g: self.by_kind(g, self.stage_d))
        run(b, self.stage_b)


def dot(a, b):
    return lax.dot_general(a, b, (((1,), (0,)), ((), ())), preferred_element_type=F32)


def dot_nt(a, b):
    return lax.dot_general(a, b, (((1,), (1,)), ((), ())), preferred_element_type=F32)


START, LINK, SIBLING, HOP, ISSUE, LEAD = 6.0, 50.0, 300.0, 2.0, 0.05, 4.0
PIECES = [(-1, 0, 1024, True)]
PIECES += [(k, 512 * h, 512, k == 2 and h == 0) for h in range(2) for k in range(3)]
PIECES += [(-2, 0, 1024, True), (3, 0, 1024, False)]
PIECES += [(4 + n, 0, 1024, n in (1, 4, 6, 7)) for n in range(8)]
COND_TWO, OUT_W, UP_W, DOWN_W = 7, 8, 9, 13


SHARED = {4: 3, 5: 0, 6: 0, 7: 0, 9: 8, 10: 8}


class Gatherer:
    def __init__(self, refs):
        self.cond, self.thirds, self.mats, self.send, self.recv = refs
        self.me = lax.axis_index("fsdp")
        core = lax.rem(self.me, 2)
        chip = lax.div(self.me, 2)
        xbit, ybit = lax.rem(chip, 2), lax.div(chip, 2)
        self.x = (ybit * 2 + 1 - xbit) * 2 + core
        self.y = ((1 - ybit) * 2 + xbit) * 2 + core
        self.d = ((1 - ybit) * 2 + 1 - xbit) * 2 + core
        self.sib = chip * 2 + 1 - core
        row = lax.axis_index("rows")
        self.half = lax.rem(row, 2)
        self.to_z = {"rows": row + 1 - 2 * self.half}
        self.time = START
        self.free = {"x": 0.0, "y": 0.0, "z": 0.0, "s": 0.0}
        self.due = {}
        self.waiting = []
        self.begun, self.whole = 0, set()

    @staticmethod
    def scratch():
        return [
            pltpu.VMEM((8, 64, 1024), BF),
            pltpu.VMEM((3, 2, 8, 128, 512), BF),
            pltpu.VMEM((9, 8, 128, 1024), BF),
            pltpu.SemaphoreType.DMA((len(PIECES), 11)),
            pltpu.SemaphoreType.DMA((len(PIECES), 11)),
        ]

    def enter(self):
        barrier = pltpu.get_barrier_semaphore()
        for to in ({"fsdp": self.sib}, {"fsdp": self.x}, {"fsdp": self.y}, self.to_z):
            pl.semaphore_signal(barrier, inc=1, device_id=to, device_id_type=MESH)
        pl.semaphore_wait(barrier, 4)

    @staticmethod
    def direct(c):
        return PIECES[c][3]

    def shard(self, c, owner, start=0, size=None):
        mat, col, cols, _ = PIECES[c]
        if mat < 0:
            base = 32 * (-1 - mat)
            return self.cond.at[owner, pl.ds(base + start, 32 if size is None else size)]
        rows = pl.ds(start, 128 if size is None else size)
        return self.thirds.at[mat, col // 512, owner, rows] if mat < 3 else self.mats.at[mat - 3, owner, rows]

    def copy(self, c, kind, owner, to, start=0, size=None):
        ref = self.shard(c, owner, start, size)
        return pltpu.make_async_remote_copy(
            src_ref=ref, dst_ref=ref, send_sem=self.send.at[c, kind], recv_sem=self.recv.at[c, SHARED.get(kind, kind)],
            device_id=to, device_id_type=MESH)

    def landed(self, c, kind, rows):
        mat, _, cols, _ = PIECES[c]
        if mat < 0:
            ref = self.cond.at[pl.ds(0, 4), pl.ds(0, 32)] if rows == 128 else self.cond.at[0, pl.ds(0, rows)]
        else:
            base = self.thirds.at[mat, 0] if mat < 3 else self.mats.at[mat - 3]
            ref = base.at[pl.ds(0, rows // 128)] if rows >= 128 else base.at[0, pl.ds(0, rows)]
            if rows == 192:
                ref = base.at[pl.ds(0, 3), pl.ds(0, 64)]
        pltpu.make_async_remote_copy(
            src_ref=ref, dst_ref=ref, send_sem=self.send.at[c, kind], recv_sem=self.recv.at[c, kind],
            device_id={"fsdp": self.sib}, device_id_type=MESH).wait_recv()

    def span(self, c, k=None):
        rows = 32 if PIECES[c][0] < 0 else 128
        if self.direct(c):
            return (0, None) if k is None else (k * (rows // 2), rows // 2)
        return (self.half * 64, 64) if k is None else (self.half * 64 + 32 * k, 32)

    def post(self, link, mark, copy):
        copy.start()
        rows, cols = copy.src_ref.shape[-2:]
        self.time += ISSUE
        self.free[link] = max(self.free[link], self.time) + rows * cols * 2e-3 / (SIBLING if link == "s" else LINK)
        self.due[mark] = self.free[link] + HOP

    def take(self, mark, copy):
        copy.wait_recv()
        self.time = max(self.time, self.due[mark]) + ISSUE

    def take_all(self, c, kinds, rows):
        self.landed(c, kinds[0], rows)
        self.time = max([self.time] + [self.due[c, kind] for kind in kinds]) + ISSUE

    def onward(self, c, kind, owner):
        if self.direct(c):
            self.post("s", (c, 5 + kind), self.copy(c, 5 + kind, owner, {"fsdp": self.sib}))
        else:
            self.post("z", (c, 8 + kind), self.copy(c, 8 + kind, owner, self.to_z, *self.span(c)))

    def s1(self, c):
        self.post("x", (c, 1), self.copy(c, 1, self.me, {"fsdp": self.x}, *self.span(c)))
        self.post("y", (c, 2), self.copy(c, 2, self.me, {"fsdp": self.y}, *self.span(c)))
        self.post("s", (c, 0), self.copy(c, 0, self.me, {"fsdp": self.sib}))
        self.begun = c + 1
        self.waiting.append((2, c))

    def s2(self, c):
        self.take((c, 1), self.copy(c, 1, self.x, {"fsdp": self.x}, *self.span(c)))
        self.post("y", (c, 3), self.copy(c, 3, self.x, {"fsdp": self.y}, *self.span(c, 0)))
        self.onward(c, 0, self.x)
        self.take((c, 2), self.copy(c, 2, self.y, {"fsdp": self.y}, *self.span(c)))
        self.post("x", (c, 4), self.copy(c, 4, self.y, {"fsdp": self.x}, *self.span(c, 1)))
        self.onward(c, 1, self.y)
        self.waiting.append((3, c))

    def s3(self, c):
        self.take_all(c, (3, 4), self.moved(c))
        self.onward(c, 2, self.d)
        self.waiting.append((5 if self.direct(c) else 4, c))

    def s4(self, c):
        self.take_all(c, (8, 9, 10), 192)
        for kind, owner in enumerate((self.x, self.y, self.d)):
            self.post("s", (c, 5 + kind), self.copy(c, 5 + kind, owner, {"fsdp": self.sib}))
        self.waiting.append((5, c))

    def moved(self, c):
        rows = 32 if PIECES[c][0] < 0 else 128
        return rows if self.direct(c) else rows // 2

    def s5(self, c):
        self.take_all(c, (0, 5, 6, 7), 128 if PIECES[c][0] < 0 else 512)
        self.whole.add(c)

    def ready(self, event):
        stage, c = event
        marks = {2: (1, 2), 3: (3, 4), 4: (8, 9, 10), 5: (0, 5, 6, 7)}[stage]
        return max(self.due[c, kind] for kind in marks)

    def feed(self):
        while self.begun < len(PIECES) and min(self.free["x"], self.free["y"]) - self.time < LEAD:
            self.s1(self.begun)

    def step(self, event):
        self.waiting.remove(event)
        stage, c = event
        (self.s2, self.s3, self.s4, self.s5)[stage - 2](c)

    def spend(self, time):
        self.time += time
        while True:
            self.feed()
            landed = [event for event in self.waiting if self.ready(event) <= self.time]
            if not landed:
                break
            self.step(min(landed, key=lambda event: (self.ready(event), event)))

    def need(self, c):
        while c not in self.whole:
            self.feed()
            self.step(min(self.waiting, key=lambda event: (self.ready(event), event)))

    def finish(self):
        for c in range(len(PIECES)):
            self.copy(c, 0, self.me, {"fsdp": self.sib}).wait_send()
            for kind in (1, 2):
                self.copy(c, kind, self.me, {"fsdp": self.x}, *self.span(c)).wait_send()
            for k in range(2):
                self.copy(c, 3 + k, self.x, {"fsdp": self.x}, *self.span(c, k)).wait_send()
            for kind in range(3):
                self.copy(c, 5 + kind, self.x, {"fsdp": self.sib}).wait_send()
                if not self.direct(c):
                    self.copy(c, 8 + kind, self.x, self.to_z, *self.span(c)).wait_send()


def forward_kernel(
    seg_in, freq_in, te_in, x_in, cot_hbm, mixing_hbm, cond_hbm, up_hbm, down_hbm,
    lse_out, scales_out, turn_out, feat_out, thirds_hbm, w_hbm, lt_hbm, dpre_hbm, qkv_hbm, mid_hbm, back_hbm, out_hbm,
    four, wide, condf, nrm, qkv, att, mid, te_at, act, cot, ltb, gbuf, eye, in_sem, w_sem, lt_sem, g_sem, o_sem, *shared,
):
    gat = Gatherer(shared)
    me = gat.me
    thirds, mats = gat.thirds, gat.mats

    def load(src, dst, n):
        return pltpu.make_async_copy(src, dst, in_sem.at[n])

    loads = [load(cond_hbm, condf, 0)]
    loads += [load(mixing_hbm.at[k], four.at[k], 1 + k) for k in range(4)]
    loads += [load(up_hbm, wide, 5), load(cot_hbm, cot, 6)]
    for copy in loads:
        copy.start()
    gat.enter()
    obuf = att
    loads[0].wait()
    for k in range(2):
        gat.cond[me, 32 * k:32 * k + 32] = condf[k].astype(BF)
    gat.s1(0)
    for k in range(4):
        loads[1 + k].wait()
        if k < 3:
            for h in range(2):
                thirds[k, h, me] = four[k, :, 512 * h:512 * h + 512].astype(BF)
            if k < 2:
                gat.s1(1 + k)
        else:
            mats[0, me] = four[k].astype(BF)
    later = [load(down_hbm.at[pl.ds(128 * i, 128)], four.at[i], 7 + i) for i in range(4)]
    for copy in later:
        copy.start()
    ids = seg_in[...].astype(F32)
    column = jnp.broadcast_to(ids, (128, 512)).T[:, :1]
    before = jnp.sum(jnp.where(ids < column, 1.0, 0.0), axis=1, keepdims=True)
    offset = lax.broadcasted_iota(jnp.int32, (512, 1), 0).astype(F32) - before
    angle = offset * freq_in[...]
    lanes = lax.broadcasted_iota(jnp.int32, (1, 128), 1)
    lane_in = lax.rem(lanes, 64)
    low_half = lane_in < 32
    turn_out[0] = jnp.cos(angle)
    turn_out[1] = jnp.where(low_half, -1.0, 1.0) * jnp.sin(angle)
    spot = lane_in.astype(F32)
    square = (lax.broadcasted_iota(jnp.int32, (256, 256), n) for n in range(2))
    eye[...] = jnp.where(next(square) == next(square), 1.0, 0.0).astype(BF)
    feat_out[0] = jnp.where(jnp.logical_and(lane_in < 4, spot != column), 1.0, 0.0).astype(BF)
    feat_out[1] = jnp.where(spot == column, -1e30, 0.0).astype(BF)
    te_column = jnp.broadcast_to(te_in[...].astype(F32), (128, 256)).T[:, :1]
    for f in range(8):
        te_at[f] = te_column[32 * f:32 * f + 32]
    loads[5].wait()
    for i in range(4):
        for f in range(8):
            mats[1 + i, me, :, 128 * f:128 * f + 128] = wide[:, 512 * f + 128 * i:512 * f + 128 * i + 128].astype(BF)
    for i in range(4):
        later[i].wait()
        mats[5 + i, me] = four[i].astype(BF)

    def save_w(m):
        if m < 3:
            return pltpu.make_async_copy(thirds.at[m], thirds_hbm.at[m], w_sem.at[m])
        return pltpu.make_async_copy(mats.at[0], w_hbm, w_sem.at[m])

    def save_lt(n, slot):
        return pltpu.make_async_copy(ltb.at[slot], lt_hbm.at[n], lt_sem.at[slot])

    def turn(block, b, slot):
        rows = slice(128 * b, 128 * b + 128) if isinstance(b, int) else pl.ds(pl.multiple_of(b * 128, 128), 128)
        turned = dot_nt(eye[...], block).astype(BF)
        for a in range(2):
            ltb[slot, a, rows] = turned[128 * a:128 * a + 128]

    def scale_of(k):
        total = jnp.zeros((32, 1024), F32)
        for f in range(8):
            total = total + te_at[f] * gat.cond[f, 32 * k:32 * k + 32].astype(F32)
        scales_out[k:k + 1] = 1.0 + jnp.sum(total, axis=0, keepdims=True)

    def norm_rows(source, scale):
        def block(b, carry):
            rows = pl.ds(pl.multiple_of(b * 64, 64), 64)
            values = source[rows].astype(F32)
            center = values - jnp.mean(values, axis=-1, keepdims=True)
            spread = jnp.mean(center * center, axis=-1, keepdims=True)
            nrm[rows] = (center * lax.rsqrt(spread + 1e-05) * scale).astype(BF)
            return carry

        lax.fori_loop(0, 8, block, 0, unroll=2)

    gat.need(0)
    scale_of(0)
    norm_rows(x_in, scales_out[0:1])
    gat.spend(1.2)

    def save_qkv(k):
        return pltpu.make_async_copy(qkv.at[k], qkv_hbm.at[k], o_sem.at[k])

    def project(k, half):
        at = slice(512 * half, 512 * half + 512)
        result = dot(nrm[...], thirds[k, half].reshape(1024, 512))
        if k == 0:
            for b in range(2):
                turn(nrm[:, 512 * half + 256 * b:512 * half + 256 * b + 256], 2 * half + b, 0)
        if k < 2:
            sides = []
            for n in range(4):
                part = result[:, 128 * n:128 * n + 128]
                other = jnp.where(low_half, pltpu.roll(part, 96, 1), pltpu.roll(part, 32, 1))
                sides.append(part * turn_out[0] + other * turn_out[1])
            result = jnp.concatenate(sides, axis=1)
        result = result.astype(BF)
        qkv[k, :, at] = result * jnp.asarray(0.125, BF) if k == 0 else result

    def attend(pair, carry):
        at = pl.ds(pl.multiple_of(pair * 128, 128), 128)
        q_pair, k_pair = qkv[0, :, at], qkv[1, :, at]
        v_turned = qkv[2, :, at].T
        heads = [lax.div(lanes, 64) == j for j in range(2)]
        raws = [dot_nt(jnp.where(mine, k_pair, feat_out[1]), jnp.where(mine, q_pair, feat_out[0])) for mine in heads]
        peaks = [jnp.max(raw, axis=0, keepdims=True) for raw in raws]
        grown = [jnp.exp(raw - peak) for raw, peak in zip(raws, peaks)]
        totals = [jnp.sum(value, axis=0, keepdims=True) for value in grown]
        sides = [dot(v_turned[64 * j:64 * j + 64], grown[j].astype(BF)) * (1.0 / totals[j]) for j in range(2)]
        sums = [peak + jnp.log(total) for peak, total in zip(peaks, totals)]
        lse_out[pair] = jnp.concatenate(sums, axis=0)
        block = jnp.concatenate(sides, axis=0).astype(BF)
        ltb[1, lax.rem(pair, 2), pl.ds(pl.multiple_of(lax.div(pair, 2) * 128, 128), 128)] = block
        att[:, at] = block.T
        return carry

    for half in range(2):
        for k in range(3):
            gat.need(1 + 3 * half + k)
            project(k, half)
            gat.spend(0.9)
        if half == 1:
            for k in range(3):
                save_w(k).start()
                save_qkv(k).start()
            save_lt(6, 0).start()
        for part in range(2):
            begin = 4 * half + 2 * part
            lax.fori_loop(begin, begin + 2, attend, 0)
            gat.spend(3.6)
    save_lt(5, 1).start()
    gat.need(COND_TWO)
    scale_of(1)
    gat.need(OUT_W)
    save_w(3).start()

    def join(b, carry):
        at = pl.ds(pl.multiple_of(b * 512, 512), 512)
        mid[:, at] = x_in[:, at].astype(F32) + dot(att[...], mats[0, :, :, at].reshape(1024, 512))
        return carry

    lax.fori_loop(0, 2, join, 0)
    gat.spend(1.8)
    save_mid = pltpu.make_async_copy(mid, mid_hbm, o_sem.at[3])
    save_mid.start()
    norm_rows(mid, scales_out[1:2])
    gat.spend(2.4)
    befores = {0: 6, 1: 5, 2: 4}

    def save_dpre(i):
        return pltpu.make_async_copy(gbuf.at[i], dpre_hbm.at[i], g_sem.at[i])

    for i in range(4):
        gat.need(UP_W + i)
        save_lt(befores[i % 3], i % 3).wait()

        def expand(b, carry):
            at = pl.ds(pl.multiple_of(b * 512, 512), 512)
            u = dot(nrm[...], mats[1 + i, :, :, at].reshape(1024, 512))
            root = 0.7978845608028654
            square = u * u
            bend = jnp.tanh(root * u * (1.0 + 0.044715 * square))
            side = 0.5 * (1.0 + bend)
            result = (u * side).astype(BF)
            act[i, :, at] = result
            for n in range(2):
                turn(result[:, 256 * n:256 * n + 256], 2 * b + n, i % 3)
                if i == 0:
                    turn(nrm[:, pl.ds(pl.multiple_of(b * 512 + n * 256, 256), 256)], 2 * b + n, 2)
            slope = side + 0.5 * u * (1.0 - bend * bend) * (root * (1.0 + 3.0 * 0.044715 * square))
            gbuf[i, :, at] = slope.astype(BF)
            return carry

        lax.fori_loop(0, 2, expand, 0)
        save_lt(i, i % 3).start()
        befores[i % 3] = i
        if i == 0:
            save_lt(4, 2).start()
        gat.spend(3.0)
    for i in range(4):
        gat.need(DOWN_W + i)
        if i == 0:
            loads[6].wait()

        def slopes(b, carry):
            at = pl.ds(pl.multiple_of(b * 512, 512), 512)
            d_act = dot_nt(cot[...], mats[5 + i, pl.ds(4 * b, 4)].reshape(512, 1024))
            gbuf[i, :, at] = (d_act * gbuf[i, :, at].astype(F32)).astype(BF)
            return carry

        lax.fori_loop(0, 2, slopes, 0)
        save_dpre(i).start()
        gat.spend(1.2)

    def shrink(b, carry):
        at = pl.ds(pl.multiple_of(b * 512, 512), 512)
        total = mid[:, at]
        for i in range(4):
            total = total + dot(act[i], mats[5 + i, :, :, at].reshape(1024, 512))
        obuf[:, at] = total.astype(BF)
        back = dot_nt(gbuf[0], mats[1, pl.ds(4 * b, 4)].reshape(512, 1024))
        for i in range(1, 4):
            back = back + dot_nt(gbuf[i], mats[1 + i, pl.ds(4 * b, 4)].reshape(512, 1024))
        four[:, :, at] = back.reshape(4, 128, 512)
        return carry

    lax.fori_loop(0, 2, shrink, 0)
    save_out = pltpu.make_async_copy(obuf, out_hbm, o_sem.at[4])
    save_out.start()
    save_back = pltpu.make_async_copy(four, back_hbm, o_sem.at[5])
    save_back.start()
    gat.finish()
    for m in range(4):
        save_w(m).wait()
    for k in range(3):
        save_qkv(k).wait()
        save_lt(befores[k], k).wait()
    save_mid.wait()
    for i in range(4):
        save_dpre(i).wait()
    save_out.wait()
    save_back.wait()


def forward(seg, te, x, cot, mixing_w, cond_w, up_w, down_w):
    vmem = pl.BlockSpec(memory_space=pltpu.VMEM)
    anyw = pl.BlockSpec(memory_space=pl.ANY)
    shape = jax.ShapeDtypeStruct
    freq = 10000.0 ** (-(np.arange(128) % 32) * 2.0 / HEAD_DIM)
    return pl.pallas_call(
        forward_kernel,
        out_shape=(
            shape((8, 2, 512), F32), shape((2, 1024), F32), shape((2, 512, 128), F32), shape((2, 512, 128), BF),
            shape((3, 2, 8, 128, 512), BF), shape((8, 128, 1024), BF), shape((7, 2, 512, 512), BF), shape((4, 512, 1024), BF),
            shape((3, 512, 1024), BF), shape((512, 1024), F32), shape((4, 128, 1024), F32), shape((512, 1024), BF)),
        in_specs=[vmem] * 4 + [anyw] * 5,
        out_specs=(vmem,) * 4 + (anyw,) * 8,
        scratch_shapes=[
            pltpu.VMEM((4, 128, 1024), F32),
            pltpu.VMEM((128, 4096), F32),
            pltpu.VMEM((2, 32, 1024), F32),
            pltpu.VMEM((512, 1024), BF),
            pltpu.VMEM((3, 512, 1024), BF),
            pltpu.VMEM((512, 1024), BF),
            pltpu.VMEM((512, 1024), F32),
            pltpu.VMEM((8, 32, 1), F32),
            pltpu.VMEM((4, 512, 1024), BF),
            pltpu.VMEM((512, 1024), BF),
            pltpu.VMEM((3, 2, 512, 512), BF),
            pltpu.VMEM((4, 512, 1024), BF),
            pltpu.VMEM((256, 256), BF),
            pltpu.SemaphoreType.DMA((11,)),
            pltpu.SemaphoreType.DMA((4,)),
            pltpu.SemaphoreType.DMA((3,)),
            pltpu.SemaphoreType.DMA((4,)),
            pltpu.SemaphoreType.DMA((6,)),
        ] + Gatherer.scratch(),
        compiler_params=pltpu.CompilerParams(collective_id=2, has_side_effects=True, vmem_limit_bytes=63 * 2**20),
    )(seg, jnp.asarray(freq[None], F32), te, x, cot, mixing_w, cond_w, up_w, down_w)


def norm_back(values, grads, scale):
    center = values - jnp.mean(values, axis=-1, keepdims=True)
    recip = lax.rsqrt(jnp.mean(center * center, axis=-1, keepdims=True) + 1e-05)
    unit = center * recip
    g = grads * scale
    back = recip * (g - jnp.mean(g, axis=-1, keepdims=True) - unit * jnp.mean(g * unit, axis=-1, keepdims=True))
    return back, grads * unit


def backward_kernel(
    turn_in, lse_in, scales_in, te_in, feat_in, thirds_hbm, w_hbm, lt_hbm, cot_hbm, dpre_hbm, qkv_hbm, mid_hbm, back_hbm, x_hbm,
    sums, in_grad,
    lt, rh, thirds, wout, qkv, mid, acc, dmid, datt, xin, dscale, obuf, te_at, load_sem, out_sem, *shared,
):
    red = Reducer(shared)
    core = red.core

    def load(src, dst, n):
        return pltpu.make_async_copy(src, dst, load_sem.at[n])

    load_lt = [load(lt_hbm.at[n], lt.at[n], n) for n in range(7)]
    load_cot = load(cot_hbm, rh.at[0], 7)
    load_mid = load(mid_hbm, mid, 8)
    load_back = load(back_hbm, acc, 9)
    load_w3 = load(w_hbm, wout, 10)
    load_qkv = load(qkv_hbm, qkv, 11)
    load_dpre = load(dpre_hbm, rh.at[pl.ds(1, 4)], 12)
    load_w = load(thirds_hbm, thirds, 13)
    load_x = load(x_hbm, xin, 14)
    for copy in (load_cot, load_lt[0], load_mid, load_back, load_w3):
        copy.start()
    later = (load_lt[1], load_qkv, load_lt[2], load_lt[3], load_lt[4], load_dpre, load_lt[5], load_w, load_lt[6], load_x)
    arrivals = {1: (load_lt[1], load_qkv), 2: (load_lt[2],), 3: (load_lt[3],), 4: (load_lt[4], load_dpre), 8: (load_lt[5],),
                9: (load_lt[6], load_w, load_x)}
    red.enter()

    def operands(g):
        left = jnp.where(g < 8, lax.div(g, 2), jnp.where(g < 16, 4, jnp.where(g < 18, 5, 6)))
        right = jnp.where(g < 8, 0, jnp.where(g < 16, 1 + lax.div(g - 8, 2), jnp.where(g < 18, 5, 6 + lax.div(g - 18, 2))))
        return left, rh[right, :, pl.ds(pl.multiple_of(lax.rem(g, 2) * 512, 512), 512)]

    def give(g):
        left, right = operands(g)
        red.away[lax.rem(g, SLOTS)] = dot(lt[left, 1 - core], right).astype(BF).reshape(4, 128, 512)
        red.part[lax.rem(g, PART_SLOTS)] = dot(lt[left, core], right).astype(BF).reshape(4, 128, 512)
        red.c_sib(g).start()

    def cond_part(parity):
        rows = []
        for chip in range(4):
            column = te_at[2 * chip + parity]
            rows.append(jnp.concatenate([column * dscale[k:k + 1, 512 * h:512 * h + 512] for k in range(2) for h in range(2)], axis=0)[None])
        return jnp.concatenate(rows, axis=0)

    def put(g, value):
        sums[g] = value

    te_column = jnp.broadcast_to(te_in[...].astype(F32), (128, 256)).T[:, :1]
    for f in range(8):
        te_at[f] = te_column[32 * f:32 * f + 32]
    lanes = lax.broadcasted_iota(jnp.int32, (1, 128), 1)
    low_half = lax.rem(lanes, 64) < 32

    def unrotate(block):
        other = jnp.where(low_half, pltpu.roll(block, 96, 1), pltpu.roll(block, 32, 1))
        return block * turn_in[0] - other * turn_in[1]

    def middle_back():
        for copy in later:
            copy.start()
        load_mid.wait()
        load_back.wait()

        def norm_two(b, total):
            rows = pl.ds(pl.multiple_of(b * 64, 64), 64)
            back, terms = norm_back(mid[rows], acc[rows], scales_in[1:2])
            back = back + rh[0, rows].astype(F32)
            dmid[rows] = back
            rh[5, rows] = back.astype(BF)
            return total + jnp.sum(terms.reshape(8, 8, 1024), axis=0)

        total = lax.fori_loop(0, 8, norm_two, jnp.zeros((8, 1024), F32), unroll=2)
        dscale[1:2] = jnp.sum(total, axis=0, keepdims=True)
        load_w3.wait()
        for n in range(2):
            cols = slice(512 * n, 512 * n + 512)
            datt[:, cols] = dot_nt(rh[5], wout[cols, :]).astype(BF)

    def attend_back(pair):
        at = pl.ds(pl.multiple_of(pair * 128, 128), 128)
        q_pair, k_pair, v_pair, d_pair = qkv[0, :, at], qkv[1, :, at], qkv[2, :, at], datt[:, at]
        k_turned = (k_pair * jnp.asarray(0.125, BF)).T
        heads = [lax.div(lanes, 64) == j for j in range(2)]
        raws = [dot_nt(jnp.where(mine, k_pair, feat_in[1]), jnp.where(mine, q_pair, feat_in[0])) for mine in heads]
        d_probs = [dot_nt(v_pair, jnp.where(mine, d_pair, jnp.zeros_like(d_pair))) for mine in heads]
        made = []
        for j in range(2):
            probs = jnp.exp(raws[j] - lse_in[pair, j:j + 1])
            delta = jnp.sum(probs * d_probs[j], axis=0, keepdims=True)
            d_raw = (probs * (d_probs[j] - delta)).astype(BF)
            made.append((dot(k_turned[64 * j:64 * j + 64], d_raw), dot(d_raw, q_pair), dot(probs.astype(BF), d_pair)))
        rh[6, :, at] = unrotate(jnp.concatenate([made[0][0], made[1][0]], axis=0).T).astype(BF)
        rh[7, :, at] = unrotate(jnp.where(heads[0], made[0][1], made[1][1])).astype(BF)
        rh[8, :, at] = jnp.where(heads[0], made[0][2], made[1][2]).astype(BF)

    def first_back(k):
        for h in range(2):
            cols = slice(512 * h, 512 * h + 512)
            part = dot_nt(rh[6 + k, :, :512], thirds[k, 0, cols]) + dot_nt(rh[6 + k, :, 512:], thirds[k, 1, cols])

            @pl.when(k == 0)
            def _():
                acc[:, cols] = part

            @pl.when(k > 0)
            def _():
                acc[:, cols] += part

    def input_back():
        def norm_one(b, total):
            rows = pl.ds(pl.multiple_of(b * 64, 64), 64)
            back, terms = norm_back(xin[rows].astype(F32), acc[rows], scales_in[0:1])
            obuf[rows] = (dmid[rows] + back).astype(BF)
            return total + jnp.sum(terms.reshape(8, 8, 1024), axis=0)

        total = lax.fori_loop(0, 8, norm_one, jnp.zeros((8, 1024), F32), unroll=2)
        dscale[0:1] = jnp.sum(total, axis=0, keepdims=True)
        store_out.start()
        red.away[(CHUNKS - 1) % SLOTS] = cond_part(1 - core).astype(BF)
        red.part[(CHUNKS - 1) % PART_SLOTS] = cond_part(core).astype(BF)
        red.c_sib(jnp.int32(CHUNKS - 1)).start()

    store_out = pltpu.make_async_copy(obuf, in_grad, out_sem)
    load_cot.wait()
    load_lt[0].wait()

    def turn(m, carry):
        for when, copies in arrivals.items():
            @pl.when(m == when)
            def _(copies=copies):
                for copy in copies:
                    copy.wait()

        @pl.when(m < 12)
        def _():
            give(2 * m)
            give(2 * m + 1)

        pl.when(m == 0)(middle_back)
        pl.when(jnp.logical_and(m >= 1, m < 9))(lambda: attend_back(m - 1))

        pl.when(jnp.logical_and(m >= 9, m < 12))(lambda: first_back(m - 9))
        pl.when(m == 12)(input_back)
        def ticks(t, carry):
            red.tick(t, put)
            return carry

        lax.fori_loop(2 * m, 2 * m + 2, ticks, 0)

        return carry

    lax.fori_loop(0, (CHUNKS + LAGS[-1] + 1) // 2, turn, 0)
    store_out.wait()


def backward(turn, lse, scales, te, feat, thirds, w, lt, cot, dpre, qkv, mid, back, x):
    vmem = pl.BlockSpec(memory_space=pltpu.VMEM)
    anyw = pl.BlockSpec(memory_space=pl.ANY)
    shape = jax.ShapeDtypeStruct
    return pl.pallas_call(
        backward_kernel,
        out_shape=(
            shape((CHUNKS, 128, 512), BF), shape((512, 1024), BF)),
        in_specs=[vmem] * 5 + [anyw] * 9,
        out_specs=(vmem, anyw),
        scratch_shapes=[
            pltpu.VMEM((7, 2, 512, 512), BF),
            pltpu.VMEM((9, 512, 1024), BF),
            pltpu.VMEM((3, 2, 1024, 512), BF),
            pltpu.VMEM((1024, 1024), BF),
            pltpu.VMEM((3, 512, 1024), BF),
            pltpu.VMEM((512, 1024), F32),
            pltpu.VMEM((512, 1024), F32),
            pltpu.VMEM((512, 1024), F32),
            pltpu.VMEM((512, 1024), BF),
            pltpu.VMEM((512, 1024), BF),
            pltpu.VMEM((2, 1024), F32),
            pltpu.VMEM((512, 1024), BF),
            pltpu.VMEM((8, 32, 1), F32),
            pltpu.SemaphoreType.DMA((16,)),
            pltpu.SemaphoreType.DMA,
        ] + Reducer.scratch(),
        compiler_params=pltpu.CompilerParams(collective_id=1, has_side_effects=True, vmem_limit_bytes=63 * 2**20),
    )(turn, lse, scales, te, feat, thirds.reshape(3, 2, 1024, 512), w.reshape(1024, 1024), lt, cot, dpre, qkv, mid, back.reshape(512, 1024), x)


def update_kernel(*refs):
    sums, states, rows, outs, rows_out = refs[0], refs[1:17], refs[17:19], refs[19:39], refs[39:41]
    fresh, held, made, passed, in_sem, out_sem, pass_sem = refs[41:]
    mix, cond, up, down = range(4)
    units = [(kind, i) for kind in (down, up, mix) for i in range(4)] + [(cond, 0)]
    keep_one = 1.0 / (1.0 - 0.5**STEP)

    def piece(ref, kind, i):
        if kind == up:
            return ref.at[:, pl.ds(1024 * i, 1024)]
        if kind == cond:
            return ref
        return ref.at[i] if len(ref.shape) == 3 else ref.at[pl.ds(128 * i, 128)]

    def summed(kind, i, buffer):
        if kind == cond:
            return [(sums.at[24, pl.ds(64 * k + 32 * h, 32)], buffer.at[pl.ds(32 * k, 32), pl.ds(512 * h, 512)])
                    for k in range(2) for h in range(2)]
        if kind == up:
            half, first = i // 2, 2 * (i % 2)
            return [(sums.at[8 + 2 * n + half, :, pl.ds(128 * (first + a), 128)], buffer.at[:, pl.ds(512 * a + 128 * n, 128)])
                    for n in range(4) for a in range(2)]
        chunk = 2 * i if kind == down else 16 + 2 * ((i + 1) % 4)
        return [(sums.at[chunk + h], buffer.at[:, pl.ds(512 * h, 512)]) for h in range(2)]

    def loads(u):
        kind, i = units[u]
        s = u % RING
        copies = [(a, b, in_sem.at[s, 8 + n]) for n, (a, b) in enumerate(summed(kind, i, fresh.at[s]))]
        for n, ref in enumerate(states[4 * kind:4 * kind + 4]):
            if kind == cond:
                for k in range(2):
                    copies.append((ref.at[k], held.at[s, n, pl.ds(32 * k, 32)], in_sem.at[s, 4 * k + n]))
            else:
                copies.append((piece(ref, kind, i), held.at[s, n], in_sem.at[s, n]))
        return [pltpu.make_async_copy(*c) for c in copies]

    def saves(u):
        kind, i = units[u]
        s = u % RING
        copies = []
        for n in range(5):
            ref, buffer = outs[5 * kind + n], made.at[s, n]
            if kind == cond:
                for k in range(2):
                    copies.append((buffer.at[pl.ds(32 * k, 32)], ref.at[k], out_sem.at[s, 5 * k + n]))
            else:
                copies.append((buffer, piece(ref, kind, i), out_sem.at[s, n]))
        return [pltpu.make_async_copy(*c) for c in copies]

    enter = [pltpu.make_async_copy(rows[n], passed.at[n], pass_sem.at[n]) for n in range(2)]
    leave = [pltpu.make_async_copy(passed.at[n], rows_out[n].at[0], pass_sem.at[n]) for n in range(2)]
    for u in range(RING - 1):
        for copy in loads(u):
            copy.start()
    for copy in enter:
        copy.start()
    for u in range(len(units)):
        s = u % RING
        if u == 2:
            for n in range(2):
                enter[n].wait()
                leave[n].start()
        if u + RING - 1 < len(units):
            for copy in loads(u + RING - 1):
                copy.start()
        if u >= RING:
            for copy in saves(u - RING):
                copy.wait()
        for copy in loads(u):
            copy.wait()

        def rows_step(b, carry):
            rows = pl.ds(pl.multiple_of(b * 16, 16), 16)
            g = fresh[s, rows].astype(F32)
            w = held[s, 0, rows]
            m = 0.5 * held[s, 1, rows] + 0.5 * g
            v = 0.5 * held[s, 2, rows] + 0.5 * g * g
            w_new = w - 0.01 * (m * keep_one / (jnp.sqrt(v * keep_one) + 1e-08) + 0.1 * w)
            made[s, 0, rows] = g
            made[s, 1, rows] = m
            made[s, 2, rows] = v
            made[s, 3, rows] = w_new
            made[s, 4, rows] = 0.8 * held[s, 3, rows] + 0.2 * w_new
            return carry

        lax.fori_loop(0, 4 if units[u][0] == cond else 8, rows_step, 0)
        for copy in saves(u):
            copy.start()
    for u in range(len(units) - RING, len(units)):
        for copy in saves(u):
            copy.wait()
    for copy in leave:
        copy.wait()


RING = 4


def update(sums, states, rows):
    anyw = pl.BlockSpec(memory_space=pl.ANY)
    outs = []
    for n in range(4):
        outs += [jax.ShapeDtypeStruct(states[4 * n].shape, F32)] * 5
    outs += [jax.ShapeDtypeStruct((1, 512, 1024), BF)] * 2
    *made, output, input_grad = pl.pallas_call(
        update_kernel,
        out_shape=tuple(outs),
        in_specs=[anyw] * 19,
        out_specs=(anyw,) * 22,
        scratch_shapes=[
            pltpu.VMEM((RING, 128, 1024), BF),
            pltpu.VMEM((RING, 4, 128, 1024), F32),
            pltpu.VMEM((RING, 5, 128, 1024), F32),
            pltpu.VMEM((2, 512, 1024), BF),
            pltpu.SemaphoreType.DMA((RING, 16)),
            pltpu.SemaphoreType.DMA((RING, 10)),
            pltpu.SemaphoreType.DMA((2,)),
        ],
        compiler_params=pltpu.CompilerParams(vmem_limit_bytes=63 * 2**20),
    )(sums, *states, *rows)
    return (output, input_grad, *made)


def normed(values):
    center = values - jnp.mean(values, axis=-1, keepdims=True)
    spread = jnp.mean(center * center, axis=-1, keepdims=True)
    return center * lax.rsqrt(spread + 1e-05)


def scaled_norm(values, gain):
    return normed(values) * gain[None, :]


def rotary_tables(segments):
    length = segments.shape[0]
    position = jnp.arange(length, dtype=jnp.int32)
    is_start = jnp.concatenate([jnp.ones((1,), dtype=bool), segments[1:] != segments[:-1]])
    seg_start = lax.cummax(jnp.where(is_start, position, jnp.zeros_like(position)), axis=0)
    offset = (position - seg_start).astype(jnp.float32)
    frequency = 10000.0 ** (-jnp.arange(HEAD_DIM // 2, dtype=jnp.float32) * 2.0 / HEAD_DIM)
    turned = offset[:, None] * frequency[None, :]
    return (jnp.cos(turned)[:, None, :], jnp.sin(turned)[:, None, :])


def rotate(parts, cos_table, sin_table):
    half_dim = parts.shape[-1] // 2
    part_a = parts[..., :half_dim]
    part_b = parts[..., half_dim:]
    return jnp.concatenate(
        [part_a * cos_table - part_b * sin_table, part_b * cos_table + part_a * sin_table], axis=-1
    )


def unrotate(grads, cos_table, sin_table):
    half_dim = grads.shape[-1] // 2
    grad_a = grads[..., :half_dim]
    grad_b = grads[..., half_dim:]
    return jnp.concatenate(
        [grad_a * cos_table + grad_b * sin_table, grad_b * cos_table - grad_a * sin_table], axis=-1
    )


def adam_update(gradient, weight, moment_one, moment_two, average):
    moment_one_new = 0.5 * moment_one + 0.5 * gradient
    moment_two_new = 0.5 * moment_two + 0.5 * gradient * gradient
    correction = 1.0 - 0.5**STEP
    update = (
        moment_one_new / correction / (jnp.sqrt(moment_two_new / correction) + 1e-08) + 0.1 * weight
    )
    weight_new = weight - 0.01 * update
    average_new = 0.8 * average + 0.2 * weight_new
    return (moment_one_new, moment_two_new, weight_new, average_new)


def local(
    tokens,
    time_embed,
    segment_ids,
    cotangent,
    mixing_w,
    mixing_m,
    mixing_v,
    mixing_avg,
    cond_w,
    cond_m,
    cond_v,
    cond_avg,
    up_w,
    up_m,
    up_v,
    up_avg,
    down_w,
    down_m,
    down_v,
    down_avg,
):
    rows_in = tokens[0].astype(jnp.float32)
    embedding = time_embed[0]
    segments = segment_ids[0]
    length = rows_in.shape[0]
    block_rows = min(512, length)
    block_count = length // block_rows
    mixing_g, cond_g = (
        lax.all_gather(mixing_w.astype(jnp.bfloat16), "fsdp", axis=1, tiled=True),
        lax.all_gather(cond_w.astype(jnp.bfloat16), "fsdp", axis=1, tiled=True),
    )
    up_g, down_g = (
        lax.all_gather(up_w.astype(jnp.bfloat16), "fsdp", axis=0, tiled=True),
        lax.all_gather(down_w.astype(jnp.bfloat16), "fsdp", axis=0, tiled=True),
    )
    scales = 1.0 + jnp.einsum("e,ked->kd", embedding, cond_g, preferred_element_type=jnp.float32)
    cos_table, sin_table = rotary_tables(segments)
    normed_one = (normed(rows_in) * scales[0][None, :]).astype(jnp.bfloat16)
    projected = jnp.einsum(
        "td,kde->kte", normed_one, mixing_g[:3], preferred_element_type=jnp.float32
    )
    queries = rotate(projected[0].reshape(length, HEADS, HEAD_DIM), cos_table, sin_table).astype(
        jnp.bfloat16
    )
    keys_rot = rotate(projected[1].reshape(length, HEADS, HEAD_DIM), cos_table, sin_table).astype(
        jnp.bfloat16
    )
    values_b = projected[2].astype(jnp.bfloat16).reshape(length, HEADS, HEAD_DIM)
    query_blocks = queries.reshape(block_count, block_rows, HEADS, HEAD_DIM)
    seg_blocks = segments.reshape(block_count, block_rows)

    def block_scores(q_block, seg_block):
        raw = (
            jnp.einsum("qhd,khd->hqk", q_block, keys_rot, preferred_element_type=jnp.float32)
            * 0.125
        )
        same_seg = seg_block[:, None] == segments[None, :]
        return jnp.where(same_seg[None], raw, -1e30)

    def attend_block(element):
        q_block, seg_block = element
        raw = block_scores(q_block, seg_block)
        peak = jnp.max(raw, axis=-1, keepdims=True)
        exp_scores = jnp.exp(raw - peak)
        totals = jnp.sum(exp_scores, axis=-1, keepdims=True)
        probs = (exp_scores / totals).astype(jnp.bfloat16)
        out_block = jnp.einsum(
            "hqk,khd->qhd", probs, values_b, preferred_element_type=jnp.float32
        ).astype(jnp.bfloat16)
        return (out_block, peak[..., 0] + jnp.log(totals[..., 0]))

    attended, log_totals = lax.map(attend_block, (query_blocks, seg_blocks))
    attended = attended.reshape(length, D)
    middle = rows_in + jnp.dot(attended, mixing_g[3], preferred_element_type=jnp.float32)
    normed_two = (normed(middle) * scales[1][None, :]).astype(jnp.bfloat16)
    hidden_pre = jnp.dot(normed_two, up_g, preferred_element_type=jnp.float32)
    hidden_act = jax.nn.gelu(hidden_pre).astype(jnp.bfloat16)
    output = (middle + jnp.dot(hidden_act, down_g, preferred_element_type=jnp.float32)).astype(
        jnp.bfloat16
    )
    mixing_b, cond_b = (
        lax.all_gather(mixing_w.astype(jnp.bfloat16), "fsdp", axis=1, tiled=True),
        lax.all_gather(cond_w.astype(jnp.bfloat16), "fsdp", axis=1, tiled=True),
    )
    up_b, down_b = (
        lax.all_gather(up_w.astype(jnp.bfloat16), "fsdp", axis=0, tiled=True),
        lax.all_gather(down_w.astype(jnp.bfloat16), "fsdp", axis=0, tiled=True),
    )
    back_out = cotangent[0]
    d_act = jnp.einsum("td,fd->tf", back_out, down_b, preferred_element_type=jnp.float32)
    d_down = jnp.einsum("tf,td->fd", hidden_act, back_out, preferred_element_type=jnp.float32)
    _, gelu_pull = jax.vjp(jax.nn.gelu, hidden_pre)
    d_pre = gelu_pull(d_act)[0].astype(jnp.bfloat16)
    d_up = jnp.einsum("td,tf->df", normed_two, d_pre, preferred_element_type=jnp.float32)
    d_normed_two = jnp.einsum("tf,df->td", d_pre, up_b, preferred_element_type=jnp.float32)
    _, norm_pull_two = jax.vjp(scaled_norm, middle, scales[1])
    d_middle, d_scale_two = norm_pull_two(d_normed_two)
    d_middle = d_middle + back_out.astype(jnp.float32)
    d_middle_b = d_middle.astype(jnp.bfloat16)
    d_out_proj = jnp.einsum("td,te->de", attended, d_middle_b, preferred_element_type=jnp.float32)
    d_attended = jnp.einsum(
        "te,de->td", d_middle_b, mixing_b[3], preferred_element_type=jnp.float32
    ).astype(jnp.bfloat16)
    d_att_blocks = d_attended.reshape(block_count, block_rows, HEADS, HEAD_DIM)

    def back_block(state_in, element):
        q_block, seg_block, d_block, log_block = element
        raw = block_scores(q_block, seg_block)
        probs_f = jnp.exp(raw - log_block[..., None])
        probs_b = probs_f.astype(jnp.bfloat16)
        d_probs = jnp.einsum("qhd,khd->hqk", d_block, values_b, preferred_element_type=jnp.float32)
        d_raw = (probs_f * (d_probs - jnp.sum(probs_f * d_probs, axis=-1, keepdims=True))).astype(
            jnp.bfloat16
        )
        d_query = (
            jnp.einsum("hqk,khd->qhd", d_raw, keys_rot, preferred_element_type=jnp.float32) * 0.125
        )
        keys_acc = (
            state_in[0]
            + jnp.einsum("hqk,qhd->khd", d_raw, q_block, preferred_element_type=jnp.float32) * 0.125
        )
        values_acc = state_in[1] + jnp.einsum(
            "hqk,qhd->khd", probs_b, d_block, preferred_element_type=jnp.float32
        )
        return ((keys_acc, values_acc), d_query)

    zero_heads = jnp.zeros((length, HEADS, HEAD_DIM), jnp.float32)
    (d_keys, d_values), d_queries = lax.scan(
        back_block, (zero_heads, zero_heads), (query_blocks, seg_blocks, d_att_blocks, log_totals)
    )
    d_queries = unrotate(d_queries.reshape(length, HEADS, HEAD_DIM), cos_table, sin_table)
    d_keys = unrotate(d_keys, cos_table, sin_table)
    d_projected = (
        jnp.stack([d_queries, d_keys, d_values]).reshape(3, length, D).astype(jnp.bfloat16)
    )
    d_qkv = jnp.einsum("td,kte->kde", normed_one, d_projected, preferred_element_type=jnp.float32)
    d_normed_one = jnp.einsum(
        "kte,kde->td", d_projected, mixing_b[:3], preferred_element_type=jnp.float32
    )
    _, norm_pull_one = jax.vjp(scaled_norm, rows_in, scales[0])
    d_rows, d_scale_one = norm_pull_one(d_normed_one)
    input_grad = (d_middle + d_rows).astype(jnp.bfloat16)
    d_scales = jnp.stack([d_scale_one, d_scale_two])
    d_cond = embedding.astype(jnp.float32)[None, :, None] * d_scales[:, None, :]
    d_mixing = jnp.concatenate([d_qkv, d_out_proj[None]], axis=0)
    mixing_part, cond_part = (
        lax.psum_scatter(d_mixing, "fsdp", scatter_dimension=1, tiled=True),
        lax.psum_scatter(d_cond, "fsdp", scatter_dimension=1, tiled=True),
    )
    up_part, down_part = (
        lax.psum_scatter(d_up, "fsdp", scatter_dimension=0, tiled=True),
        lax.psum_scatter(d_down, "fsdp", scatter_dimension=0, tiled=True),
    )
    mixing_grad, cond_grad, up_grad, down_grad = (
        lax.psum(mixing_part.astype(jnp.bfloat16), "rows").astype(jnp.float32),
        lax.psum(cond_part.astype(jnp.bfloat16), "rows").astype(jnp.float32),
        lax.psum(up_part.astype(jnp.bfloat16), "rows").astype(jnp.float32),
        lax.psum(down_part.astype(jnp.bfloat16), "rows").astype(jnp.float32),
    )
    mix_one, mix_two, mix_new, mix_average = adam_update(
        mixing_grad, mixing_w, mixing_m, mixing_v, mixing_avg
    )
    cond_one, cond_two, cond_new, cond_average = adam_update(
        cond_grad, cond_w, cond_m, cond_v, cond_avg
    )
    up_one, up_two, up_new, up_average = adam_update(up_grad, up_w, up_m, up_v, up_avg)
    down_one, down_two, down_new, down_average = adam_update(
        down_grad, down_w, down_m, down_v, down_avg
    )
    return (
        output[None],
        input_grad[None],
        mixing_grad,
        mix_one,
        mix_two,
        mix_new,
        mix_average,
        cond_grad,
        cond_one,
        cond_two,
        cond_new,
        cond_average,
        up_grad,
        up_one,
        up_two,
        up_new,
        up_average,
        down_grad,
        down_one,
        down_two,
        down_new,
        down_average,
    )


def local_small(
    tokens, time_embed, segment_ids, cotangent,
    mixing_w, mixing_m, mixing_v, mixing_avg,
    cond_w, cond_m, cond_v, cond_avg,
    up_w, up_m, up_v, up_avg,
    down_w, down_m, down_v, down_avg,
):
    x, cot = tokens[0], cotangent[0]
    lse, scales, turn, feat, thirds, w, lt, dpre, qkv, middle, back, output = forward(
        segment_ids, time_embed, x, cot, mixing_w, cond_w, up_w, down_w)
    sums, input_grad = backward(turn, lse, scales, time_embed, feat, thirds, w, lt, cot, dpre, qkv, middle, back, x)
    states = (
        mixing_w, mixing_m, mixing_v, mixing_avg, cond_w, cond_m, cond_v, cond_avg,
        up_w, up_m, up_v, up_avg, down_w, down_m, down_v, down_avg)
    return update(sums, states, (output, input_grad))


def solution(mesh):
    small = mesh.shape["rows"] == 4 and mesh.shape["fsdp"] == 8
    placed = (
        P(("rows", "fsdp"), None, None),
        P(("rows", "fsdp"), None),
        P(("rows", "fsdp"), None),
        P(("rows", "fsdp"), None, None),
        P(None, "fsdp", None),
        P(None, "fsdp", None),
        P(None, "fsdp", None),
        P(None, "fsdp", None),
        P(None, "fsdp", None),
        P(None, "fsdp", None),
        P(None, "fsdp", None),
        P(None, "fsdp", None),
        P("fsdp", None),
        P("fsdp", None),
        P("fsdp", None),
        P("fsdp", None),
        P("fsdp", None),
        P("fsdp", None),
        P("fsdp", None),
        P("fsdp", None),
    )
    return jax.shard_map(
        local_small if small else local,
        mesh=mesh,
        in_specs=placed,
        out_specs=(
            P(("rows", "fsdp"), None, None),
            P(("rows", "fsdp"), None, None),
            P(None, "fsdp", None),
            P(None, "fsdp", None),
            P(None, "fsdp", None),
            P(None, "fsdp", None),
            P(None, "fsdp", None),
            P(None, "fsdp", None),
            P(None, "fsdp", None),
            P(None, "fsdp", None),
            P(None, "fsdp", None),
            P(None, "fsdp", None),
            P("fsdp", None),
            P("fsdp", None),
            P("fsdp", None),
            P("fsdp", None),
            P("fsdp", None),
            P("fsdp", None),
            P("fsdp", None),
            P("fsdp", None),
            P("fsdp", None),
            P("fsdp", None),
        ),
        check_vma=False,
    )
```

```python
import jax
import jax.numpy as jnp
import numpy as np
from jax import lax
from jax.experimental import pallas as pl
from jax.experimental.pallas import tpu as pltpu
from jax.sharding import PartitionSpec as P

D = 1024
HEADS = 16
HEAD_DIM = 64
STEP = 7
F32 = jnp.float32
BF = jnp.bfloat16


MESH = pl.DeviceIdType.MESH
CHUNKS = 25
SLOTS = 4
SIB_SLOTS = 6
LINE_SLOTS = 6
PART_SLOTS = 10
LAGS = (1, 3, 5, 7, 9, 11, 13)


class Reducer:
    def __init__(self, refs):
        (self.away, self.part, self.sib, self.swap, self.diag, self.near, self.zin, self.zmid, self.tsum, self.out_a, self.out_b,
         self.sems_sib, self.sems_swap, self.sems_diag, self.sems_near, self.sems_zin, self.sems_zmid) = refs
        self.me = lax.axis_index("fsdp")
        self.core = lax.rem(self.me, 2)
        self.chip = lax.div(self.me, 2)
        self.row = lax.axis_index("rows")
        self.inner = jnp.logical_and(self.row >= 1, self.row <= 2)
        self.outer = jnp.logical_not(self.inner)
        self.line_to = jnp.where(self.row == 0, 1, jnp.where(self.row == 1, 0, jnp.where(self.row == 2, 3, 2)))
        self.mid_to = jnp.where(self.row == 1, 2, 1)
        xbit = lax.rem(self.chip, 2)
        ybit = lax.div(self.chip, 2)
        self.chip_x = ybit * 2 + (1 - xbit)
        self.chip_y = (1 - ybit) * 2 + xbit
        self.chip_d = (1 - ybit) * 2 + (1 - xbit)
        self.mine = pl.multiple_of(lax.rem(self.row, 2) * 64, 64)
        self.to_sib = {"fsdp": self.chip * 2 + (1 - self.core)}
        self.to_x = {"fsdp": self.chip_x * 2 + self.core}
        self.to_y = {"fsdp": self.chip_y * 2 + self.core}

    @staticmethod
    def scratch():
        s = SLOTS
        bf = jnp.bfloat16
        dma = pltpu.SemaphoreType.DMA
        return [
            pltpu.VMEM((SLOTS, 4, 128, 512), bf),
            pltpu.VMEM((PART_SLOTS, 4, 128, 512), bf),
            pltpu.VMEM((SIB_SLOTS, 4, 128, 512), bf),
            pltpu.VMEM((LINE_SLOTS, 64, 512), bf),
            pltpu.VMEM((s, 128, 512), bf),
            pltpu.VMEM((s, 2, 128, 512), bf),
            pltpu.VMEM((LINE_SLOTS, 128, 512), bf),
            pltpu.VMEM((LINE_SLOTS, 128, 512), bf),
            pltpu.VMEM((LINE_SLOTS, 128, 512), jnp.float32),
            pltpu.VMEM((LINE_SLOTS, 128, 512), bf),
            pltpu.VMEM((LINE_SLOTS, 128, 512), bf),
            dma((2, SIB_SLOTS)),
            dma((2, LINE_SLOTS)),
            dma((2, s)),
            dma((2, s)),
            dma((2, LINE_SLOTS)),
            dma((2, LINE_SLOTS)),
        ]

    def enter(self):
        barrier = pltpu.get_barrier_semaphore()
        for to in (self.to_sib, self.to_x, self.to_y, {"rows": self.line_to}):
            pl.semaphore_signal(barrier, inc=1, device_id=to, device_id_type=MESH)

        @pl.when(self.inner)
        def _():
            pl.semaphore_signal(barrier, inc=1, device_id={"rows": self.mid_to}, device_id_type=MESH)
            pl.semaphore_wait(barrier, 5)

        @pl.when(self.outer)
        def _():
            pl.semaphore_wait(barrier, 4)

    def copy(self, src, dst, sems, which, slot, to):
        return pltpu.make_async_remote_copy(
            src_ref=src, dst_ref=dst, send_sem=sems.at[which, slot], recv_sem=sems.at[which + sems.shape[0] // 2, slot],
            device_id=to, device_id_type=MESH)

    def c_sib(self, g):
        n = lax.rem(g, SIB_SLOTS)
        return self.copy(self.away.at[lax.rem(g, SLOTS)], self.sib.at[n], self.sems_sib, 0, n, self.to_sib)

    def shared(self, g):
        return jnp.logical_and(lax.rem(g, 3) != 2, g < CHUNKS - 2)

    def by_kind(self, g, stage):
        pl.when(self.shared(g))(lambda: stage(g, self.mine, 32))
        pl.when(jnp.logical_not(self.shared(g)))(lambda: stage(g, 0, 64))

    def c_swap(self, g):
        s = lax.rem(g, LINE_SLOTS)
        theirs = pl.ds(pl.multiple_of(64 - self.mine, 64), 64)
        return self.copy(self.part.at[lax.rem(g, PART_SLOTS), self.chip_d, theirs], self.swap.at[s], self.sems_swap, 0, s, {"rows": self.line_to})

    def c_diag(self, g, k, first, size):
        s, to, rows = lax.rem(g, SLOTS), (self.to_x if k == 0 else self.to_y), pl.ds(first + size * k, size)
        return self.copy(self.part.at[lax.rem(g, PART_SLOTS), self.chip_d, rows], self.diag.at[s, rows], self.sems_diag, 0, s, to)

    def c_near(self, g, k):
        s, (to, chip) = lax.rem(g, SLOTS), ((self.to_x, self.chip_x) if k == 0 else (self.to_y, self.chip_y))
        return self.copy(self.part.at[lax.rem(g, PART_SLOTS), chip], self.near.at[s, k], self.sems_near, 0, s, to)

    def both_diag(self, g, first, size):
        s, rows = lax.rem(g, SLOTS), pl.ds(first, 2 * size)
        return self.copy(self.part.at[lax.rem(g, PART_SLOTS), self.chip_d, rows], self.diag.at[s, rows], self.sems_diag, 0, s, self.to_x)

    def both_near(self, g):
        s = lax.rem(g, SLOTS)
        return self.copy(self.part.at[lax.rem(g, PART_SLOTS), pl.ds(0, 2)], self.near.at[s], self.sems_near, 0, s, self.to_x)

    def c_line(self, s):
        return self.copy(self.out_a.at[s], self.zin.at[s], self.sems_zin, 0, s, {"rows": self.line_to})

    def c_mid(self, s):
        return self.copy(self.out_b.at[s], self.zmid.at[s], self.sems_zmid, 0, s, {"rows": self.mid_to})

    def stage_b(self, g):
        p, n = lax.rem(g, PART_SLOTS), lax.rem(g, SIB_SLOTS)
        self.c_sib(g).wait()
        self.part[p] = (self.part[p].astype(jnp.float32) + self.sib[n].astype(jnp.float32)).astype(jnp.bfloat16)
        pl.when(self.shared(g))(lambda: self.c_swap(g).start())

    def add(self, g, chip, first, size, more):
        p, rows = lax.rem(g, PART_SLOTS), pl.ds(first, size)
        total = self.part[p, chip, rows].astype(jnp.float32) + more.astype(jnp.float32)
        self.part[p, chip, rows] = total.astype(jnp.bfloat16)

    def stage_d(self, g, first, size):
        if size == 32:
            self.c_swap(g).wait()
            self.add(g, self.chip_d, first, 64, self.swap[lax.rem(g, LINE_SLOTS)])
        self.c_diag(g, 0, first, size).start()
        self.c_diag(g, 1, first, size).start()

    def stage_c(self, g, first, size):
        s = lax.rem(g, SLOTS)
        self.both_diag(g, first, size).wait()
        self.add(g, self.chip_y, first, size, self.diag[s, pl.ds(first, size)])
        self.c_near(g, 1).start()
        self.add(g, self.chip_x, first + size, size, self.diag[s, pl.ds(first + size, size)])
        self.c_near(g, 0).start()

    def stage_e(self, g):
        s, p = lax.rem(g, SLOTS), lax.rem(g, PART_SLOTS)
        self.both_near(g).wait()
        total = (self.part[p, self.chip].astype(jnp.float32) + self.near[s, 0].astype(jnp.float32)) + self.near[s, 1].astype(jnp.float32)
        n = lax.rem(g, LINE_SLOTS)
        self.tsum[n] = total

        @pl.when(self.outer)
        def _():
            self.out_a[n] = total.astype(jnp.bfloat16)
            self.c_line(n).start()

    def stage_f(self, g):
        s = lax.rem(g, LINE_SLOTS)

        @pl.when(self.inner)
        def _():
            self.c_line(s).wait_recv()
            self.out_b[s] = (self.tsum[s] + self.zin[s].astype(jnp.float32)).astype(jnp.bfloat16)
            self.c_mid(s).start()

    def stage_h(self, g, put):
        s = lax.rem(g, LINE_SLOTS)

        @pl.when(self.inner)
        def _():
            self.c_mid(s).wait()
            total = (self.out_b[s].astype(jnp.float32) + self.zmid[s].astype(jnp.float32)).astype(jnp.bfloat16)
            self.out_a[s] = total
            self.c_line(s).start()
            put(g, total)

    def stage_i(self, g, put):
        s = lax.rem(g, LINE_SLOTS)

        @pl.when(self.outer)
        def _():
            self.c_line(s).wait()
            put(g, self.zin[s])

        @pl.when(self.inner)
        def _():
            self.c_line(s).wait_send()

    def tick(self, t, put):
        b, d, c, e, f, h, i = LAGS

        def run(lag, stage, *args):
            g = t - lag
            pl.when(jnp.logical_and(g >= 0, g < CHUNKS))(lambda: stage(g, *args))

        run(i, self.stage_i, put)
        run(h, self.stage_h, put)
        run(f, self.stage_f)
        run(e, self.stage_e)
        run(c, lambda g: self.by_kind(g, self.stage_c))
        run(d, lambda g: self.by_kind(g, self.stage_d))
        run(b, self.stage_b)


def dot(a, b):
    return lax.dot_general(a, b, (((1,), (0,)), ((), ())), preferred_element_type=F32)


def dot_nt(a, b):
    return lax.dot_general(a, b, (((1,), (1,)), ((), ())), preferred_element_type=F32)


START, LINK, SIBLING, HOP, ISSUE, LEAD = 6.0, 50.0, 300.0, 2.0, 0.05, 4.0
PIECES = [(-1, 0, 1024, True)]
PIECES += [(k, 512 * h, 512, k == 2 and h == 0) for h in range(2) for k in range(3)]
PIECES += [(-2, 0, 1024, True), (3, 0, 1024, False)]
PIECES += [(4 + n, 0, 1024, n in (1, 4, 6, 7)) for n in range(8)]
COND_TWO, OUT_W, UP_W, DOWN_W = 7, 8, 9, 13


SHARED = {4: 3, 5: 0, 6: 0, 7: 0, 9: 8, 10: 8}


class Gatherer:
    def __init__(self, refs):
        self.cond, self.thirds, self.mats, self.send, self.recv = refs
        self.me = lax.axis_index("fsdp")
        core = lax.rem(self.me, 2)
        chip = lax.div(self.me, 2)
        xbit, ybit = lax.rem(chip, 2), lax.div(chip, 2)
        self.x = (ybit * 2 + 1 - xbit) * 2 + core
        self.y = ((1 - ybit) * 2 + xbit) * 2 + core
        self.d = ((1 - ybit) * 2 + 1 - xbit) * 2 + core
        self.sib = chip * 2 + 1 - core
        row = lax.axis_index("rows")
        self.half = lax.rem(row, 2)
        self.to_z = {"rows": row + 1 - 2 * self.half}
        self.time = START
        self.free = {"x": 0.0, "y": 0.0, "z": 0.0, "s": 0.0}
        self.due = {}
        self.waiting = []
        self.begun, self.whole = 0, set()

    @staticmethod
    def scratch():
        return [
            pltpu.VMEM((8, 64, 1024), BF),
            pltpu.VMEM((3, 2, 8, 128, 512), BF),
            pltpu.VMEM((9, 8, 128, 1024), BF),
            pltpu.SemaphoreType.DMA((len(PIECES), 11)),
            pltpu.SemaphoreType.DMA((len(PIECES), 11)),
        ]

    def enter(self):
        barrier = pltpu.get_barrier_semaphore()
        for to in ({"fsdp": self.sib}, {"fsdp": self.x}, {"fsdp": self.y}, self.to_z):
            pl.semaphore_signal(barrier, inc=1, device_id=to, device_id_type=MESH)
        pl.semaphore_wait(barrier, 4)

    @staticmethod
    def direct(c):
        return PIECES[c][3]

    def shard(self, c, owner, start=0, size=None):
        mat, col, cols, _ = PIECES[c]
        if mat < 0:
            base = 32 * (-1 - mat)
            return self.cond.at[owner, pl.ds(base + start, 32 if size is None else size)]
        rows = pl.ds(start, 128 if size is None else size)
        return self.thirds.at[mat, col // 512, owner, rows] if mat < 3 else self.mats.at[mat - 3, owner, rows]

    def copy(self, c, kind, owner, to, start=0, size=None):
        ref = self.shard(c, owner, start, size)
        return pltpu.make_async_remote_copy(
            src_ref=ref, dst_ref=ref, send_sem=self.send.at[c, kind], recv_sem=self.recv.at[c, SHARED.get(kind, kind)],
            device_id=to, device_id_type=MESH)

    def landed(self, c, kind, rows):
        mat, _, cols, _ = PIECES[c]
        if mat < 0:
            ref = self.cond.at[pl.ds(0, 4), pl.ds(0, 32)] if rows == 128 else self.cond.at[0, pl.ds(0, rows)]
        else:
            base = self.thirds.at[mat, 0] if mat < 3 else self.mats.at[mat - 3]
            ref = base.at[pl.ds(0, rows // 128)] if rows >= 128 else base.at[0, pl.ds(0, rows)]
            if rows == 192:
                ref = base.at[pl.ds(0, 3), pl.ds(0, 64)]
        pltpu.make_async_remote_copy(
            src_ref=ref, dst_ref=ref, send_sem=self.send.at[c, kind], recv_sem=self.recv.at[c, kind],
            device_id={"fsdp": self.sib}, device_id_type=MESH).wait_recv()

    def span(self, c, k=None):
        rows = 32 if PIECES[c][0] < 0 else 128
        if self.direct(c):
            return (0, None) if k is None else (k * (rows // 2), rows // 2)
        return (self.half * 64, 64) if k is None else (self.half * 64 + 32 * k, 32)

    def post(self, link, mark, copy):
        copy.start()
        rows, cols = copy.src_ref.shape[-2:]
        self.time += ISSUE
        self.free[link] = max(self.free[link], self.time) + rows * cols * 2e-3 / (SIBLING if link == "s" else LINK)
        self.due[mark] = self.free[link] + HOP

    def take(self, mark, copy):
        copy.wait_recv()
        self.time = max(self.time, self.due[mark]) + ISSUE

    def take_all(self, c, kinds, rows):
        self.landed(c, kinds[0], rows)
        self.time = max([self.time] + [self.due[c, kind] for kind in kinds]) + ISSUE

    def onward(self, c, kind, owner):
        if self.direct(c):
            self.post("s", (c, 5 + kind), self.copy(c, 5 + kind, owner, {"fsdp": self.sib}))
        else:
            self.post("z", (c, 8 + kind), self.copy(c, 8 + kind, owner, self.to_z, *self.span(c)))

    def s1(self, c):
        self.post("x", (c, 1), self.copy(c, 1, self.me, {"fsdp": self.x}, *self.span(c)))
        self.post("y", (c, 2), self.copy(c, 2, self.me, {"fsdp": self.y}, *self.span(c)))
        self.post("s", (c, 0), self.copy(c, 0, self.me, {"fsdp": self.sib}))
        self.begun = c + 1
        self.waiting.append((2, c))

    def s2(self, c):
        self.take((c, 1), self.copy(c, 1, self.x, {"fsdp": self.x}, *self.span(c)))
        self.post("y", (c, 3), self.copy(c, 3, self.x, {"fsdp": self.y}, *self.span(c, 0)))
        self.onward(c, 0, self.x)
        self.take((c, 2), self.copy(c, 2, self.y, {"fsdp": self.y}, *self.span(c)))
        self.post("x", (c, 4), self.copy(c, 4, self.y, {"fsdp": self.x}, *self.span(c, 1)))
        self.onward(c, 1, self.y)
        self.waiting.append((3, c))

    def s3(self, c):
        self.take_all(c, (3, 4), self.moved(c))
        self.onward(c, 2, self.d)
        self.waiting.append((5 if self.direct(c) else 4, c))

    def s4(self, c):
        self.take_all(c, (8, 9, 10), 192)
        for kind, owner in enumerate((self.x, self.y, self.d)):
            self.post("s", (c, 5 + kind), self.copy(c, 5 + kind, owner, {"fsdp": self.sib}))
        self.waiting.append((5, c))

    def moved(self, c):
        rows = 32 if PIECES[c][0] < 0 else 128
        return rows if self.direct(c) else rows // 2

    def s5(self, c):
        self.take_all(c, (0, 5, 6, 7), 128 if PIECES[c][0] < 0 else 512)
        self.whole.add(c)

    def ready(self, event):
        stage, c = event
        marks = {2: (1, 2), 3: (3, 4), 4: (8, 9, 10), 5: (0, 5, 6, 7)}[stage]
        return max(self.due[c, kind] for kind in marks)

    def feed(self):
        while self.begun < len(PIECES) and min(self.free["x"], self.free["y"]) - self.time < LEAD:
            self.s1(self.begun)

    def step(self, event):
        self.waiting.remove(event)
        stage, c = event
        (self.s2, self.s3, self.s4, self.s5)[stage - 2](c)

    def spend(self, time):
        self.time += time
        while True:
            self.feed()
            landed = [event for event in self.waiting if self.ready(event) <= self.time]
            if not landed:
                break
            self.step(min(landed, key=lambda event: (self.ready(event), event)))

    def need(self, c):
        while c not in self.whole:
            self.feed()
            self.step(min(self.waiting, key=lambda event: (self.ready(event), event)))

    def finish(self):
        for c in range(len(PIECES)):
            self.copy(c, 0, self.me, {"fsdp": self.sib}).wait_send()
            for kind in (1, 2):
                self.copy(c, kind, self.me, {"fsdp": self.x}, *self.span(c)).wait_send()
            for k in range(2):
                self.copy(c, 3 + k, self.x, {"fsdp": self.x}, *self.span(c, k)).wait_send()
            for kind in range(3):
                self.copy(c, 5 + kind, self.x, {"fsdp": self.sib}).wait_send()
                if not self.direct(c):
                    self.copy(c, 8 + kind, self.x, self.to_z, *self.span(c)).wait_send()


def forward_kernel(
    seg_in, freq_in, te_in, x_in, cot_hbm, mixing_hbm, cond_hbm, up_hbm, down_hbm,
    lse_out, scales_out, turn_out, feat_out, thirds_hbm, w_hbm, lt_hbm, dpre_hbm, qkv_hbm, mid_hbm, back_hbm, out_hbm,
    four, wide, condf, nrm, qkv, att, mid, te_at, act, cot, ltb, gbuf, eye, in_sem, w_sem, lt_sem, g_sem, o_sem, *shared,
):
    gat = Gatherer(shared)
    me = gat.me
    thirds, mats = gat.thirds, gat.mats

    def load(src, dst, n):
        return pltpu.make_async_copy(src, dst, in_sem.at[n])

    loads = [load(cond_hbm, condf, 0)]
    loads += [load(mixing_hbm.at[k], four.at[k], 1 + k) for k in range(4)]
    loads += [load(up_hbm, wide, 5), load(cot_hbm, cot, 6)]
    for copy in loads:
        copy.start()
    gat.enter()
    obuf = att
    loads[0].wait()
    for k in range(2):
        gat.cond[me, 32 * k:32 * k + 32] = condf[k].astype(BF)
    gat.s1(0)
    for k in range(4):
        loads[1 + k].wait()
        if k < 3:
            for h in range(2):
                thirds[k, h, me] = four[k, :, 512 * h:512 * h + 512].astype(BF)
            if k < 2:
                gat.s1(1 + k)
        else:
            mats[0, me] = four[k].astype(BF)
    later = [load(down_hbm.at[pl.ds(128 * i, 128)], four.at[i], 7 + i) for i in range(4)]
    for copy in later:
        copy.start()
    ids = seg_in[...].astype(F32)
    column = jnp.broadcast_to(ids, (128, 512)).T[:, :1]
    before = jnp.sum(jnp.where(ids < column, 1.0, 0.0), axis=1, keepdims=True)
    offset = lax.broadcasted_iota(jnp.int32, (512, 1), 0).astype(F32) - before
    angle = offset * freq_in[...]
    lanes = lax.broadcasted_iota(jnp.int32, (1, 128), 1)
    lane_in = lax.rem(lanes, 64)
    low_half = lane_in < 32
    turn_out[0] = jnp.cos(angle)
    turn_out[1] = jnp.where(low_half, -1.0, 1.0) * jnp.sin(angle)
    spot = lane_in.astype(F32)
    square = (lax.broadcasted_iota(jnp.int32, (256, 256), n) for n in range(2))
    eye[...] = jnp.where(next(square) == next(square), 1.0, 0.0).astype(BF)
    feat_out[0] = jnp.where(jnp.logical_and(lane_in < 4, spot != column), 1.0, 0.0).astype(BF)
    feat_out[1] = jnp.where(spot == column, -1e30, 0.0).astype(BF)
    te_column = jnp.broadcast_to(te_in[...].astype(F32), (128, 256)).T[:, :1]
    for f in range(8):
        te_at[f] = te_column[32 * f:32 * f + 32]
    loads[5].wait()
    for i in range(4):
        for f in range(8):
            mats[1 + i, me, :, 128 * f:128 * f + 128] = wide[:, 512 * f + 128 * i:512 * f + 128 * i + 128].astype(BF)
    for i in range(4):
        later[i].wait()
        mats[5 + i, me] = four[i].astype(BF)

    def save_w(m):
        if m < 3:
            return pltpu.make_async_copy(thirds.at[m], thirds_hbm.at[m], w_sem.at[m])
        return pltpu.make_async_copy(mats.at[0], w_hbm, w_sem.at[m])

    def save_lt(n, slot):
        return pltpu.make_async_copy(ltb.at[slot], lt_hbm.at[n], lt_sem.at[slot])

    def turn(block, b, slot):
        rows = slice(128 * b, 128 * b + 128) if isinstance(b, int) else pl.ds(pl.multiple_of(b * 128, 128), 128)
        turned = dot_nt(eye[...], block).astype(BF)
        for a in range(2):
            ltb[slot, a, rows] = turned[128 * a:128 * a + 128]

    def scale_of(k):
        total = jnp.zeros((32, 1024), F32)
        for f in range(8):
            total = total + te_at[f] * gat.cond[f, 32 * k:32 * k + 32].astype(F32)
        scales_out[k:k + 1] = 1.0 + jnp.sum(total, axis=0, keepdims=True)

    def norm_rows(source, scale):
        def block(b, carry):
            rows = pl.ds(pl.multiple_of(b * 64, 64), 64)
            values = source[rows].astype(F32)
            center = values - jnp.mean(values, axis=-1, keepdims=True)
            spread = jnp.mean(center * center, axis=-1, keepdims=True)
            nrm[rows] = (center * lax.rsqrt(spread + 1e-05) * scale).astype(BF)
            return carry

        lax.fori_loop(0, 8, block, 0, unroll=2)

    gat.need(0)
    scale_of(0)
    norm_rows(x_in, scales_out[0:1])
    gat.spend(1.2)

    def save_qkv(k):
        return pltpu.make_async_copy(qkv.at[k], qkv_hbm.at[k], o_sem.at[k])

    def project(k, half):
        at = slice(512 * half, 512 * half + 512)
        result = dot(nrm[...], thirds[k, half].reshape(1024, 512))
        if k == 0:
            for b in range(2):
                turn(nrm[:, 512 * half + 256 * b:512 * half + 256 * b + 256], 2 * half + b, 0)
        if k < 2:
            sides = []
            for n in range(4):
                part = result[:, 128 * n:128 * n + 128]
                other = jnp.where(low_half, pltpu.roll(part, 96, 1), pltpu.roll(part, 32, 1))
                sides.append(part * turn_out[0] + other * turn_out[1])
            result = jnp.concatenate(sides, axis=1)
        result = result.astype(BF)
        qkv[k, :, at] = result * jnp.asarray(0.125, BF) if k == 0 else result

    def attend(pair, carry):
        at = pl.ds(pl.multiple_of(pair * 128, 128), 128)
        q_pair, k_pair = qkv[0, :, at], qkv[1, :, at]
        v_turned = qkv[2, :, at].T
        heads = [lax.div(lanes, 64) == j for j in range(2)]
        raws = [dot_nt(jnp.where(mine, k_pair, feat_out[1]), jnp.where(mine, q_pair, feat_out[0])) for mine in heads]
        peaks = [jnp.max(raw, axis=0, keepdims=True) for raw in raws]
        grown = [jnp.exp(raw - peak) for raw, peak in zip(raws, peaks)]
        totals = [jnp.sum(value, axis=0, keepdims=True) for value in grown]
        sides = [dot(v_turned[64 * j:64 * j + 64], grown[j].astype(BF)) * (1.0 / totals[j]) for j in range(2)]
        sums = [peak + jnp.log(total) for peak, total in zip(peaks, totals)]
        lse_out[pair] = jnp.concatenate(sums, axis=0)
        block = jnp.concatenate(sides, axis=0).astype(BF)
        ltb[1, lax.rem(pair, 2), pl.ds(pl.multiple_of(lax.div(pair, 2) * 128, 128), 128)] = block
        att[:, at] = block.T
        return carry

    for half in range(2):
        for k in range(3):
            gat.need(1 + 3 * half + k)
            project(k, half)
            gat.spend(0.9)
        if half == 1:
            for k in range(3):
                save_w(k).start()
                save_qkv(k).start()
            save_lt(6, 0).start()
        for part in range(2):
            begin = 4 * half + 2 * part
            lax.fori_loop(begin, begin + 2, attend, 0)
            gat.spend(3.6)
    save_lt(5, 1).start()
    gat.need(COND_TWO)
    scale_of(1)
    gat.need(OUT_W)
    save_w(3).start()

    def join(b, carry):
        at = pl.ds(pl.multiple_of(b * 512, 512), 512)
        mid[:, at] = x_in[:, at].astype(F32) + dot(att[...], mats[0, :, :, at].reshape(1024, 512))
        return carry

    lax.fori_loop(0, 2, join, 0)
    gat.spend(1.8)
    save_mid = pltpu.make_async_copy(mid, mid_hbm, o_sem.at[3])
    save_mid.start()
    norm_rows(mid, scales_out[1:2])
    gat.spend(2.4)
    befores = {0: 6, 1: 5, 2: 4}

    def save_dpre(i):
        return pltpu.make_async_copy(gbuf.at[i], dpre_hbm.at[i], g_sem.at[i])

    for i in range(4):
        gat.need(UP_W + i)
        save_lt(befores[i % 3], i % 3).wait()

        def expand(b, carry):
            at = pl.ds(pl.multiple_of(b * 512, 512), 512)
            u = dot(nrm[...], mats[1 + i, :, :, at].reshape(1024, 512))
            root = 0.7978845608028654
            square = u * u
            bend = jnp.tanh(root * u * (1.0 + 0.044715 * square))
            side = 0.5 * (1.0 + bend)
            result = (u * side).astype(BF)
            act[i, :, at] = result
            for n in range(2):
                turn(result[:, 256 * n:256 * n + 256], 2 * b + n, i % 3)
                if i == 0:
                    turn(nrm[:, pl.ds(pl.multiple_of(b * 512 + n * 256, 256), 256)], 2 * b + n, 2)
            slope = side + 0.5 * u * (1.0 - bend * bend) * (root * (1.0 + 3.0 * 0.044715 * square))
            gbuf[i, :, at] = slope.astype(BF)
            return carry

        lax.fori_loop(0, 2, expand, 0)
        save_lt(i, i % 3).start()
        befores[i % 3] = i
        if i == 0:
            save_lt(4, 2).start()
        gat.spend(3.0)
    for i in range(4):
        gat.need(DOWN_W + i)
        if i == 0:
            loads[6].wait()

        def slopes(b, carry):
            at = pl.ds(pl.multiple_of(b * 512, 512), 512)
            d_act = dot_nt(cot[...], mats[5 + i, pl.ds(4 * b, 4)].reshape(512, 1024))
            gbuf[i, :, at] = (d_act * gbuf[i, :, at].astype(F32)).astype(BF)
            return carry

        lax.fori_loop(0, 2, slopes, 0)
        save_dpre(i).start()
        gat.spend(1.2)

    def shrink(b, carry):
        at = pl.ds(pl.multiple_of(b * 512, 512), 512)
        total = mid[:, at]
        for i in range(4):
            total = total + dot(act[i], mats[5 + i, :, :, at].reshape(1024, 512))
        obuf[:, at] = total.astype(BF)
        back = dot_nt(gbuf[0], mats[1, pl.ds(4 * b, 4)].reshape(512, 1024))
        for i in range(1, 4):
            back = back + dot_nt(gbuf[i], mats[1 + i, pl.ds(4 * b, 4)].reshape(512, 1024))
        four[:, :, at] = back.reshape(4, 128, 512)
        return carry

    lax.fori_loop(0, 2, shrink, 0)
    save_out = pltpu.make_async_copy(obuf, out_hbm, o_sem.at[4])
    save_out.start()
    save_back = pltpu.make_async_copy(four, back_hbm, o_sem.at[5])
    save_back.start()
    gat.finish()
    for m in range(4):
        save_w(m).wait()
    for k in range(3):
        save_qkv(k).wait()
        save_lt(befores[k], k).wait()
    save_mid.wait()
    for i in range(4):
        save_dpre(i).wait()
    save_out.wait()
    save_back.wait()


def forward(seg, te, x, cot, mixing_w, cond_w, up_w, down_w):
    vmem = pl.BlockSpec(memory_space=pltpu.VMEM)
    anyw = pl.BlockSpec(memory_space=pl.ANY)
    shape = jax.ShapeDtypeStruct
    freq = 10000.0 ** (-(np.arange(128) % 32) * 2.0 / HEAD_DIM)
    return pl.pallas_call(
        forward_kernel,
        out_shape=(
            shape((8, 2, 512), F32), shape((2, 1024), F32), shape((2, 512, 128), F32), shape((2, 512, 128), BF),
            shape((3, 2, 8, 128, 512), BF), shape((8, 128, 1024), BF), shape((7, 2, 512, 512), BF), shape((4, 512, 1024), BF),
            shape((3, 512, 1024), BF), shape((512, 1024), F32), shape((4, 128, 1024), F32), shape((512, 1024), BF)),
        in_specs=[vmem] * 4 + [anyw] * 5,
        out_specs=(vmem,) * 4 + (anyw,) * 8,
        scratch_shapes=[
            pltpu.VMEM((4, 128, 1024), F32),
            pltpu.VMEM((128, 4096), F32),
            pltpu.VMEM((2, 32, 1024), F32),
            pltpu.VMEM((512, 1024), BF),
            pltpu.VMEM((3, 512, 1024), BF),
            pltpu.VMEM((512, 1024), BF),
            pltpu.VMEM((512, 1024), F32),
            pltpu.VMEM((8, 32, 1), F32),
            pltpu.VMEM((4, 512, 1024), BF),
            pltpu.VMEM((512, 1024), BF),
            pltpu.VMEM((3, 2, 512, 512), BF),
            pltpu.VMEM((4, 512, 1024), BF),
            pltpu.VMEM((256, 256), BF),
            pltpu.SemaphoreType.DMA((11,)),
            pltpu.SemaphoreType.DMA((4,)),
            pltpu.SemaphoreType.DMA((3,)),
            pltpu.SemaphoreType.DMA((4,)),
            pltpu.SemaphoreType.DMA((6,)),
        ] + Gatherer.scratch(),
        compiler_params=pltpu.CompilerParams(collective_id=2, has_side_effects=True, vmem_limit_bytes=63 * 2**20),
    )(seg, jnp.asarray(freq[None], F32), te, x, cot, mixing_w, cond_w, up_w, down_w)


def norm_back(values, grads, scale):
    center = values - jnp.mean(values, axis=-1, keepdims=True)
    recip = lax.rsqrt(jnp.mean(center * center, axis=-1, keepdims=True) + 1e-05)
    unit = center * recip
    g = grads * scale
    back = recip * (g - jnp.mean(g, axis=-1, keepdims=True) - unit * jnp.mean(g * unit, axis=-1, keepdims=True))
    return back, grads * unit


def backward_kernel(
    turn_in, lse_in, scales_in, te_in, feat_in, thirds_hbm, w_hbm, lt_hbm, cot_hbm, dpre_hbm, qkv_hbm, mid_hbm, back_hbm, x_hbm,
    sums, in_grad,
    lt, rh, thirds, wout, qkv, mid, acc, dmid, datt, xin, dscale, obuf, te_at, load_sem, out_sem, *shared,
):
    red = Reducer(shared)
    core = red.core

    def load(src, dst, n):
        return pltpu.make_async_copy(src, dst, load_sem.at[n])

    load_lt = [load(lt_hbm.at[n], lt.at[n], n) for n in range(7)]
    load_cot = load(cot_hbm, rh.at[0], 7)
    load_mid = load(mid_hbm, mid, 8)
    load_back = load(back_hbm, acc, 9)
    load_w3 = load(w_hbm, wout, 10)
    load_qkv = load(qkv_hbm, qkv, 11)
    load_dpre = load(dpre_hbm, rh.at[pl.ds(1, 4)], 12)
    load_w = load(thirds_hbm, thirds, 13)
    load_x = load(x_hbm, xin, 14)
    for copy in (load_cot, load_lt[0], load_mid, load_back, load_w3):
        copy.start()
    later = (load_lt[1], load_qkv, load_lt[2], load_lt[3], load_lt[4], load_dpre, load_lt[5], load_w, load_lt[6], load_x)
    arrivals = {1: (load_lt[1], load_qkv), 2: (load_lt[2],), 3: (load_lt[3],), 4: (load_lt[4], load_dpre), 8: (load_lt[5],),
                9: (load_lt[6], load_w, load_x)}
    red.enter()

    def operands(g):
        left = jnp.where(g < 8, lax.div(g, 2), jnp.where(g < 16, 4, jnp.where(g < 18, 5, 6)))
        right = jnp.where(g < 8, 0, jnp.where(g < 16, 1 + lax.div(g - 8, 2), jnp.where(g < 18, 5, 6 + lax.div(g - 18, 2))))
        return left, rh[right, :, pl.ds(pl.multiple_of(lax.rem(g, 2) * 512, 512), 512)]

    def give(g):
        left, right = operands(g)
        red.away[lax.rem(g, SLOTS)] = dot(lt[left, 1 - core], right).astype(BF).reshape(4, 128, 512)
        red.part[lax.rem(g, PART_SLOTS)] = dot(lt[left, core], right).astype(BF).reshape(4, 128, 512)
        red.c_sib(g).start()

    def cond_part(parity):
        rows = []
        for chip in range(4):
            column = te_at[2 * chip + parity]
            rows.append(jnp.concatenate([column * dscale[k:k + 1, 512 * h:512 * h + 512] for k in range(2) for h in range(2)], axis=0)[None])
        return jnp.concatenate(rows, axis=0)

    def put(g, value):
        sums[g] = value

    te_column = jnp.broadcast_to(te_in[...].astype(F32), (128, 256)).T[:, :1]
    for f in range(8):
        te_at[f] = te_column[32 * f:32 * f + 32]
    lanes = lax.broadcasted_iota(jnp.int32, (1, 128), 1)
    low_half = lax.rem(lanes, 64) < 32

    def unrotate(block):
        other = jnp.where(low_half, pltpu.roll(block, 96, 1), pltpu.roll(block, 32, 1))
        return block * turn_in[0] - other * turn_in[1]

    def middle_back():
        for copy in later:
            copy.start()
        load_mid.wait()
        load_back.wait()

        def norm_two(b, total):
            rows = pl.ds(pl.multiple_of(b * 64, 64), 64)
            back, terms = norm_back(mid[rows], acc[rows], scales_in[1:2])
            back = back + rh[0, rows].astype(F32)
            dmid[rows] = back
            rh[5, rows] = back.astype(BF)
            return total + jnp.sum(terms.reshape(8, 8, 1024), axis=0)

        total = lax.fori_loop(0, 8, norm_two, jnp.zeros((8, 1024), F32), unroll=2)
        dscale[1:2] = jnp.sum(total, axis=0, keepdims=True)
        load_w3.wait()
        for n in range(2):
            cols = slice(512 * n, 512 * n + 512)
            datt[:, cols] = dot_nt(rh[5], wout[cols, :]).astype(BF)

    def attend_back(pair):
        at = pl.ds(pl.multiple_of(pair * 128, 128), 128)
        q_pair, k_pair, v_pair, d_pair = qkv[0, :, at], qkv[1, :, at], qkv[2, :, at], datt[:, at]
        k_turned = (k_pair * jnp.asarray(0.125, BF)).T
        heads = [lax.div(lanes, 64) == j for j in range(2)]
        raws = [dot_nt(jnp.where(mine, k_pair, feat_in[1]), jnp.where(mine, q_pair, feat_in[0])) for mine in heads]
        d_probs = [dot_nt(v_pair, jnp.where(mine, d_pair, jnp.zeros_like(d_pair))) for mine in heads]
        made = []
        for j in range(2):
            probs = jnp.exp(raws[j] - lse_in[pair, j:j + 1])
            delta = jnp.sum(probs * d_probs[j], axis=0, keepdims=True)
            d_raw = (probs * (d_probs[j] - delta)).astype(BF)
            made.append((dot(k_turned[64 * j:64 * j + 64], d_raw), dot(d_raw, q_pair), dot(probs.astype(BF), d_pair)))
        rh[6, :, at] = unrotate(jnp.concatenate([made[0][0], made[1][0]], axis=0).T).astype(BF)
        rh[7, :, at] = unrotate(jnp.where(heads[0], made[0][1], made[1][1])).astype(BF)
        rh[8, :, at] = jnp.where(heads[0], made[0][2], made[1][2]).astype(BF)

    def first_back(k):
        for h in range(2):
            cols = slice(512 * h, 512 * h + 512)
            part = dot_nt(rh[6 + k, :, :512], thirds[k, 0, cols]) + dot_nt(rh[6 + k, :, 512:], thirds[k, 1, cols])

            @pl.when(k == 0)
            def _():
                acc[:, cols] = part

            @pl.when(k > 0)
            def _():
                acc[:, cols] += part

    def input_back():
        def norm_one(b, total):
            rows = pl.ds(pl.multiple_of(b * 64, 64), 64)
            back, terms = norm_back(xin[rows].astype(F32), acc[rows], scales_in[0:1])
            obuf[rows] = (dmid[rows] + back).astype(BF)
            return total + jnp.sum(terms.reshape(8, 8, 1024), axis=0)

        total = lax.fori_loop(0, 8, norm_one, jnp.zeros((8, 1024), F32), unroll=2)
        dscale[0:1] = jnp.sum(total, axis=0, keepdims=True)
        store_out.start()
        red.away[(CHUNKS - 1) % SLOTS] = cond_part(1 - core).astype(BF)
        red.part[(CHUNKS - 1) % PART_SLOTS] = cond_part(core).astype(BF)
        red.c_sib(jnp.int32(CHUNKS - 1)).start()

    store_out = pltpu.make_async_copy(obuf, in_grad, out_sem)
    load_cot.wait()
    load_lt[0].wait()

    def turn(m, carry):
        for when, copies in arrivals.items():
            @pl.when(m == when)
            def _(copies=copies):
                for copy in copies:
                    copy.wait()

        @pl.when(m < 12)
        def _():
            give(2 * m)
            give(2 * m + 1)

        pl.when(jnp.logical_and(m >= 1, m < 9))(lambda: attend_back(m - 1))

        pl.when(jnp.logical_and(m >= 9, m < 12))(lambda: first_back(m - 9))
        pl.when(m == 12)(input_back)
        def ticks(t, carry):
            red.tick(t, put)
            return carry

        lax.fori_loop(2 * m, 2 * m + 2, ticks, 0)
        pl.when(m == 0)(middle_back)

        return carry

    lax.fori_loop(0, (CHUNKS + LAGS[-1] + 1) // 2, turn, 0)
    store_out.wait()


def backward(turn, lse, scales, te, feat, thirds, w, lt, cot, dpre, qkv, mid, back, x):
    vmem = pl.BlockSpec(memory_space=pltpu.VMEM)
    anyw = pl.BlockSpec(memory_space=pl.ANY)
    shape = jax.ShapeDtypeStruct
    return pl.pallas_call(
        backward_kernel,
        out_shape=(
            shape((CHUNKS, 128, 512), BF), shape((512, 1024), BF)),
        in_specs=[vmem] * 5 + [anyw] * 9,
        out_specs=(vmem, anyw),
        scratch_shapes=[
            pltpu.VMEM((7, 2, 512, 512), BF),
            pltpu.VMEM((9, 512, 1024), BF),
            pltpu.VMEM((3, 2, 1024, 512), BF),
            pltpu.VMEM((1024, 1024), BF),
            pltpu.VMEM((3, 512, 1024), BF),
            pltpu.VMEM((512, 1024), F32),
            pltpu.VMEM((512, 1024), F32),
            pltpu.VMEM((512, 1024), F32),
            pltpu.VMEM((512, 1024), BF),
            pltpu.VMEM((512, 1024), BF),
            pltpu.VMEM((2, 1024), F32),
            pltpu.VMEM((512, 1024), BF),
            pltpu.VMEM((8, 32, 1), F32),
            pltpu.SemaphoreType.DMA((16,)),
            pltpu.SemaphoreType.DMA,
        ] + Reducer.scratch(),
        compiler_params=pltpu.CompilerParams(collective_id=1, has_side_effects=True, vmem_limit_bytes=63 * 2**20),
    )(turn, lse, scales, te, feat, thirds.reshape(3, 2, 1024, 512), w.reshape(1024, 1024), lt, cot, dpre, qkv, mid, back.reshape(512, 1024), x)


def update_kernel(*refs):
    sums, states, rows, outs, rows_out = refs[0], refs[1:17], refs[17:19], refs[19:39], refs[39:41]
    fresh, held, made, passed, in_sem, out_sem, pass_sem = refs[41:]
    mix, cond, up, down = range(4)
    units = [(kind, i) for kind in (down, up, mix) for i in range(4)] + [(cond, 0)]
    keep_one = 1.0 / (1.0 - 0.5**STEP)

    def piece(ref, kind, i):
        if kind == up:
            return ref.at[:, pl.ds(1024 * i, 1024)]
        if kind == cond:
            return ref
        return ref.at[i] if len(ref.shape) == 3 else ref.at[pl.ds(128 * i, 128)]

    def summed(kind, i, buffer):
        if kind == cond:
            return [(sums.at[24, pl.ds(64 * k + 32 * h, 32)], buffer.at[pl.ds(32 * k, 32), pl.ds(512 * h, 512)])
                    for k in range(2) for h in range(2)]
        if kind == up:
            half, first = i // 2, 2 * (i % 2)
            return [(sums.at[8 + 2 * n + half, :, pl.ds(128 * (first + a), 128)], buffer.at[:, pl.ds(512 * a + 128 * n, 128)])
                    for n in range(4) for a in range(2)]
        chunk = 2 * i if kind == down else 16 + 2 * ((i + 1) % 4)
        return [(sums.at[chunk + h], buffer.at[:, pl.ds(512 * h, 512)]) for h in range(2)]

    def loads(u):
        kind, i = units[u]
        s = u % RING
        copies = [(a, b, in_sem.at[s, 8 + n]) for n, (a, b) in enumerate(summed(kind, i, fresh.at[s]))]
        for n, ref in enumerate(states[4 * kind:4 * kind + 4]):
            if kind == cond:
                for k in range(2):
                    copies.append((ref.at[k], held.at[s, n, pl.ds(32 * k, 32)], in_sem.at[s, 4 * k + n]))
            else:
                copies.append((piece(ref, kind, i), held.at[s, n], in_sem.at[s, n]))
        return [pltpu.make_async_copy(*c) for c in copies]

    def saves(u):
        kind, i = units[u]
        s = u % RING
        copies = []
        for n in range(5):
            ref, buffer = outs[5 * kind + n], made.at[s, n]
            if kind == cond:
                for k in range(2):
                    copies.append((buffer.at[pl.ds(32 * k, 32)], ref.at[k], out_sem.at[s, 5 * k + n]))
            else:
                copies.append((buffer, piece(ref, kind, i), out_sem.at[s, n]))
        return [pltpu.make_async_copy(*c) for c in copies]

    enter = [pltpu.make_async_copy(rows[n], passed.at[n], pass_sem.at[n]) for n in range(2)]
    leave = [pltpu.make_async_copy(passed.at[n], rows_out[n].at[0], pass_sem.at[n]) for n in range(2)]
    for u in range(RING - 1):
        for copy in loads(u):
            copy.start()
    for copy in enter:
        copy.start()
    for u in range(len(units)):
        s = u % RING
        if u == 2:
            for n in range(2):
                enter[n].wait()
                leave[n].start()
        if u + RING - 1 < len(units):
            for copy in loads(u + RING - 1):
                copy.start()
        if u >= RING:
            for copy in saves(u - RING):
                copy.wait()
        for copy in loads(u):
            copy.wait()

        def rows_step(b, carry):
            rows = pl.ds(pl.multiple_of(b * 16, 16), 16)
            g = fresh[s, rows].astype(F32)
            w = held[s, 0, rows]
            m = 0.5 * held[s, 1, rows] + 0.5 * g
            v = 0.5 * held[s, 2, rows] + 0.5 * g * g
            w_new = w - 0.01 * (m * keep_one / (jnp.sqrt(v * keep_one) + 1e-08) + 0.1 * w)
            made[s, 0, rows] = g
            made[s, 1, rows] = m
            made[s, 2, rows] = v
            made[s, 3, rows] = w_new
            made[s, 4, rows] = 0.8 * held[s, 3, rows] + 0.2 * w_new
            return carry

        lax.fori_loop(0, 4 if units[u][0] == cond else 8, rows_step, 0)
        for copy in saves(u):
            copy.start()
    for u in range(len(units) - RING, len(units)):
        for copy in saves(u):
            copy.wait()
    for copy in leave:
        copy.wait()


RING = 4


def update(sums, states, rows):
    anyw = pl.BlockSpec(memory_space=pl.ANY)
    outs = []
    for n in range(4):
        outs += [jax.ShapeDtypeStruct(states[4 * n].shape, F32)] * 5
    outs += [jax.ShapeDtypeStruct((1, 512, 1024), BF)] * 2
    *made, output, input_grad = pl.pallas_call(
        update_kernel,
        out_shape=tuple(outs),
        in_specs=[anyw] * 19,
        out_specs=(anyw,) * 22,
        scratch_shapes=[
            pltpu.VMEM((RING, 128, 1024), BF),
            pltpu.VMEM((RING, 4, 128, 1024), F32),
            pltpu.VMEM((RING, 5, 128, 1024), F32),
            pltpu.VMEM((2, 512, 1024), BF),
            pltpu.SemaphoreType.DMA((RING, 16)),
            pltpu.SemaphoreType.DMA((RING, 10)),
            pltpu.SemaphoreType.DMA((2,)),
        ],
        compiler_params=pltpu.CompilerParams(vmem_limit_bytes=63 * 2**20),
    )(sums, *states, *rows)
    return (output, input_grad, *made)


def normed(values):
    center = values - jnp.mean(values, axis=-1, keepdims=True)
    spread = jnp.mean(center * center, axis=-1, keepdims=True)
    return center * lax.rsqrt(spread + 1e-05)


def scaled_norm(values, gain):
    return normed(values) * gain[None, :]


def rotary_tables(segments):
    length = segments.shape[0]
    position = jnp.arange(length, dtype=jnp.int32)
    is_start = jnp.concatenate([jnp.ones((1,), dtype=bool), segments[1:] != segments[:-1]])
    seg_start = lax.cummax(jnp.where(is_start, position, jnp.zeros_like(position)), axis=0)
    offset = (position - seg_start).astype(jnp.float32)
    frequency = 10000.0 ** (-jnp.arange(HEAD_DIM // 2, dtype=jnp.float32) * 2.0 / HEAD_DIM)
    turned = offset[:, None] * frequency[None, :]
    return (jnp.cos(turned)[:, None, :], jnp.sin(turned)[:, None, :])


def rotate(parts, cos_table, sin_table):
    half_dim = parts.shape[-1] // 2
    part_a = parts[..., :half_dim]
    part_b = parts[..., half_dim:]
    return jnp.concatenate(
        [part_a * cos_table - part_b * sin_table, part_b * cos_table + part_a * sin_table], axis=-1
    )


def unrotate(grads, cos_table, sin_table):
    half_dim = grads.shape[-1] // 2
    grad_a = grads[..., :half_dim]
    grad_b = grads[..., half_dim:]
    return jnp.concatenate(
        [grad_a * cos_table + grad_b * sin_table, grad_b * cos_table - grad_a * sin_table], axis=-1
    )


def adam_update(gradient, weight, moment_one, moment_two, average):
    moment_one_new = 0.5 * moment_one + 0.5 * gradient
    moment_two_new = 0.5 * moment_two + 0.5 * gradient * gradient
    correction = 1.0 - 0.5**STEP
    update = (
        moment_one_new / correction / (jnp.sqrt(moment_two_new / correction) + 1e-08) + 0.1 * weight
    )
    weight_new = weight - 0.01 * update
    average_new = 0.8 * average + 0.2 * weight_new
    return (moment_one_new, moment_two_new, weight_new, average_new)


def local(
    tokens,
    time_embed,
    segment_ids,
    cotangent,
    mixing_w,
    mixing_m,
    mixing_v,
    mixing_avg,
    cond_w,
    cond_m,
    cond_v,
    cond_avg,
    up_w,
    up_m,
    up_v,
    up_avg,
    down_w,
    down_m,
    down_v,
    down_avg,
):
    rows_in = tokens[0].astype(jnp.float32)
    embedding = time_embed[0]
    segments = segment_ids[0]
    length = rows_in.shape[0]
    block_rows = min(512, length)
    block_count = length // block_rows
    mixing_g, cond_g = (
        lax.all_gather(mixing_w.astype(jnp.bfloat16), "fsdp", axis=1, tiled=True),
        lax.all_gather(cond_w.astype(jnp.bfloat16), "fsdp", axis=1, tiled=True),
    )
    up_g, down_g = (
        lax.all_gather(up_w.astype(jnp.bfloat16), "fsdp", axis=0, tiled=True),
        lax.all_gather(down_w.astype(jnp.bfloat16), "fsdp", axis=0, tiled=True),
    )
    scales = 1.0 + jnp.einsum("e,ked->kd", embedding, cond_g, preferred_element_type=jnp.float32)
    cos_table, sin_table = rotary_tables(segments)
    normed_one = (normed(rows_in) * scales[0][None, :]).astype(jnp.bfloat16)
    projected = jnp.einsum(
        "td,kde->kte", normed_one, mixing_g[:3], preferred_element_type=jnp.float32
    )
    queries = rotate(projected[0].reshape(length, HEADS, HEAD_DIM), cos_table, sin_table).astype(
        jnp.bfloat16
    )
    keys_rot = rotate(projected[1].reshape(length, HEADS, HEAD_DIM), cos_table, sin_table).astype(
        jnp.bfloat16
    )
    values_b = projected[2].astype(jnp.bfloat16).reshape(length, HEADS, HEAD_DIM)
    query_blocks = queries.reshape(block_count, block_rows, HEADS, HEAD_DIM)
    seg_blocks = segments.reshape(block_count, block_rows)

    def block_scores(q_block, seg_block):
        raw = (
            jnp.einsum("qhd,khd->hqk", q_block, keys_rot, preferred_element_type=jnp.float32)
            * 0.125
        )
        same_seg = seg_block[:, None] == segments[None, :]
        return jnp.where(same_seg[None], raw, -1e30)

    def attend_block(element):
        q_block, seg_block = element
        raw = block_scores(q_block, seg_block)
        peak = jnp.max(raw, axis=-1, keepdims=True)
        exp_scores = jnp.exp(raw - peak)
        totals = jnp.sum(exp_scores, axis=-1, keepdims=True)
        probs = (exp_scores / totals).astype(jnp.bfloat16)
        out_block = jnp.einsum(
            "hqk,khd->qhd", probs, values_b, preferred_element_type=jnp.float32
        ).astype(jnp.bfloat16)
        return (out_block, peak[..., 0] + jnp.log(totals[..., 0]))

    attended, log_totals = lax.map(attend_block, (query_blocks, seg_blocks))
    attended = attended.reshape(length, D)
    middle = rows_in + jnp.dot(attended, mixing_g[3], preferred_element_type=jnp.float32)
    normed_two = (normed(middle) * scales[1][None, :]).astype(jnp.bfloat16)
    hidden_pre = jnp.dot(normed_two, up_g, preferred_element_type=jnp.float32)
    hidden_act = jax.nn.gelu(hidden_pre).astype(jnp.bfloat16)
    output = (middle + jnp.dot(hidden_act, down_g, preferred_element_type=jnp.float32)).astype(
        jnp.bfloat16
    )
    mixing_b, cond_b = (
        lax.all_gather(mixing_w.astype(jnp.bfloat16), "fsdp", axis=1, tiled=True),
        lax.all_gather(cond_w.astype(jnp.bfloat16), "fsdp", axis=1, tiled=True),
    )
    up_b, down_b = (
        lax.all_gather(up_w.astype(jnp.bfloat16), "fsdp", axis=0, tiled=True),
        lax.all_gather(down_w.astype(jnp.bfloat16), "fsdp", axis=0, tiled=True),
    )
    back_out = cotangent[0]
    d_act = jnp.einsum("td,fd->tf", back_out, down_b, preferred_element_type=jnp.float32)
    d_down = jnp.einsum("tf,td->fd", hidden_act, back_out, preferred_element_type=jnp.float32)
    _, gelu_pull = jax.vjp(jax.nn.gelu, hidden_pre)
    d_pre = gelu_pull(d_act)[0].astype(jnp.bfloat16)
    d_up = jnp.einsum("td,tf->df", normed_two, d_pre, preferred_element_type=jnp.float32)
    d_normed_two = jnp.einsum("tf,df->td", d_pre, up_b, preferred_element_type=jnp.float32)
    _, norm_pull_two = jax.vjp(scaled_norm, middle, scales[1])
    d_middle, d_scale_two = norm_pull_two(d_normed_two)
    d_middle = d_middle + back_out.astype(jnp.float32)
    d_middle_b = d_middle.astype(jnp.bfloat16)
    d_out_proj = jnp.einsum("td,te->de", attended, d_middle_b, preferred_element_type=jnp.float32)
    d_attended = jnp.einsum(
        "te,de->td", d_middle_b, mixing_b[3], preferred_element_type=jnp.float32
    ).astype(jnp.bfloat16)
    d_att_blocks = d_attended.reshape(block_count, block_rows, HEADS, HEAD_DIM)

    def back_block(state_in, element):
        q_block, seg_block, d_block, log_block = element
        raw = block_scores(q_block, seg_block)
        probs_f = jnp.exp(raw - log_block[..., None])
        probs_b = probs_f.astype(jnp.bfloat16)
        d_probs = jnp.einsum("qhd,khd->hqk", d_block, values_b, preferred_element_type=jnp.float32)
        d_raw = (probs_f * (d_probs - jnp.sum(probs_f * d_probs, axis=-1, keepdims=True))).astype(
            jnp.bfloat16
        )
        d_query = (
            jnp.einsum("hqk,khd->qhd", d_raw, keys_rot, preferred_element_type=jnp.float32) * 0.125
        )
        keys_acc = (
            state_in[0]
            + jnp.einsum("hqk,qhd->khd", d_raw, q_block, preferred_element_type=jnp.float32) * 0.125
        )
        values_acc = state_in[1] + jnp.einsum(
            "hqk,qhd->khd", probs_b, d_block, preferred_element_type=jnp.float32
        )
        return ((keys_acc, values_acc), d_query)

    zero_heads = jnp.zeros((length, HEADS, HEAD_DIM), jnp.float32)
    (d_keys, d_values), d_queries = lax.scan(
        back_block, (zero_heads, zero_heads), (query_blocks, seg_blocks, d_att_blocks, log_totals)
    )
    d_queries = unrotate(d_queries.reshape(length, HEADS, HEAD_DIM), cos_table, sin_table)
    d_keys = unrotate(d_keys, cos_table, sin_table)
    d_projected = (
        jnp.stack([d_queries, d_keys, d_values]).reshape(3, length, D).astype(jnp.bfloat16)
    )
    d_qkv = jnp.einsum("td,kte->kde", normed_one, d_projected, preferred_element_type=jnp.float32)
    d_normed_one = jnp.einsum(
        "kte,kde->td", d_projected, mixing_b[:3], preferred_element_type=jnp.float32
    )
    _, norm_pull_one = jax.vjp(scaled_norm, rows_in, scales[0])
    d_rows, d_scale_one = norm_pull_one(d_normed_one)
    input_grad = (d_middle + d_rows).astype(jnp.bfloat16)
    d_scales = jnp.stack([d_scale_one, d_scale_two])
    d_cond = embedding.astype(jnp.float32)[None, :, None] * d_scales[:, None, :]
    d_mixing = jnp.concatenate([d_qkv, d_out_proj[None]], axis=0)
    mixing_part, cond_part = (
        lax.psum_scatter(d_mixing, "fsdp", scatter_dimension=1, tiled=True),
        lax.psum_scatter(d_cond, "fsdp", scatter_dimension=1, tiled=True),
    )
    up_part, down_part = (
        lax.psum_scatter(d_up, "fsdp", scatter_dimension=0, tiled=True),
        lax.psum_scatter(d_down, "fsdp", scatter_dimension=0, tiled=True),
    )
    mixing_grad, cond_grad, up_grad, down_grad = (
        lax.psum(mixing_part.astype(jnp.bfloat16), "rows").astype(jnp.float32),
        lax.psum(cond_part.astype(jnp.bfloat16), "rows").astype(jnp.float32),
        lax.psum(up_part.astype(jnp.bfloat16), "rows").astype(jnp.float32),
        lax.psum(down_part.astype(jnp.bfloat16), "rows").astype(jnp.float32),
    )
    mix_one, mix_two, mix_new, mix_average = adam_update(
        mixing_grad, mixing_w, mixing_m, mixing_v, mixing_avg
    )
    cond_one, cond_two, cond_new, cond_average = adam_update(
        cond_grad, cond_w, cond_m, cond_v, cond_avg
    )
    up_one, up_two, up_new, up_average = adam_update(up_grad, up_w, up_m, up_v, up_avg)
    down_one, down_two, down_new, down_average = adam_update(
        down_grad, down_w, down_m, down_v, down_avg
    )
    return (
        output[None],
        input_grad[None],
        mixing_grad,
        mix_one,
        mix_two,
        mix_new,
        mix_average,
        cond_grad,
        cond_one,
        cond_two,
        cond_new,
        cond_average,
        up_grad,
        up_one,
        up_two,
        up_new,
        up_average,
        down_grad,
        down_one,
        down_two,
        down_new,
        down_average,
    )


def local_small(
    tokens, time_embed, segment_ids, cotangent,
    mixing_w, mixing_m, mixing_v, mixing_avg,
    cond_w, cond_m, cond_v, cond_avg,
    up_w, up_m, up_v, up_avg,
    down_w, down_m, down_v, down_avg,
):
    x, cot = tokens[0], cotangent[0]
    lse, scales, turn, feat, thirds, w, lt, dpre, qkv, middle, back, output = forward(
        segment_ids, time_embed, x, cot, mixing_w, cond_w, up_w, down_w)
    sums, input_grad = backward(turn, lse, scales, time_embed, feat, thirds, w, lt, cot, dpre, qkv, middle, back, x)
    states = (
        mixing_w, mixing_m, mixing_v, mixing_avg, cond_w, cond_m, cond_v, cond_avg,
        up_w, up_m, up_v, up_avg, down_w, down_m, down_v, down_avg)
    return update(sums, states, (output, input_grad))


def solution(mesh):
    small = mesh.shape["rows"] == 4 and mesh.shape["fsdp"] == 8
    placed = (
        P(("rows", "fsdp"), None, None),
        P(("rows", "fsdp"), None),
        P(("rows", "fsdp"), None),
        P(("rows", "fsdp"), None, None),
        P(None, "fsdp", None),
        P(None, "fsdp", None),
        P(None, "fsdp", None),
        P(None, "fsdp", None),
        P(None, "fsdp", None),
        P(None, "fsdp", None),
        P(None, "fsdp", None),
        P(None, "fsdp", None),
        P("fsdp", None),
        P("fsdp", None),
        P("fsdp", None),
        P("fsdp", None),
        P("fsdp", None),
        P("fsdp", None),
        P("fsdp", None),
        P("fsdp", None),
    )
    return jax.shard_map(
        local_small if small else local,
        mesh=mesh,
        in_specs=placed,
        out_specs=(
            P(("rows", "fsdp"), None, None),
            P(("rows", "fsdp"), None, None),
            P(None, "fsdp", None),
            P(None, "fsdp", None),
            P(None, "fsdp", None),
            P(None, "fsdp", None),
            P(None, "fsdp", None),
            P(None, "fsdp", None),
            P(None, "fsdp", None),
            P(None, "fsdp", None),
            P(None, "fsdp", None),
            P(None, "fsdp", None),
            P("fsdp", None),
            P("fsdp", None),
            P("fsdp", None),
            P("fsdp", None),
            P("fsdp", None),
            P("fsdp", None),
            P("fsdp", None),
            P("fsdp", None),
            P("fsdp", None),
            P("fsdp", None),
        ),
        check_vma=False,
    )
```

```python
import jax
import jax.numpy as jnp
import numpy as np
from jax import lax
from jax.experimental import pallas as pl
from jax.experimental.pallas import tpu as pltpu
from jax.sharding import PartitionSpec as P

D = 1024
HEADS = 16
HEAD_DIM = 64
STEP = 7
F32 = jnp.float32
BF = jnp.bfloat16


MESH = pl.DeviceIdType.MESH
CHUNKS = 25
SLOTS = 4
SIB_SLOTS = 6
LINE_SLOTS = 6
PART_SLOTS = 10
LAGS = (1, 3, 5, 7, 9, 11, 13)


class Reducer:
    def __init__(self, refs):
        (self.away, self.part, self.sib, self.swap, self.diag, self.near, self.zin, self.zmid, self.tsum, self.out_a, self.out_b,
         self.sems_sib, self.sems_swap, self.sems_diag, self.sems_near, self.sems_zin, self.sems_zmid) = refs
        self.me = lax.axis_index("fsdp")
        self.core = lax.rem(self.me, 2)
        self.chip = lax.div(self.me, 2)
        self.row = lax.axis_index("rows")
        self.inner = jnp.logical_and(self.row >= 1, self.row <= 2)
        self.outer = jnp.logical_not(self.inner)
        self.line_to = jnp.where(self.row == 0, 1, jnp.where(self.row == 1, 0, jnp.where(self.row == 2, 3, 2)))
        self.mid_to = jnp.where(self.row == 1, 2, 1)
        xbit = lax.rem(self.chip, 2)
        ybit = lax.div(self.chip, 2)
        self.chip_x = ybit * 2 + (1 - xbit)
        self.chip_y = (1 - ybit) * 2 + xbit
        self.chip_d = (1 - ybit) * 2 + (1 - xbit)
        self.mine = pl.multiple_of(lax.rem(self.row, 2) * 64, 64)
        self.to_sib = {"fsdp": self.chip * 2 + (1 - self.core)}
        self.to_x = {"fsdp": self.chip_x * 2 + self.core}
        self.to_y = {"fsdp": self.chip_y * 2 + self.core}

    @staticmethod
    def scratch():
        s = SLOTS
        bf = jnp.bfloat16
        dma = pltpu.SemaphoreType.DMA
        return [
            pltpu.VMEM((SLOTS, 4, 128, 512), bf),
            pltpu.VMEM((PART_SLOTS, 4, 128, 512), bf),
            pltpu.VMEM((SIB_SLOTS, 4, 128, 512), bf),
            pltpu.VMEM((LINE_SLOTS, 64, 512), bf),
            pltpu.VMEM((s, 128, 512), bf),
            pltpu.VMEM((s, 2, 128, 512), bf),
            pltpu.VMEM((LINE_SLOTS, 128, 512), bf),
            pltpu.VMEM((LINE_SLOTS, 128, 512), bf),
            pltpu.VMEM((LINE_SLOTS, 128, 512), jnp.float32),
            pltpu.VMEM((LINE_SLOTS, 128, 512), bf),
            pltpu.VMEM((LINE_SLOTS, 128, 512), bf),
            dma((2, SIB_SLOTS)),
            dma((2, LINE_SLOTS)),
            dma((2, s)),
            dma((2, s)),
            dma((2, LINE_SLOTS)),
            dma((2, LINE_SLOTS)),
        ]

    def enter(self):
        barrier = pltpu.get_barrier_semaphore()
        for to in (self.to_sib, self.to_x, self.to_y, {"rows": self.line_to}):
            pl.semaphore_signal(barrier, inc=1, device_id=to, device_id_type=MESH)

        @pl.when(self.inner)
        def _():
            pl.semaphore_signal(barrier, inc=1, device_id={"rows": self.mid_to}, device_id_type=MESH)
            pl.semaphore_wait(barrier, 5)

        @pl.when(self.outer)
        def _():
            pl.semaphore_wait(barrier, 4)

    def copy(self, src, dst, sems, which, slot, to):
        return pltpu.make_async_remote_copy(
            src_ref=src, dst_ref=dst, send_sem=sems.at[which, slot], recv_sem=sems.at[which + sems.shape[0] // 2, slot],
            device_id=to, device_id_type=MESH)

    def c_sib(self, g):
        n = lax.rem(g, SIB_SLOTS)
        return self.copy(self.away.at[lax.rem(g, SLOTS)], self.sib.at[n], self.sems_sib, 0, n, self.to_sib)

    def shared(self, g):
        return jnp.logical_and(lax.rem(g, 3) != 2, g < CHUNKS - 2)

    def by_kind(self, g, stage):
        pl.when(self.shared(g))(lambda: stage(g, self.mine, 32))
        pl.when(jnp.logical_not(self.shared(g)))(lambda: stage(g, 0, 64))

    def c_swap(self, g):
        s = lax.rem(g, LINE_SLOTS)
        theirs = pl.ds(pl.multiple_of(64 - self.mine, 64), 64)
        return self.copy(self.part.at[lax.rem(g, PART_SLOTS), self.chip_d, theirs], self.swap.at[s], self.sems_swap, 0, s, {"rows": self.line_to})

    def c_diag(self, g, k, first, size):
        s, to, rows = lax.rem(g, SLOTS), (self.to_x if k == 0 else self.to_y), pl.ds(first + size * k, size)
        return self.copy(self.part.at[lax.rem(g, PART_SLOTS), self.chip_d, rows], self.diag.at[s, rows], self.sems_diag, 0, s, to)

    def c_near(self, g, k):
        s, (to, chip) = lax.rem(g, SLOTS), ((self.to_x, self.chip_x) if k == 0 else (self.to_y, self.chip_y))
        return self.copy(self.part.at[lax.rem(g, PART_SLOTS), chip], self.near.at[s, k], self.sems_near, 0, s, to)

    def both_diag(self, g, first, size):
        s, rows = lax.rem(g, SLOTS), pl.ds(first, 2 * size)
        return self.copy(self.part.at[lax.rem(g, PART_SLOTS), self.chip_d, rows], self.diag.at[s, rows], self.sems_diag, 0, s, self.to_x)

    def both_near(self, g):
        s = lax.rem(g, SLOTS)
        return self.copy(self.part.at[lax.rem(g, PART_SLOTS), pl.ds(0, 2)], self.near.at[s], self.sems_near, 0, s, self.to_x)

    def c_line(self, s):
        return self.copy(self.out_a.at[s], self.zin.at[s], self.sems_zin, 0, s, {"rows": self.line_to})

    def c_mid(self, s):
        return self.copy(self.out_b.at[s], self.zmid.at[s], self.sems_zmid, 0, s, {"rows": self.mid_to})

    def stage_b(self, g):
        p, n = lax.rem(g, PART_SLOTS), lax.rem(g, SIB_SLOTS)
        self.c_sib(g).wait()
        self.part[p] = (self.part[p].astype(jnp.float32) + self.sib[n].astype(jnp.float32)).astype(jnp.bfloat16)
        pl.when(self.shared(g))(lambda: self.c_swap(g).start())

    def add(self, g, chip, first, size, more):
        p, rows = lax.rem(g, PART_SLOTS), pl.ds(first, size)
        total = self.part[p, chip, rows].astype(jnp.float32) + more.astype(jnp.float32)
        self.part[p, chip, rows] = total.astype(jnp.bfloat16)

    def stage_d(self, g, first, size):
        if size == 32:
            self.c_swap(g).wait()
            self.add(g, self.chip_d, first, 64, self.swap[lax.rem(g, LINE_SLOTS)])
        self.c_diag(g, 0, first, size).start()
        self.c_diag(g, 1, first, size).start()

    def stage_c(self, g, first, size):
        s = lax.rem(g, SLOTS)
        self.both_diag(g, first, size).wait()
        self.add(g, self.chip_y, first, size, self.diag[s, pl.ds(first, size)])
        self.c_near(g, 1).start()
        self.add(g, self.chip_x, first + size, size, self.diag[s, pl.ds(first + size, size)])
        self.c_near(g, 0).start()

    def stage_e(self, g):
        s, p = lax.rem(g, SLOTS), lax.rem(g, PART_SLOTS)
        self.both_near(g).wait()
        total = (self.part[p, self.chip].astype(jnp.float32) + self.near[s, 0].astype(jnp.float32)) + self.near[s, 1].astype(jnp.float32)
        n = lax.rem(g, LINE_SLOTS)
        self.tsum[n] = total

        @pl.when(self.outer)
        def _():
            self.out_a[n] = total.astype(jnp.bfloat16)
            self.c_line(n).start()

    def stage_f(self, g):
        s = lax.rem(g, LINE_SLOTS)

        @pl.when(self.inner)
        def _():
            self.c_line(s).wait_recv()
            self.out_b[s] = (self.tsum[s] + self.zin[s].astype(jnp.float32)).astype(jnp.bfloat16)
            self.c_mid(s).start()

    def stage_h(self, g, put):
        s = lax.rem(g, LINE_SLOTS)

        @pl.when(self.inner)
        def _():
            self.c_mid(s).wait()
            total = (self.out_b[s].astype(jnp.float32) + self.zmid[s].astype(jnp.float32)).astype(jnp.bfloat16)
            self.out_a[s] = total
            self.c_line(s).start()
            put(g, total)

    def stage_i(self, g, put):
        s = lax.rem(g, LINE_SLOTS)

        @pl.when(self.outer)
        def _():
            self.c_line(s).wait()
            put(g, self.zin[s])

        @pl.when(self.inner)
        def _():
            self.c_line(s).wait_send()

    def tick(self, t, put):
        b, d, c, e, f, h, i = LAGS

        def run(lag, stage, *args):
            g = t - lag
            pl.when(jnp.logical_and(g >= 0, g < CHUNKS))(lambda: stage(g, *args))

        run(i, self.stage_i, put)
        run(h, self.stage_h, put)
        run(f, self.stage_f)
        run(e, self.stage_e)
        run(c, lambda g: self.by_kind(g, self.stage_c))
        run(d, lambda g: self.by_kind(g, self.stage_d))
        run(b, self.stage_b)


def dot(a, b):
    return lax.dot_general(a, b, (((1,), (0,)), ((), ())), preferred_element_type=F32)


def dot_nt(a, b):
    return lax.dot_general(a, b, (((1,), (1,)), ((), ())), preferred_element_type=F32)


START, LINK, SIBLING, HOP, ISSUE, LEAD = 6.0, 50.0, 300.0, 2.0, 0.05, 4.0
PIECES = [(-1, 0, 1024, True)]
PIECES += [(k, 512 * h, 512, k == 2 and h == 0) for h in range(2) for k in range(3)]
PIECES += [(-2, 0, 1024, True), (3, 0, 1024, False)]
PIECES += [(4 + n, 0, 1024, n in (1, 4, 6, 7)) for n in range(8)]
COND_TWO, OUT_W, UP_W, DOWN_W = 7, 8, 9, 13


SHARED = {4: 3, 5: 0, 6: 0, 7: 0, 9: 8, 10: 8}


class Gatherer:
    def __init__(self, refs):
        self.cond, self.thirds, self.mats, self.send, self.recv = refs
        self.me = lax.axis_index("fsdp")
        core = lax.rem(self.me, 2)
        chip = lax.div(self.me, 2)
        xbit, ybit = lax.rem(chip, 2), lax.div(chip, 2)
        self.x = (ybit * 2 + 1 - xbit) * 2 + core
        self.y = ((1 - ybit) * 2 + xbit) * 2 + core
        self.d = ((1 - ybit) * 2 + 1 - xbit) * 2 + core
        self.sib = chip * 2 + 1 - core
        row = lax.axis_index("rows")
        self.half = lax.rem(row, 2)
        self.to_z = {"rows": row + 1 - 2 * self.half}
        self.time = START
        self.free = {"x": 0.0, "y": 0.0, "z": 0.0, "s": 0.0}
        self.due = {}
        self.waiting = []
        self.begun, self.whole = 0, set()

    @staticmethod
    def scratch():
        return [
            pltpu.VMEM((8, 64, 1024), BF),
            pltpu.VMEM((3, 2, 8, 128, 512), BF),
            pltpu.VMEM((9, 8, 128, 1024), BF),
            pltpu.SemaphoreType.DMA((len(PIECES), 11)),
            pltpu.SemaphoreType.DMA((len(PIECES), 11)),
        ]

    def enter(self):
        barrier = pltpu.get_barrier_semaphore()
        for to in ({"fsdp": self.sib}, {"fsdp": self.x}, {"fsdp": self.y}, self.to_z):
            pl.semaphore_signal(barrier, inc=1, device_id=to, device_id_type=MESH)
        pl.semaphore_wait(barrier, 4)

    @staticmethod
    def direct(c):
        return PIECES[c][3]

    def shard(self, c, owner, start=0, size=None):
        mat, col, cols, _ = PIECES[c]
        if mat < 0:
            base = 32 * (-1 - mat)
            return self.cond.at[owner, pl.ds(base + start, 32 if size is None else size)]
        rows = pl.ds(start, 128 if size is None else size)
        return self.thirds.at[mat, col // 512, owner, rows] if mat < 3 else self.mats.at[mat - 3, owner, rows]

    def copy(self, c, kind, owner, to, start=0, size=None):
        ref = self.shard(c, owner, start, size)
        return pltpu.make_async_remote_copy(
            src_ref=ref, dst_ref=ref, send_sem=self.send.at[c, kind], recv_sem=self.recv.at[c, SHARED.get(kind, kind)],
            device_id=to, device_id_type=MESH)

    def landed(self, c, kind, rows):
        mat, _, cols, _ = PIECES[c]
        if mat < 0:
            ref = self.cond.at[pl.ds(0, 4), pl.ds(0, 32)] if rows == 128 else self.cond.at[0, pl.ds(0, rows)]
        else:
            base = self.thirds.at[mat, 0] if mat < 3 else self.mats.at[mat - 3]
            ref = base.at[pl.ds(0, rows // 128)] if rows >= 128 else base.at[0, pl.ds(0, rows)]
            if rows == 192:
                ref = base.at[pl.ds(0, 3), pl.ds(0, 64)]
        pltpu.make_async_remote_copy(
            src_ref=ref, dst_ref=ref, send_sem=self.send.at[c, kind], recv_sem=self.recv.at[c, kind],
            device_id={"fsdp": self.sib}, device_id_type=MESH).wait_recv()

    def span(self, c, k=None):
        rows = 32 if PIECES[c][0] < 0 else 128
        if self.direct(c):
            return (0, None) if k is None else (k * (rows // 2), rows // 2)
        return (self.half * 64, 64) if k is None else (self.half * 64 + 32 * k, 32)

    def post(self, link, mark, copy):
        copy.start()
        rows, cols = copy.src_ref.shape[-2:]
        self.time += ISSUE
        self.free[link] = max(self.free[link], self.time) + rows * cols * 2e-3 / (SIBLING if link == "s" else LINK)
        self.due[mark] = self.free[link] + HOP

    def take(self, mark, copy):
        copy.wait_recv()
        self.time = max(self.time, self.due[mark]) + ISSUE

    def take_all(self, c, kinds, rows):
        self.landed(c, kinds[0], rows)
        self.time = max([self.time] + [self.due[c, kind] for kind in kinds]) + ISSUE

    def onward(self, c, kind, owner):
        if self.direct(c):
            self.post("s", (c, 5 + kind), self.copy(c, 5 + kind, owner, {"fsdp": self.sib}))
        else:
            self.post("z", (c, 8 + kind), self.copy(c, 8 + kind, owner, self.to_z, *self.span(c)))

    def s1(self, c):
        self.post("x", (c, 1), self.copy(c, 1, self.me, {"fsdp": self.x}, *self.span(c)))
        self.post("y", (c, 2), self.copy(c, 2, self.me, {"fsdp": self.y}, *self.span(c)))
        self.post("s", (c, 0), self.copy(c, 0, self.me, {"fsdp": self.sib}))
        self.begun = c + 1
        self.waiting.append((2, c))

    def s2(self, c):
        self.take((c, 1), self.copy(c, 1, self.x, {"fsdp": self.x}, *self.span(c)))
        self.post("y", (c, 3), self.copy(c, 3, self.x, {"fsdp": self.y}, *self.span(c, 0)))
        self.onward(c, 0, self.x)
        self.take((c, 2), self.copy(c, 2, self.y, {"fsdp": self.y}, *self.span(c)))
        self.post("x", (c, 4), self.copy(c, 4, self.y, {"fsdp": self.x}, *self.span(c, 1)))
        self.onward(c, 1, self.y)
        self.waiting.append((3, c))

    def s3(self, c):
        self.take_all(c, (3, 4), self.moved(c))
        self.onward(c, 2, self.d)
        self.waiting.append((5 if self.direct(c) else 4, c))

    def s4(self, c):
        self.take_all(c, (8, 9, 10), 192)
        for kind, owner in enumerate((self.x, self.y, self.d)):
            self.post("s", (c, 5 + kind), self.copy(c, 5 + kind, owner, {"fsdp": self.sib}))
        self.waiting.append((5, c))

    def moved(self, c):
        rows = 32 if PIECES[c][0] < 0 else 128
        return rows if self.direct(c) else rows // 2

    def s5(self, c):
        self.take_all(c, (0, 5, 6, 7), 128 if PIECES[c][0] < 0 else 512)
        self.whole.add(c)

    def ready(self, event):
        stage, c = event
        marks = {2: (1, 2), 3: (3, 4), 4: (8, 9, 10), 5: (0, 5, 6, 7)}[stage]
        return max(self.due[c, kind] for kind in marks)

    def feed(self):
        while self.begun < len(PIECES) and min(self.free["x"], self.free["y"]) - self.time < LEAD:
            self.s1(self.begun)

    def step(self, event):
        self.waiting.remove(event)
        stage, c = event
        (self.s2, self.s3, self.s4, self.s5)[stage - 2](c)

    def spend(self, time):
        self.time += time
        while True:
            self.feed()
            landed = [event for event in self.waiting if self.ready(event) <= self.time]
            if not landed:
                break
            self.step(min(landed, key=lambda event: (self.ready(event), event)))

    def need(self, c):
        while c not in self.whole:
            self.feed()
            self.step(min(self.waiting, key=lambda event: (self.ready(event), event)))

    def finish(self):
        for c in range(len(PIECES)):
            self.copy(c, 0, self.me, {"fsdp": self.sib}).wait_send()
            for kind in (1, 2):
                self.copy(c, kind, self.me, {"fsdp": self.x}, *self.span(c)).wait_send()
            for k in range(2):
                self.copy(c, 3 + k, self.x, {"fsdp": self.x}, *self.span(c, k)).wait_send()
            for kind in range(3):
                self.copy(c, 5 + kind, self.x, {"fsdp": self.sib}).wait_send()
                if not self.direct(c):
                    self.copy(c, 8 + kind, self.x, self.to_z, *self.span(c)).wait_send()


def forward_kernel(
    seg_in, freq_in, te_in, x_in, cot_hbm, mixing_hbm, cond_hbm, up_hbm, down_hbm,
    lse_out, scales_out, turn_out, feat_out, thirds_hbm, w_hbm, lt_hbm, dpre_hbm, qkv_hbm, mid_hbm, back_hbm, out_hbm,
    four, wide, condf, nrm, qkv, att, mid, te_at, act, cot, ltb, gbuf, eye, in_sem, w_sem, lt_sem, g_sem, o_sem, *shared,
):
    gat = Gatherer(shared)
    me = gat.me
    thirds, mats = gat.thirds, gat.mats

    def load(src, dst, n):
        return pltpu.make_async_copy(src, dst, in_sem.at[n])

    loads = [load(cond_hbm, condf, 0)]
    loads += [load(mixing_hbm.at[k], four.at[k], 1 + k) for k in range(4)]
    loads += [load(up_hbm, wide, 5), load(cot_hbm, cot, 6)]
    for copy in loads:
        copy.start()
    gat.enter()
    obuf = att
    loads[0].wait()
    for k in range(2):
        gat.cond[me, 32 * k:32 * k + 32] = condf[k].astype(BF)
    gat.s1(0)
    for k in range(4):
        loads[1 + k].wait()
        if k < 3:
            for h in range(2):
                thirds[k, h, me] = four[k, :, 512 * h:512 * h + 512].astype(BF)
            if k < 2:
                gat.s1(1 + k)
        else:
            mats[0, me] = four[k].astype(BF)
    later = [load(down_hbm.at[pl.ds(128 * i, 128)], four.at[i], 7 + i) for i in range(4)]
    for copy in later:
        copy.start()
    ids = seg_in[...].astype(F32)
    column = jnp.broadcast_to(ids, (128, 512)).T[:, :1]
    before = jnp.sum(jnp.where(ids < column, 1.0, 0.0), axis=1, keepdims=True)
    offset = lax.broadcasted_iota(jnp.int32, (512, 1), 0).astype(F32) - before
    angle = offset * freq_in[...]
    lanes = lax.broadcasted_iota(jnp.int32, (1, 128), 1)
    lane_in = lax.rem(lanes, 64)
    low_half = lane_in < 32
    turn_out[0] = jnp.cos(angle)
    turn_out[1] = jnp.where(low_half, -1.0, 1.0) * jnp.sin(angle)
    spot = lane_in.astype(F32)
    square = (lax.broadcasted_iota(jnp.int32, (256, 256), n) for n in range(2))
    eye[...] = jnp.where(next(square) == next(square), 1.0, 0.0).astype(BF)
    feat_out[0] = jnp.where(jnp.logical_and(lane_in < 4, spot != column), 1.0, 0.0).astype(BF)
    feat_out[1] = jnp.where(spot == column, -1e30, 0.0).astype(BF)
    te_column = jnp.broadcast_to(te_in[...].astype(F32), (128, 256)).T[:, :1]
    for f in range(8):
        te_at[f] = te_column[32 * f:32 * f + 32]
    loads[5].wait()
    for i in range(4):
        for f in range(8):
            mats[1 + i, me, :, 128 * f:128 * f + 128] = wide[:, 512 * f + 128 * i:512 * f + 128 * i + 128].astype(BF)
    for i in range(4):
        later[i].wait()
        mats[5 + i, me] = four[i].astype(BF)

    def save_w(m):
        if m < 3:
            return pltpu.make_async_copy(thirds.at[m], thirds_hbm.at[m], w_sem.at[m])
        return pltpu.make_async_copy(mats.at[0], w_hbm, w_sem.at[m])

    def save_lt(n, slot):
        return pltpu.make_async_copy(ltb.at[slot], lt_hbm.at[n], lt_sem.at[slot])

    def turn(block, b, slot):
        rows = slice(128 * b, 128 * b + 128) if isinstance(b, int) else pl.ds(pl.multiple_of(b * 128, 128), 128)
        turned = dot_nt(eye[...], block).astype(BF)
        for a in range(2):
            ltb[slot, a, rows] = turned[128 * a:128 * a + 128]

    def scale_of(k):
        total = jnp.zeros((32, 1024), F32)
        for f in range(8):
            total = total + te_at[f] * gat.cond[f, 32 * k:32 * k + 32].astype(F32)
        scales_out[k:k + 1] = 1.0 + jnp.sum(total, axis=0, keepdims=True)

    def norm_rows(source, scale):
        def block(b, carry):
            rows = pl.ds(pl.multiple_of(b * 64, 64), 64)
            values = source[rows].astype(F32)
            center = values - jnp.mean(values, axis=-1, keepdims=True)
            spread = jnp.mean(center * center, axis=-1, keepdims=True)
            nrm[rows] = (center * lax.rsqrt(spread + 1e-05) * scale).astype(BF)
            return carry

        lax.fori_loop(0, 8, block, 0, unroll=2)

    gat.need(0)
    scale_of(0)
    norm_rows(x_in, scales_out[0:1])
    gat.spend(1.2)

    def save_qkv(k):
        return pltpu.make_async_copy(qkv.at[k], qkv_hbm.at[k], o_sem.at[k])

    def project(k, half):
        at = slice(512 * half, 512 * half + 512)
        result = dot(nrm[...], thirds[k, half].reshape(1024, 512))
        if k == 0:
            for b in range(2):
                turn(nrm[:, 512 * half + 256 * b:512 * half + 256 * b + 256], 2 * half + b, 0)
        if k < 2:
            sides = []
            for n in range(4):
                part = result[:, 128 * n:128 * n + 128]
                other = jnp.where(low_half, pltpu.roll(part, 96, 1), pltpu.roll(part, 32, 1))
                sides.append(part * turn_out[0] + other * turn_out[1])
            result = jnp.concatenate(sides, axis=1)
        result = result.astype(BF)
        qkv[k, :, at] = result * jnp.asarray(0.125, BF) if k == 0 else result

    def attend(pair, carry):
        at = pl.ds(pl.multiple_of(pair * 128, 128), 128)
        q_pair, k_pair = qkv[0, :, at], qkv[1, :, at]
        v_turned = qkv[2, :, at].T
        heads = [lax.div(lanes, 64) == j for j in range(2)]
        raws = [dot_nt(jnp.where(mine, k_pair, feat_out[1]), jnp.where(mine, q_pair, feat_out[0])) for mine in heads]
        peaks = [jnp.max(raw, axis=0, keepdims=True) for raw in raws]
        grown = [jnp.exp(raw - peak) for raw, peak in zip(raws, peaks)]
        totals = [jnp.sum(value, axis=0, keepdims=True) for value in grown]
        sides = [dot(v_turned[64 * j:64 * j + 64], grown[j].astype(BF)) * (1.0 / totals[j]) for j in range(2)]
        sums = [peak + jnp.log(total) for peak, total in zip(peaks, totals)]
        lse_out[pair] = jnp.concatenate(sums, axis=0)
        block = jnp.concatenate(sides, axis=0).astype(BF)
        ltb[1, lax.rem(pair, 2), pl.ds(pl.multiple_of(lax.div(pair, 2) * 128, 128), 128)] = block
        att[:, at] = block.T
        return carry

    for half in range(2):
        for k in range(3):
            gat.need(1 + 3 * half + k)
            project(k, half)
            gat.spend(0.9)
        if half == 1:
            for k in range(3):
                save_w(k).start()
                save_qkv(k).start()
            save_lt(6, 0).start()
        for part in range(2):
            begin = 4 * half + 2 * part
            lax.fori_loop(begin, begin + 2, attend, 0)
            gat.spend(3.6)
    save_lt(5, 1).start()
    gat.need(COND_TWO)
    scale_of(1)
    gat.need(OUT_W)
    save_w(3).start()

    def join(b, carry):
        at = pl.ds(pl.multiple_of(b * 512, 512), 512)
        mid[:, at] = x_in[:, at].astype(F32) + dot(att[...], mats[0, :, :, at].reshape(1024, 512))
        return carry

    lax.fori_loop(0, 2, join, 0)
    gat.spend(1.8)
    save_mid = pltpu.make_async_copy(mid, mid_hbm, o_sem.at[3])
    save_mid.start()
    norm_rows(mid, scales_out[1:2])
    gat.spend(2.4)
    befores = {0: 6, 1: 5, 2: 4}

    def save_dpre(i):
        return pltpu.make_async_copy(gbuf.at[i], dpre_hbm.at[i], g_sem.at[i])

    for i in range(4):
        gat.need(UP_W + i)
        save_lt(befores[i % 3], i % 3).wait()

        def expand(b, carry):
            at = pl.ds(pl.multiple_of(b * 512, 512), 512)
            u = dot(nrm[...], mats[1 + i, :, :, at].reshape(1024, 512))
            root = 0.7978845608028654
            square = u * u
            bend = jnp.tanh(root * u * (1.0 + 0.044715 * square))
            side = 0.5 * (1.0 + bend)
            result = (u * side).astype(BF)
            act[i, :, at] = result
            for n in range(2):
                turn(result[:, 256 * n:256 * n + 256], 2 * b + n, i % 3)
                if i == 0:
                    turn(nrm[:, pl.ds(pl.multiple_of(b * 512 + n * 256, 256), 256)], 2 * b + n, 2)
            slope = side + 0.5 * u * (1.0 - bend * bend) * (root * (1.0 + 3.0 * 0.044715 * square))
            gbuf[i, :, at] = slope.astype(BF)
            return carry

        lax.fori_loop(0, 2, expand, 0)
        save_lt(i, i % 3).start()
        befores[i % 3] = i
        if i == 0:
            save_lt(4, 2).start()
        gat.spend(3.0)
    for i in range(4):
        gat.need(DOWN_W + i)
        if i == 0:
            loads[6].wait()

        def slopes(b, carry):
            at = pl.ds(pl.multiple_of(b * 512, 512), 512)
            d_act = dot_nt(cot[...], mats[5 + i, pl.ds(4 * b, 4)].reshape(512, 1024))
            gbuf[i, :, at] = (d_act * gbuf[i, :, at].astype(F32)).astype(BF)
            return carry

        lax.fori_loop(0, 2, slopes, 0)
        save_dpre(i).start()
        gat.spend(1.2)

    def shrink(b, carry):
        at = pl.ds(pl.multiple_of(b * 512, 512), 512)
        total = mid[:, at]
        for i in range(4):
            total = total + dot(act[i], mats[5 + i, :, :, at].reshape(1024, 512))
        obuf[:, at] = total.astype(BF)
        back = dot_nt(gbuf[0], mats[1, pl.ds(4 * b, 4)].reshape(512, 1024))
        for i in range(1, 4):
            back = back + dot_nt(gbuf[i], mats[1 + i, pl.ds(4 * b, 4)].reshape(512, 1024))
        four[:, :, at] = back.reshape(4, 128, 512)
        return carry

    lax.fori_loop(0, 2, shrink, 0)
    save_out = pltpu.make_async_copy(obuf, out_hbm, o_sem.at[4])
    save_out.start()
    save_back = pltpu.make_async_copy(four, back_hbm, o_sem.at[5])
    save_back.start()
    gat.finish()
    for m in range(4):
        save_w(m).wait()
    for k in range(3):
        save_qkv(k).wait()
        save_lt(befores[k], k).wait()
    save_mid.wait()
    for i in range(4):
        save_dpre(i).wait()
    save_out.wait()
    save_back.wait()


def forward(seg, te, x, cot, mixing_w, cond_w, up_w, down_w):
    vmem = pl.BlockSpec(memory_space=pltpu.VMEM)
    anyw = pl.BlockSpec(memory_space=pl.ANY)
    shape = jax.ShapeDtypeStruct
    freq = 10000.0 ** (-(np.arange(128) % 32) * 2.0 / HEAD_DIM)
    return pl.pallas_call(
        forward_kernel,
        out_shape=(
            shape((8, 2, 512), F32), shape((2, 1024), F32), shape((2, 512, 128), F32), shape((2, 512, 128), BF),
            shape((3, 2, 8, 128, 512), BF), shape((8, 128, 1024), BF), shape((7, 2, 512, 512), BF), shape((4, 512, 1024), BF),
            shape((3, 512, 1024), BF), shape((512, 1024), F32), shape((4, 128, 1024), F32), shape((512, 1024), BF)),
        in_specs=[vmem] * 4 + [anyw] * 5,
        out_specs=(vmem,) * 4 + (anyw,) * 8,
        scratch_shapes=[
            pltpu.VMEM((4, 128, 1024), F32),
            pltpu.VMEM((128, 4096), F32),
            pltpu.VMEM((2, 32, 1024), F32),
            pltpu.VMEM((512, 1024), BF),
            pltpu.VMEM((3, 512, 1024), BF),
            pltpu.VMEM((512, 1024), BF),
            pltpu.VMEM((512, 1024), F32),
            pltpu.VMEM((8, 32, 1), F32),
            pltpu.VMEM((4, 512, 1024), BF),
            pltpu.VMEM((512, 1024), BF),
            pltpu.VMEM((3, 2, 512, 512), BF),
            pltpu.VMEM((4, 512, 1024), BF),
            pltpu.VMEM((256, 256), BF),
            pltpu.SemaphoreType.DMA((11,)),
            pltpu.SemaphoreType.DMA((4,)),
            pltpu.SemaphoreType.DMA((3,)),
            pltpu.SemaphoreType.DMA((4,)),
            pltpu.SemaphoreType.DMA((6,)),
        ] + Gatherer.scratch(),
        compiler_params=pltpu.CompilerParams(collective_id=2, has_side_effects=True, vmem_limit_bytes=63 * 2**20),
    )(seg, jnp.asarray(freq[None], F32), te, x, cot, mixing_w, cond_w, up_w, down_w)


def norm_back(values, grads, scale):
    center = values - jnp.mean(values, axis=-1, keepdims=True)
    recip = lax.rsqrt(jnp.mean(center * center, axis=-1, keepdims=True) + 1e-05)
    unit = center * recip
    g = grads * scale
    back = recip * (g - jnp.mean(g, axis=-1, keepdims=True) - unit * jnp.mean(g * unit, axis=-1, keepdims=True))
    return back, grads * unit


def backward_kernel(
    turn_in, lse_in, scales_in, te_in, feat_in, thirds_hbm, w_hbm, lt_hbm, cot_hbm, dpre_hbm, qkv_hbm, mid_hbm, back_hbm, x_hbm,
    sums, in_grad,
    lt, rh, thirds, wout, qkv, mid, acc, dmid, datt, xin, dscale, obuf, te_at, load_sem, out_sem, *shared,
):
    red = Reducer(shared)
    core = red.core

    def load(src, dst, n):
        return pltpu.make_async_copy(src, dst, load_sem.at[n])

    load_lt = [load(lt_hbm.at[n], lt.at[n], n) for n in range(7)]
    load_cot = load(cot_hbm, rh.at[0], 7)
    load_mid = load(mid_hbm, mid, 8)
    load_back = load(back_hbm, acc, 9)
    load_w3 = load(w_hbm, wout, 10)
    load_qkv = load(qkv_hbm, qkv, 11)
    load_dpre = load(dpre_hbm, rh.at[pl.ds(1, 4)], 12)
    load_w = load(thirds_hbm, thirds, 13)
    load_x = load(x_hbm, xin, 14)
    for copy in (load_cot, load_lt[0], load_mid, load_back, load_w3):
        copy.start()
    later = (load_lt[1], load_qkv, load_lt[2], load_lt[3], load_lt[4], load_dpre, load_lt[5], load_w, load_lt[6], load_x)
    arrivals = {1: (load_lt[1], load_qkv), 2: (load_lt[2],), 3: (load_lt[3],), 4: (load_lt[4], load_dpre), 8: (load_lt[5],),
                9: (load_lt[6], load_w, load_x)}
    red.enter()

    def operands(g):
        left = jnp.where(g < 8, lax.div(g, 2), jnp.where(g < 16, 4, jnp.where(g < 18, 5, 6)))
        right = jnp.where(g < 8, 0, jnp.where(g < 16, 1 + lax.div(g - 8, 2), jnp.where(g < 18, 5, 6 + lax.div(g - 18, 2))))
        return left, rh[right, :, pl.ds(pl.multiple_of(lax.rem(g, 2) * 512, 512), 512)]

    def give(g):
        left, right = operands(g)
        halves = dot(lt[left].reshape(1024, 512), right).astype(BF).reshape(2, 4, 128, 512)
        for p in range(2):
            @pl.when(core == p)
            def _(p=p):
                red.away[lax.rem(g, SLOTS)] = halves[1 - p]
                red.part[lax.rem(g, PART_SLOTS)] = halves[p]

        red.c_sib(g).start()

    def cond_part(parity):
        rows = []
        for chip in range(4):
            column = te_at[2 * chip + parity]
            rows.append(jnp.concatenate([column * dscale[k:k + 1, 512 * h:512 * h + 512] for k in range(2) for h in range(2)], axis=0)[None])
        return jnp.concatenate(rows, axis=0)

    def put(g, value):
        sums[g] = value

    te_column = jnp.broadcast_to(te_in[...].astype(F32), (128, 256)).T[:, :1]
    for f in range(8):
        te_at[f] = te_column[32 * f:32 * f + 32]
    lanes = lax.broadcasted_iota(jnp.int32, (1, 128), 1)
    low_half = lax.rem(lanes, 64) < 32

    def unrotate(block):
        other = jnp.where(low_half, pltpu.roll(block, 96, 1), pltpu.roll(block, 32, 1))
        return block * turn_in[0] - other * turn_in[1]

    def middle_back():
        for copy in later:
            copy.start()
        load_mid.wait()
        load_back.wait()

        def norm_two(b, total):
            rows = pl.ds(pl.multiple_of(b * 64, 64), 64)
            back, terms = norm_back(mid[rows], acc[rows], scales_in[1:2])
            back = back + rh[0, rows].astype(F32)
            dmid[rows] = back
            rh[5, rows] = back.astype(BF)
            return total + jnp.sum(terms.reshape(8, 8, 1024), axis=0)

        total = lax.fori_loop(0, 8, norm_two, jnp.zeros((8, 1024), F32), unroll=2)
        dscale[1:2] = jnp.sum(total, axis=0, keepdims=True)
        load_w3.wait()
        for n in range(2):
            cols = slice(512 * n, 512 * n + 512)
            datt[:, cols] = dot_nt(rh[5], wout[cols, :]).astype(BF)

    def attend_back(pair):
        at = pl.ds(pl.multiple_of(pair * 128, 128), 128)
        q_pair, k_pair, v_pair, d_pair = qkv[0, :, at], qkv[1, :, at], qkv[2, :, at], datt[:, at]
        k_turned = (k_pair * jnp.asarray(0.125, BF)).T
        heads = [lax.div(lanes, 64) == j for j in range(2)]
        raws = [dot_nt(jnp.where(mine, k_pair, feat_in[1]), jnp.where(mine, q_pair, feat_in[0])) for mine in heads]
        d_probs = [dot_nt(v_pair, jnp.where(mine, d_pair, jnp.zeros_like(d_pair))) for mine in heads]
        made = []
        for j in range(2):
            probs = jnp.exp(raws[j] - lse_in[pair, j:j + 1])
            delta = jnp.sum(probs * d_probs[j], axis=0, keepdims=True)
            d_raw = (probs * (d_probs[j] - delta)).astype(BF)
            made.append((dot(k_turned[64 * j:64 * j + 64], d_raw), dot(d_raw, q_pair), dot(probs.astype(BF), d_pair)))
        rh[6, :, at] = unrotate(jnp.concatenate([made[0][0], made[1][0]], axis=0).T).astype(BF)
        rh[7, :, at] = unrotate(jnp.where(heads[0], made[0][1], made[1][1])).astype(BF)
        rh[8, :, at] = jnp.where(heads[0], made[0][2], made[1][2]).astype(BF)

    def first_back(k):
        for h in range(2):
            cols = slice(512 * h, 512 * h + 512)
            part = dot_nt(rh[6 + k, :, :512], thirds[k, 0, cols]) + dot_nt(rh[6 + k, :, 512:], thirds[k, 1, cols])

            @pl.when(k == 0)
            def _():
                acc[:, cols] = part

            @pl.when(k > 0)
            def _():
                acc[:, cols] += part

    def input_back():
        def norm_one(b, total):
            rows = pl.ds(pl.multiple_of(b * 64, 64), 64)
            back, terms = norm_back(xin[rows].astype(F32), acc[rows], scales_in[0:1])
            obuf[rows] = (dmid[rows] + back).astype(BF)
            return total + jnp.sum(terms.reshape(8, 8, 1024), axis=0)

        total = lax.fori_loop(0, 8, norm_one, jnp.zeros((8, 1024), F32), unroll=2)
        dscale[0:1] = jnp.sum(total, axis=0, keepdims=True)
        store_out.start()
        red.away[(CHUNKS - 1) % SLOTS] = cond_part(1 - core).astype(BF)
        red.part[(CHUNKS - 1) % PART_SLOTS] = cond_part(core).astype(BF)
        red.c_sib(jnp.int32(CHUNKS - 1)).start()

    store_out = pltpu.make_async_copy(obuf, in_grad, out_sem)
    load_cot.wait()
    load_lt[0].wait()

    def turn(m, carry):
        for when, copies in arrivals.items():
            @pl.when(m == when)
            def _(copies=copies):
                for copy in copies:
                    copy.wait()

        @pl.when(m < 12)
        def _():
            give(2 * m)
            give(2 * m + 1)

        pl.when(jnp.logical_and(m >= 1, m < 9))(lambda: attend_back(m - 1))

        pl.when(jnp.logical_and(m >= 9, m < 12))(lambda: first_back(m - 9))
        pl.when(m == 12)(input_back)
        def ticks(t, carry):
            red.tick(t, put)
            return carry

        lax.fori_loop(2 * m, 2 * m + 2, ticks, 0)
        pl.when(m == 0)(middle_back)

        return carry

    lax.fori_loop(0, (CHUNKS + LAGS[-1] + 1) // 2, turn, 0)
    store_out.wait()


def backward(turn, lse, scales, te, feat, thirds, w, lt, cot, dpre, qkv, mid, back, x):
    vmem = pl.BlockSpec(memory_space=pltpu.VMEM)
    anyw = pl.BlockSpec(memory_space=pl.ANY)
    shape = jax.ShapeDtypeStruct
    return pl.pallas_call(
        backward_kernel,
        out_shape=(
            shape((CHUNKS, 128, 512), BF), shape((512, 1024), BF)),
        in_specs=[vmem] * 5 + [anyw] * 9,
        out_specs=(vmem, anyw),
        scratch_shapes=[
            pltpu.VMEM((7, 2, 512, 512), BF),
            pltpu.VMEM((9, 512, 1024), BF),
            pltpu.VMEM((3, 2, 1024, 512), BF),
            pltpu.VMEM((1024, 1024), BF),
            pltpu.VMEM((3, 512, 1024), BF),
            pltpu.VMEM((512, 1024), F32),
            pltpu.VMEM((512, 1024), F32),
            pltpu.VMEM((512, 1024), F32),
            pltpu.VMEM((512, 1024), BF),
            pltpu.VMEM((512, 1024), BF),
            pltpu.VMEM((2, 1024), F32),
            pltpu.VMEM((512, 1024), BF),
            pltpu.VMEM((8, 32, 1), F32),
            pltpu.SemaphoreType.DMA((16,)),
            pltpu.SemaphoreType.DMA,
        ] + Reducer.scratch(),
        compiler_params=pltpu.CompilerParams(collective_id=1, has_side_effects=True, vmem_limit_bytes=63 * 2**20),
    )(turn, lse, scales, te, feat, thirds.reshape(3, 2, 1024, 512), w.reshape(1024, 1024), lt, cot, dpre, qkv, mid, back.reshape(512, 1024), x)


def update_kernel(*refs):
    sums, states, rows, outs, rows_out = refs[0], refs[1:17], refs[17:19], refs[19:39], refs[39:41]
    fresh, held, made, passed, in_sem, out_sem, pass_sem = refs[41:]
    mix, cond, up, down = range(4)
    units = [(kind, i) for kind in (down, up, mix) for i in range(4)] + [(cond, 0)]
    keep_one = 1.0 / (1.0 - 0.5**STEP)

    def piece(ref, kind, i):
        if kind == up:
            return ref.at[:, pl.ds(1024 * i, 1024)]
        if kind == cond:
            return ref
        return ref.at[i] if len(ref.shape) == 3 else ref.at[pl.ds(128 * i, 128)]

    def summed(kind, i, buffer):
        if kind == cond:
            return [(sums.at[24, pl.ds(64 * k + 32 * h, 32)], buffer.at[pl.ds(32 * k, 32), pl.ds(512 * h, 512)])
                    for k in range(2) for h in range(2)]
        if kind == up:
            half, first = i // 2, 2 * (i % 2)
            return [(sums.at[8 + 2 * n + half, :, pl.ds(128 * (first + a), 128)], buffer.at[:, pl.ds(512 * a + 128 * n, 128)])
                    for n in range(4) for a in range(2)]
        chunk = 2 * i if kind == down else 16 + 2 * ((i + 1) % 4)
        return [(sums.at[chunk + h], buffer.at[:, pl.ds(512 * h, 512)]) for h in range(2)]

    def loads(u):
        kind, i = units[u]
        s = u % RING
        copies = [(a, b, in_sem.at[s, 8 + n]) for n, (a, b) in enumerate(summed(kind, i, fresh.at[s]))]
        for n, ref in enumerate(states[4 * kind:4 * kind + 4]):
            if kind == cond:
                for k in range(2):
                    copies.append((ref.at[k], held.at[s, n, pl.ds(32 * k, 32)], in_sem.at[s, 4 * k + n]))
            else:
                copies.append((piece(ref, kind, i), held.at[s, n], in_sem.at[s, n]))
        return [pltpu.make_async_copy(*c) for c in copies]

    def saves(u):
        kind, i = units[u]
        s = u % RING
        copies = []
        for n in range(5):
            ref, buffer = outs[5 * kind + n], made.at[s, n]
            if kind == cond:
                for k in range(2):
                    copies.append((buffer.at[pl.ds(32 * k, 32)], ref.at[k], out_sem.at[s, 5 * k + n]))
            else:
                copies.append((buffer, piece(ref, kind, i), out_sem.at[s, n]))
        return [pltpu.make_async_copy(*c) for c in copies]

    enter = [pltpu.make_async_copy(rows[n], passed.at[n], pass_sem.at[n]) for n in range(2)]
    leave = [pltpu.make_async_copy(passed.at[n], rows_out[n].at[0], pass_sem.at[n]) for n in range(2)]
    for u in range(RING - 1):
        for copy in loads(u):
            copy.start()
    for copy in enter:
        copy.start()
    for u in range(len(units)):
        s = u % RING
        if u == 2:
            for n in range(2):
                enter[n].wait()
                leave[n].start()
        if u + RING - 1 < len(units):
            for copy in loads(u + RING - 1):
                copy.start()
        if u >= RING:
            for copy in saves(u - RING):
                copy.wait()
        for copy in loads(u):
            copy.wait()

        def rows_step(b, carry):
            rows = pl.ds(pl.multiple_of(b * 16, 16), 16)
            g = fresh[s, rows].astype(F32)
            w = held[s, 0, rows]
            m = 0.5 * held[s, 1, rows] + 0.5 * g
            v = 0.5 * held[s, 2, rows] + 0.5 * g * g
            w_new = w - 0.01 * (m * keep_one / (jnp.sqrt(v * keep_one) + 1e-08) + 0.1 * w)
            made[s, 0, rows] = g
            made[s, 1, rows] = m
            made[s, 2, rows] = v
            made[s, 3, rows] = w_new
            made[s, 4, rows] = 0.8 * held[s, 3, rows] + 0.2 * w_new
            return carry

        lax.fori_loop(0, 4 if units[u][0] == cond else 8, rows_step, 0)
        for copy in saves(u):
            copy.start()
    for u in range(len(units) - RING, len(units)):
        for copy in saves(u):
            copy.wait()
    for copy in leave:
        copy.wait()


RING = 4


def update(sums, states, rows):
    anyw = pl.BlockSpec(memory_space=pl.ANY)
    outs = []
    for n in range(4):
        outs += [jax.ShapeDtypeStruct(states[4 * n].shape, F32)] * 5
    outs += [jax.ShapeDtypeStruct((1, 512, 1024), BF)] * 2
    *made, output, input_grad = pl.pallas_call(
        update_kernel,
        out_shape=tuple(outs),
        in_specs=[anyw] * 19,
        out_specs=(anyw,) * 22,
        scratch_shapes=[
            pltpu.VMEM((RING, 128, 1024), BF),
            pltpu.VMEM((RING, 4, 128, 1024), F32),
            pltpu.VMEM((RING, 5, 128, 1024), F32),
            pltpu.VMEM((2, 512, 1024), BF),
            pltpu.SemaphoreType.DMA((RING, 16)),
            pltpu.SemaphoreType.DMA((RING, 10)),
            pltpu.SemaphoreType.DMA((2,)),
        ],
        compiler_params=pltpu.CompilerParams(vmem_limit_bytes=63 * 2**20),
    )(sums, *states, *rows)
    return (output, input_grad, *made)


def normed(values):
    center = values - jnp.mean(values, axis=-1, keepdims=True)
    spread = jnp.mean(center * center, axis=-1, keepdims=True)
    return center * lax.rsqrt(spread + 1e-05)


def scaled_norm(values, gain):
    return normed(values) * gain[None, :]


def rotary_tables(segments):
    length = segments.shape[0]
    position = jnp.arange(length, dtype=jnp.int32)
    is_start = jnp.concatenate([jnp.ones((1,), dtype=bool), segments[1:] != segments[:-1]])
    seg_start = lax.cummax(jnp.where(is_start, position, jnp.zeros_like(position)), axis=0)
    offset = (position - seg_start).astype(jnp.float32)
    frequency = 10000.0 ** (-jnp.arange(HEAD_DIM // 2, dtype=jnp.float32) * 2.0 / HEAD_DIM)
    turned = offset[:, None] * frequency[None, :]
    return (jnp.cos(turned)[:, None, :], jnp.sin(turned)[:, None, :])


def rotate(parts, cos_table, sin_table):
    half_dim = parts.shape[-1] // 2
    part_a = parts[..., :half_dim]
    part_b = parts[..., half_dim:]
    return jnp.concatenate(
        [part_a * cos_table - part_b * sin_table, part_b * cos_table + part_a * sin_table], axis=-1
    )


def unrotate(grads, cos_table, sin_table):
    half_dim = grads.shape[-1] // 2
    grad_a = grads[..., :half_dim]
    grad_b = grads[..., half_dim:]
    return jnp.concatenate(
        [grad_a * cos_table + grad_b * sin_table, grad_b * cos_table - grad_a * sin_table], axis=-1
    )


def adam_update(gradient, weight, moment_one, moment_two, average):
    moment_one_new = 0.5 * moment_one + 0.5 * gradient
    moment_two_new = 0.5 * moment_two + 0.5 * gradient * gradient
    correction = 1.0 - 0.5**STEP
    update = (
        moment_one_new / correction / (jnp.sqrt(moment_two_new / correction) + 1e-08) + 0.1 * weight
    )
    weight_new = weight - 0.01 * update
    average_new = 0.8 * average + 0.2 * weight_new
    return (moment_one_new, moment_two_new, weight_new, average_new)


def local(
    tokens,
    time_embed,
    segment_ids,
    cotangent,
    mixing_w,
    mixing_m,
    mixing_v,
    mixing_avg,
    cond_w,
    cond_m,
    cond_v,
    cond_avg,
    up_w,
    up_m,
    up_v,
    up_avg,
    down_w,
    down_m,
    down_v,
    down_avg,
):
    rows_in = tokens[0].astype(jnp.float32)
    embedding = time_embed[0]
    segments = segment_ids[0]
    length = rows_in.shape[0]
    block_rows = min(512, length)
    block_count = length // block_rows
    mixing_g, cond_g = (
        lax.all_gather(mixing_w.astype(jnp.bfloat16), "fsdp", axis=1, tiled=True),
        lax.all_gather(cond_w.astype(jnp.bfloat16), "fsdp", axis=1, tiled=True),
    )
    up_g, down_g = (
        lax.all_gather(up_w.astype(jnp.bfloat16), "fsdp", axis=0, tiled=True),
        lax.all_gather(down_w.astype(jnp.bfloat16), "fsdp", axis=0, tiled=True),
    )
    scales = 1.0 + jnp.einsum("e,ked->kd", embedding, cond_g, preferred_element_type=jnp.float32)
    cos_table, sin_table = rotary_tables(segments)
    normed_one = (normed(rows_in) * scales[0][None, :]).astype(jnp.bfloat16)
    projected = jnp.einsum(
        "td,kde->kte", normed_one, mixing_g[:3], preferred_element_type=jnp.float32
    )
    queries = rotate(projected[0].reshape(length, HEADS, HEAD_DIM), cos_table, sin_table).astype(
        jnp.bfloat16
    )
    keys_rot = rotate(projected[1].reshape(length, HEADS, HEAD_DIM), cos_table, sin_table).astype(
        jnp.bfloat16
    )
    values_b = projected[2].astype(jnp.bfloat16).reshape(length, HEADS, HEAD_DIM)
    query_blocks = queries.reshape(block_count, block_rows, HEADS, HEAD_DIM)
    seg_blocks = segments.reshape(block_count, block_rows)

    def block_scores(q_block, seg_block):
        raw = (
            jnp.einsum("qhd,khd->hqk", q_block, keys_rot, preferred_element_type=jnp.float32)
            * 0.125
        )
        same_seg = seg_block[:, None] == segments[None, :]
        return jnp.where(same_seg[None], raw, -1e30)

    def attend_block(element):
        q_block, seg_block = element
        raw = block_scores(q_block, seg_block)
        peak = jnp.max(raw, axis=-1, keepdims=True)
        exp_scores = jnp.exp(raw - peak)
        totals = jnp.sum(exp_scores, axis=-1, keepdims=True)
        probs = (exp_scores / totals).astype(jnp.bfloat16)
        out_block = jnp.einsum(
            "hqk,khd->qhd", probs, values_b, preferred_element_type=jnp.float32
        ).astype(jnp.bfloat16)
        return (out_block, peak[..., 0] + jnp.log(totals[..., 0]))

    attended, log_totals = lax.map(attend_block, (query_blocks, seg_blocks))
    attended = attended.reshape(length, D)
    middle = rows_in + jnp.dot(attended, mixing_g[3], preferred_element_type=jnp.float32)
    normed_two = (normed(middle) * scales[1][None, :]).astype(jnp.bfloat16)
    hidden_pre = jnp.dot(normed_two, up_g, preferred_element_type=jnp.float32)
    hidden_act = jax.nn.gelu(hidden_pre).astype(jnp.bfloat16)
    output = (middle + jnp.dot(hidden_act, down_g, preferred_element_type=jnp.float32)).astype(
        jnp.bfloat16
    )
    mixing_b, cond_b = (
        lax.all_gather(mixing_w.astype(jnp.bfloat16), "fsdp", axis=1, tiled=True),
        lax.all_gather(cond_w.astype(jnp.bfloat16), "fsdp", axis=1, tiled=True),
    )
    up_b, down_b = (
        lax.all_gather(up_w.astype(jnp.bfloat16), "fsdp", axis=0, tiled=True),
        lax.all_gather(down_w.astype(jnp.bfloat16), "fsdp", axis=0, tiled=True),
    )
    back_out = cotangent[0]
    d_act = jnp.einsum("td,fd->tf", back_out, down_b, preferred_element_type=jnp.float32)
    d_down = jnp.einsum("tf,td->fd", hidden_act, back_out, preferred_element_type=jnp.float32)
    _, gelu_pull = jax.vjp(jax.nn.gelu, hidden_pre)
    d_pre = gelu_pull(d_act)[0].astype(jnp.bfloat16)
    d_up = jnp.einsum("td,tf->df", normed_two, d_pre, preferred_element_type=jnp.float32)
    d_normed_two = jnp.einsum("tf,df->td", d_pre, up_b, preferred_element_type=jnp.float32)
    _, norm_pull_two = jax.vjp(scaled_norm, middle, scales[1])
    d_middle, d_scale_two = norm_pull_two(d_normed_two)
    d_middle = d_middle + back_out.astype(jnp.float32)
    d_middle_b = d_middle.astype(jnp.bfloat16)
    d_out_proj = jnp.einsum("td,te->de", attended, d_middle_b, preferred_element_type=jnp.float32)
    d_attended = jnp.einsum(
        "te,de->td", d_middle_b, mixing_b[3], preferred_element_type=jnp.float32
    ).astype(jnp.bfloat16)
    d_att_blocks = d_attended.reshape(block_count, block_rows, HEADS, HEAD_DIM)

    def back_block(state_in, element):
        q_block, seg_block, d_block, log_block = element
        raw = block_scores(q_block, seg_block)
        probs_f = jnp.exp(raw - log_block[..., None])
        probs_b = probs_f.astype(jnp.bfloat16)
        d_probs = jnp.einsum("qhd,khd->hqk", d_block, values_b, preferred_element_type=jnp.float32)
        d_raw = (probs_f * (d_probs - jnp.sum(probs_f * d_probs, axis=-1, keepdims=True))).astype(
            jnp.bfloat16
        )
        d_query = (
            jnp.einsum("hqk,khd->qhd", d_raw, keys_rot, preferred_element_type=jnp.float32) * 0.125
        )
        keys_acc = (
            state_in[0]
            + jnp.einsum("hqk,qhd->khd", d_raw, q_block, preferred_element_type=jnp.float32) * 0.125
        )
        values_acc = state_in[1] + jnp.einsum(
            "hqk,qhd->khd", probs_b, d_block, preferred_element_type=jnp.float32
        )
        return ((keys_acc, values_acc), d_query)

    zero_heads = jnp.zeros((length, HEADS, HEAD_DIM), jnp.float32)
    (d_keys, d_values), d_queries = lax.scan(
        back_block, (zero_heads, zero_heads), (query_blocks, seg_blocks, d_att_blocks, log_totals)
    )
    d_queries = unrotate(d_queries.reshape(length, HEADS, HEAD_DIM), cos_table, sin_table)
    d_keys = unrotate(d_keys, cos_table, sin_table)
    d_projected = (
        jnp.stack([d_queries, d_keys, d_values]).reshape(3, length, D).astype(jnp.bfloat16)
    )
    d_qkv = jnp.einsum("td,kte->kde", normed_one, d_projected, preferred_element_type=jnp.float32)
    d_normed_one = jnp.einsum(
        "kte,kde->td", d_projected, mixing_b[:3], preferred_element_type=jnp.float32
    )
    _, norm_pull_one = jax.vjp(scaled_norm, rows_in, scales[0])
    d_rows, d_scale_one = norm_pull_one(d_normed_one)
    input_grad = (d_middle + d_rows).astype(jnp.bfloat16)
    d_scales = jnp.stack([d_scale_one, d_scale_two])
    d_cond = embedding.astype(jnp.float32)[None, :, None] * d_scales[:, None, :]
    d_mixing = jnp.concatenate([d_qkv, d_out_proj[None]], axis=0)
    mixing_part, cond_part = (
        lax.psum_scatter(d_mixing, "fsdp", scatter_dimension=1, tiled=True),
        lax.psum_scatter(d_cond, "fsdp", scatter_dimension=1, tiled=True),
    )
    up_part, down_part = (
        lax.psum_scatter(d_up, "fsdp", scatter_dimension=0, tiled=True),
        lax.psum_scatter(d_down, "fsdp", scatter_dimension=0, tiled=True),
    )
    mixing_grad, cond_grad, up_grad, down_grad = (
        lax.psum(mixing_part.astype(jnp.bfloat16), "rows").astype(jnp.float32),
        lax.psum(cond_part.astype(jnp.bfloat16), "rows").astype(jnp.float32),
        lax.psum(up_part.astype(jnp.bfloat16), "rows").astype(jnp.float32),
        lax.psum(down_part.astype(jnp.bfloat16), "rows").astype(jnp.float32),
    )
    mix_one, mix_two, mix_new, mix_average = adam_update(
        mixing_grad, mixing_w, mixing_m, mixing_v, mixing_avg
    )
    cond_one, cond_two, cond_new, cond_average = adam_update(
        cond_grad, cond_w, cond_m, cond_v, cond_avg
    )
    up_one, up_two, up_new, up_average = adam_update(up_grad, up_w, up_m, up_v, up_avg)
    down_one, down_two, down_new, down_average = adam_update(
        down_grad, down_w, down_m, down_v, down_avg
    )
    return (
        output[None],
        input_grad[None],
        mixing_grad,
        mix_one,
        mix_two,
        mix_new,
        mix_average,
        cond_grad,
        cond_one,
        cond_two,
        cond_new,
        cond_average,
        up_grad,
        up_one,
        up_two,
        up_new,
        up_average,
        down_grad,
        down_one,
        down_two,
        down_new,
        down_average,
    )


def local_small(
    tokens, time_embed, segment_ids, cotangent,
    mixing_w, mixing_m, mixing_v, mixing_avg,
    cond_w, cond_m, cond_v, cond_avg,
    up_w, up_m, up_v, up_avg,
    down_w, down_m, down_v, down_avg,
):
    x, cot = tokens[0], cotangent[0]
    lse, scales, turn, feat, thirds, w, lt, dpre, qkv, middle, back, output = forward(
        segment_ids, time_embed, x, cot, mixing_w, cond_w, up_w, down_w)
    sums, input_grad = backward(turn, lse, scales, time_embed, feat, thirds, w, lt, cot, dpre, qkv, middle, back, x)
    states = (
        mixing_w, mixing_m, mixing_v, mixing_avg, cond_w, cond_m, cond_v, cond_avg,
        up_w, up_m, up_v, up_avg, down_w, down_m, down_v, down_avg)
    return update(sums, states, (output, input_grad))


def solution(mesh):
    small = mesh.shape["rows"] == 4 and mesh.shape["fsdp"] == 8
    placed = (
        P(("rows", "fsdp"), None, None),
        P(("rows", "fsdp"), None),
        P(("rows", "fsdp"), None),
        P(("rows", "fsdp"), None, None),
        P(None, "fsdp", None),
        P(None, "fsdp", None),
        P(None, "fsdp", None),
        P(None, "fsdp", None),
        P(None, "fsdp", None),
        P(None, "fsdp", None),
        P(None, "fsdp", None),
        P(None, "fsdp", None),
        P("fsdp", None),
        P("fsdp", None),
        P("fsdp", None),
        P("fsdp", None),
        P("fsdp", None),
        P("fsdp", None),
        P("fsdp", None),
        P("fsdp", None),
    )
    return jax.shard_map(
        local_small if small else local,
        mesh=mesh,
        in_specs=placed,
        out_specs=(
            P(("rows", "fsdp"), None, None),
            P(("rows", "fsdp"), None, None),
            P(None, "fsdp", None),
            P(None, "fsdp", None),
            P(None, "fsdp", None),
            P(None, "fsdp", None),
            P(None, "fsdp", None),
            P(None, "fsdp", None),
            P(None, "fsdp", None),
            P(None, "fsdp", None),
            P(None, "fsdp", None),
            P(None, "fsdp", None),
            P("fsdp", None),
            P("fsdp", None),
            P("fsdp", None),
            P("fsdp", None),
            P("fsdp", None),
            P("fsdp", None),
            P("fsdp", None),
            P("fsdp", None),
            P("fsdp", None),
            P("fsdp", None),
        ),
        check_vma=False,
    )
```
